32 devices in a mesh: row: 4 (over x, core), col: 8 (over z, y).
Axes of the slice: x: 2, y: 2, z: 4, core: 2. Of those that a mesh axis runs over, the one named last changes fastest.
Arguments:
- trail: bfloat16 [8192, 8192], P('row', 'col'), may hold values from -0.0625 to 0.0625
- row_one: bfloat16 [128, 8192], P('row', 'col'), may hold values from -0.5 to 0.5
- row_two: bfloat16 [128, 8192], P('row', 'col'), may hold values from -0.5 to 0.5
- diag_one: float32 [128, 128], replicated, may hold values from -1 to 2, as said below
- diag_two: float32 [128, 128], replicated, may hold values from -1 to 2, as said below
- adj_trail: float32 [8192, 8192], P('row', 'col'), may hold values from -6 to 6
- adj_row_one: float32 [128, 8192], P('row', 'col'), may hold values from -6 to 6
- adj_row_two: float32 [128, 8192], P('row', 'col'), may hold values from -6 to 6
- adj_diag_one: float32 [128, 128], replicated, may hold values from -6 to 6
- adj_diag_two: float32 [128, 128], replicated, may hold values from -6 to 6
Outputs:
- grad_trail: bfloat16 [8192, 8192], P('row', 'col')
- grad_row_one: float32 [128, 8192], P('row', 'col')
- grad_row_two: float32 [128, 8192], P('row', 'col')
- grad_diag_one: float32 [128, 128], replicated
- grad_diag_two: float32 [128, 128], replicated
The draws below stay inside these ranges and needn't reach their ends.
Inputs may be any that keep to these rules, and one draw needn't show every extreme that they name: `diag_one`: lower triangular with a positive diagonal. `diag_two`: lower triangular with a positive diagonal.
All inputs are finite; a program needn't handle non-finite values.
Results may differ from the reference program's by a relative error of at most 0.014.
Values may be sent and summed in bfloat16 or wider, within the bound.
No kernel may reach another device: no remote copies, remote signals or barrier semaphores. Data moves between devices by JAX's collectives and lax.ppermute only.
A program may use at most 128 MiB of HBM per device.

```python
import jax
import jax.numpy as jnp
from jax import lax

PANEL = 128
WC = 1024
M = 8192
W = 8192
N_COL = 8


def lower_block(key, order):
    first, second = jax.random.split(key)
    diagonal = jax.random.uniform(first, (order,), jnp.float32, 1.0, 2.0)
    below = 0.03 * jax.random.normal(second, (order, order), jnp.float32)
    below = jnp.clip(below, -0.5, 0.5)
    return jnp.tril(below, -1) + jnp.diag(diagonal)


def draw_diag_one(key, part):
    return lower_block(jax.random.fold_in(key, 11), PANEL)


def draw_diag_two(key, part):
    return lower_block(jax.random.fold_in(key, 12), PANEL)


def block_scale(own_key, dims, cuts, low, high):
    level = 1.0
    for position, shards_of in cuts:
        heights = jax.random.uniform(jax.random.fold_in(jax.random.fold_in(own_key, 6), position), (shards_of,), jnp.float32, low / len(cuts), high / len(cuts))
        level = level * jnp.repeat(jnp.exp(heights), dims[position] // shards_of).reshape((-1,) + (1,) * (len(dims) - 1 - position))
    return level


def scatter_about(rng, extent, spread, most, shards=(), kind=jnp.bfloat16):
    loudness = block_scale(rng, extent, shards, -0.22, 0.18) if shards else 1.0
    array = jax.random.normal(rng, extent, jnp.float32) * spread * loudness
    return jnp.minimum(jnp.maximum(array, -most), most).astype(kind)


def setup_inputs(seed: int = 0) -> dict:
    arg_keys = jax.random.split(jax.random.key(seed), 11)
    return {
        "trail": scatter_about(arg_keys[0], (M, W), M ** -0.5, 0.0625, ((0, 4), (1, 8))),
        "row_one": scatter_about(arg_keys[1], (PANEL, W), PANEL ** -0.5, 0.5, ((0, 4), (1, 8))),
        "row_two": scatter_about(arg_keys[2], (PANEL, W), PANEL ** -0.5, 0.5, ((0, 4), (1, 8))),
        "diag_one": draw_diag_one(jax.random.fold_in(arg_keys[10], 71), 0),
        "diag_two": draw_diag_two(jax.random.fold_in(arg_keys[10], 71), 0),
        "adj_trail": scatter_about(arg_keys[5], (M, W), 1.0, 6.0, ((0, 4), (1, 8)), jnp.float32),
        "adj_row_one": scatter_about(arg_keys[6], (PANEL, W), 1.0, 6.0, ((0, 4), (1, 8)), jnp.float32),
        "adj_row_two": scatter_about(arg_keys[7], (PANEL, W), 1.0, 6.0, ((0, 4), (1, 8)), jnp.float32),
        "adj_diag_one": scatter_about(arg_keys[8], (PANEL, PANEL), 1.0, 6.0, (), jnp.float32),
        "adj_diag_two": scatter_about(arg_keys[9], (PANEL, PANEL), 1.0, 6.0, (), jnp.float32),
    }


exact_mode = lax.Precision.HIGHEST

def halved_lower(matrix):
    order = matrix.shape[0]
    keep = jnp.tril(jnp.ones((order, order), matrix.dtype)) - 0.5 * jnp.eye(order, dtype=matrix.dtype)
    return matrix * keep

def inverse_lower(block):
    ident = jnp.eye(block.shape[0], dtype=block.dtype)
    return lax.linalg.triangular_solve(block, ident, left_side=True, lower=True)

def block_adjoint(block, inverse, seed_adj):
    inner = halved_lower(jnp.dot(block.T, seed_adj, precision=exact_mode))
    middle = jnp.dot(inverse.T, inner, precision=exact_mode)
    return halved_lower(jnp.dot(middle, inverse, precision=exact_mode))

def reference(trail, row_one, row_two, diag_one, diag_two, adj_trail, adj_row_one, adj_row_two, adj_diag_one, adj_diag_two):
    one_start = (N_COL - 1) * WC - PANEL
    two_start = N_COL * WC - PANEL
    one_end = one_start + PANEL
    inverse_two = inverse_lower(diag_two)
    solved_two = jnp.dot(adj_trail[:, two_start:], inverse_two, precision=exact_mode).astype(jnp.bfloat16)
    seed_two = jnp.tril(adj_diag_two - jnp.dot(solved_two.T.astype(jnp.float32), trail[:, two_start:].astype(jnp.float32), preferred_element_type=jnp.float32))
    grad_diag_two = block_adjoint(diag_two, inverse_two, seed_two)
    mirror_two = grad_diag_two + grad_diag_two.T
    adj_two = adj_row_two - jnp.dot(solved_two.T.astype(jnp.float32), trail.astype(jnp.float32), preferred_element_type=jnp.float32) - jnp.dot(mirror_two, row_two.astype(jnp.float32), precision=exact_mode)
    adj_next = adj_trail - jnp.dot(solved_two.astype(jnp.float32), row_two.astype(jnp.float32), preferred_element_type=jnp.float32)
    inverse_one = inverse_lower(diag_one)
    stacked = jnp.concatenate([adj_two[:, one_start:one_end], adj_next[:, one_start:one_end]], 0)
    solved_one = jnp.dot(stacked, inverse_one, precision=exact_mode).astype(jnp.bfloat16)
    head_rows = solved_one[:PANEL]
    tail_rows = solved_one[PANEL:]
    cross_one = jnp.dot(head_rows.T.astype(jnp.float32), row_two[:, one_start:one_end].astype(jnp.float32), preferred_element_type=jnp.float32) + jnp.dot(tail_rows.T.astype(jnp.float32), trail[:, one_start:one_end].astype(jnp.float32), preferred_element_type=jnp.float32)
    seed_one = jnp.tril(adj_diag_one - cross_one)
    grad_diag_one = block_adjoint(diag_one, inverse_one, seed_one)
    mirror_one = grad_diag_one + grad_diag_one.T
    two_left = adj_two - jnp.dot(head_rows.astype(jnp.float32), row_one.astype(jnp.float32), preferred_element_type=jnp.float32)
    trail_left = adj_next - jnp.dot(tail_rows.astype(jnp.float32), row_one.astype(jnp.float32), preferred_element_type=jnp.float32)
    one_left = adj_row_one - jnp.dot(head_rows.T.astype(jnp.float32), row_two.astype(jnp.float32), preferred_element_type=jnp.float32) - jnp.dot(tail_rows.T.astype(jnp.float32), trail.astype(jnp.float32), preferred_element_type=jnp.float32) - jnp.dot(mirror_one, row_one.astype(jnp.float32), precision=exact_mode)
    grad_trail = trail_left.at[:, one_start:one_end].set(tail_rows.astype(jnp.float32))
    grad_trail = grad_trail.at[:, two_start:].set(solved_two.astype(jnp.float32)).astype(jnp.bfloat16)
    grad_row_one = one_left.at[:, one_start:one_end].set(0.0).at[:, two_start:].set(0.0)
    grad_row_two = two_left.at[:, one_start:one_end].set(head_rows.astype(jnp.float32)).at[:, two_start:].set(0.0)
    return (grad_trail, grad_row_one, grad_row_two, grad_diag_one, grad_diag_two)
```

```python
import jax
import jax.numpy as jnp
from jax import lax
from jax.sharding import PartitionSpec as P

EXACT = lax.Precision.HIGHEST
F32 = jnp.float32
BF16 = jnp.bfloat16


def exact_dot(a, b):
    return jnp.dot(a, b, precision=EXACT)


def wide_dot(a, b):
    return jnp.dot(a, b, preferred_element_type=F32)


def halved_lower(matrix):
    order = matrix.shape[0]
    rows = lax.broadcasted_iota(jnp.int32, (order, order), 0)
    cols = lax.broadcasted_iota(jnp.int32, (order, order), 1)
    return jnp.where(rows > cols, matrix, jnp.where(rows == cols, 0.5 * matrix, 0))


def inverse_lower(blocks):
    order = blocks.shape[-1]
    rows = lax.broadcasted_iota(jnp.int32, (order, order), 0)
    cols = lax.broadcasted_iota(jnp.int32, (order, order), 1)
    diag = jnp.sum(jnp.where(rows == cols, blocks, 0), 2)
    recip = 1.0 / diag
    inverse = jnp.where(rows == cols, recip[:, :, None], 0)
    size = 1
    while size < order:
        pair = rows // (2 * size) == cols // (2 * size)
        below = (rows // size) % 2 > (cols // size) % 2
        corner = jnp.where(pair & below, blocks, 0)
        if size == 1:
            change = recip[:, :, None] * corner * recip[:, None, :]
        else:
            change = jnp.matmul(
                jnp.matmul(inverse, corner, precision=EXACT), inverse, precision=EXACT
            )
        inverse = inverse - change
        size *= 2
    return inverse


def block_adjoint(block, inverse, seed_adj):
    inner = halved_lower(exact_dot(block.T, seed_adj))
    middle = exact_dot(inverse.T, inner)
    return halved_lower(exact_dot(middle, inverse))


def per_device(
    trail,
    row_one,
    row_two,
    diag_one,
    diag_two,
    adj_trail,
    adj_row_one,
    adj_row_two,
    adj_diag_one,
    adj_diag_two,
):
    panel = diag_one.shape[0]
    height, width = trail.shape
    band = row_one.shape[0]
    last = width - panel
    row_count = lax.axis_size("row")
    col_count = lax.axis_size("col")
    levels = col_count // 2
    row_here = lax.axis_index("row")
    col_here = lax.axis_index("col")
    row_start = row_here * band
    level = col_here // 2
    is_two = col_here % 2 == 1
    here_one = col_here == col_count - 2
    here_two = col_here == col_count - 1

    def own_rows(matrix):
        return lax.dynamic_slice_in_dim(matrix, row_start, band, 0)

    def row_swap(value, step):
        return lax.ppermute(value, "row", [(i, i ^ step) for i in range(row_count)])

    def pair_swap(value, which):
        pairs = [(2 * k + s, 2 * k + 1 - s) for k in which for s in range(2)]
        return lax.ppermute(value, "col", pairs)

    def spread(value):
        step = levels // 2
        holders = [0]
        while step >= 1:
            hops = [(d, d + step) for d in holders]
            pairs = []
            arrived = jnp.zeros((), jnp.bool_)
            for source, target in hops:
                for s in range(2):
                    pairs.append(
                        (
                            2 * (levels - 1 - source) + s,
                            2 * (levels - 1 - target) + s,
                        )
                    )
                arrived = arrived | (level == levels - 1 - target)
            value = jnp.where(arrived, lax.ppermute(value, "col", pairs), value)
            holders += [target for _, target in hops]
            step //= 2
        return value

    rows_all = jnp.stack([row_two, row_one])[:, None]
    step = 1
    while step < row_count:
        other = row_swap(rows_all, step)
        low = (row_here // step) % 2 == 0
        rows_all = jnp.concatenate(
            [jnp.where(low, rows_all, other), jnp.where(low, other, rows_all)], 1
        )
        step *= 2
    full_two = rows_all[0].reshape(panel, width)
    full_one = rows_all[1].reshape(panel, width)

    inverses = inverse_lower(jnp.stack([diag_one, diag_two]))
    inverse_one, inverse_two = inverses[0], inverses[1]
    solved = exact_dot(
        adj_trail[:, last:], jnp.where(is_two, inverse_two, inverse_one)
    ).astype(BF16)
    packet = jnp.concatenate([solved, full_two[:, last:]], 0)

    def tail_of(own, other):
        solved_two = jnp.where(is_two, own[:height], other[:height])
        base_one = jnp.where(is_two, other[:height], own[:height])
        cross = jnp.where(is_two, other[height:], own[height:])
        carried = exact_dot(cross.astype(F32), inverse_one)
        high = carried.astype(BF16)
        low = (carried - high.astype(F32)).astype(BF16)
        tail = base_one.astype(F32) - wide_dot(
            jnp.concatenate([solved_two, solved_two], 1), jnp.concatenate([high, low], 0)
        )
        return solved_two, tail.astype(BF16), cross

    top_other = pair_swap(packet, [levels - 1])
    top_two, top_tail, _ = tail_of(packet, top_other)
    terms = wide_dot(jnp.concatenate([top_two, top_tail], 1).T, trail[:, last:])
    placed = lax.dynamic_update_slice_in_dim(
        jnp.zeros((2 * panel, panel), F32),
        jnp.where(is_two, 0, adj_row_two[:, last:]),
        row_start,
        0,
    )
    terms = terms - placed
    step = 1
    while step < row_count:
        terms = terms + row_swap(terms, step)
        step *= 2
    terms = spread(terms.astype(BF16))
    terms_other = pair_swap(terms, range(levels))
    terms, terms_other = terms.astype(F32), terms_other.astype(F32)
    diag_term_two = jnp.where(is_two, terms[:panel], terms_other[:panel])
    crossing = jnp.where(is_two, terms_other[:panel], terms[:panel])
    diag_term_one = jnp.where(is_two, terms_other[panel:], terms[panel:])

    packet = spread(packet)
    packet_other = pair_swap(packet, range(levels - 1))
    packet_other = jnp.where(level == levels - 1, top_other, packet_other)
    solved_two, tail, cross = tail_of(packet, packet_other)
    both = jnp.concatenate([solved_two, tail], 1)
    sums = wide_dot(both.T, trail).reshape(2, panel, width)

    grad_diag_two = block_adjoint(
        diag_two, inverse_two, jnp.tril(adj_diag_two - diag_term_two)
    )
    mirror_two = grad_diag_two + grad_diag_two.T
    adj_two = -crossing - exact_dot(mirror_two, cross.astype(F32))
    head = exact_dot(adj_two, inverse_one).astype(BF16)
    seed_one = jnp.tril(adj_diag_one - wide_dot(head.T, cross) - diag_term_one)
    grad_diag_one = block_adjoint(diag_one, inverse_one, seed_one)
    mirror_one = grad_diag_one + grad_diag_one.T

    parts = sums.reshape(2, row_count, band, width)
    step = 1
    while step < row_count:
        low = (row_here // step) % 2 == 0
        parts = parts.reshape(2, -1, 2, band, width)
        keep = jnp.where(low, parts[:, :, 0], parts[:, :, 1])
        give = jnp.where(low, parts[:, :, 1], parts[:, :, 0])
        parts = keep + row_swap(give.astype(BF16), step).astype(F32)
        step *= 2
    parts = parts.reshape(2, band, width)

    head_wide = head.astype(F32)
    mix_two = jnp.concatenate([own_rows(mirror_two), own_rows(head_wide)], 1)
    mix_one = jnp.concatenate([own_rows(head_wide.T), own_rows(mirror_one)], 1)
    full_both = jnp.concatenate([full_two, full_one], 0)
    mixed = exact_dot(jnp.concatenate([mix_two, mix_one], 0), full_both.astype(F32))
    two_left = adj_row_two - mixed[:band] - parts[0]
    one_left = adj_row_one - mixed[band:] - parts[1]

    trail_left = adj_trail - wide_dot(both, full_both)
    column = lax.broadcasted_iota(jnp.int32, (1, width), 1)
    in_block = column >= last

    def put(matrix, block_one, block_two):
        block = jnp.where(here_one, block_one, block_two).astype(F32)
        block = jnp.pad(block, ((0, 0), (last, 0)))
        return jnp.where(in_block & (here_one | here_two), block, matrix)

    grad_trail = put(trail_left, tail, solved_two).astype(BF16)
    nothing = jnp.zeros((band, panel), F32)
    grad_row_one = put(one_left, nothing, nothing)
    grad_row_two = put(two_left, own_rows(head_wide), nothing)
    return (grad_trail, grad_row_one, grad_row_two, grad_diag_one, grad_diag_two)


def solution(mesh):
    split = P("row", "col")
    in_specs = (split, split, split, P(), P(), split, split, split, P(), P())
    out_specs = (split, split, split, P(), P())
    return jax.shard_map(
        per_device, mesh=mesh, in_specs=in_specs, out_specs=out_specs, check_vma=False
    )
```

```python
import functools

import jax
import jax.numpy as jnp
from jax import lax
from jax.experimental import pallas as pl
from jax.experimental.pallas import tpu as pltpu
from jax.sharding import PartitionSpec as P

EXACT = lax.Precision.HIGHEST
F32 = jnp.float32
BF16 = jnp.bfloat16
PIECES = 3


def exact_dot(a, b):
    return jnp.dot(a, b, precision=EXACT, preferred_element_type=F32)


def wide_dot(a, b):
    return jnp.dot(a, b, preferred_element_type=F32)


def halves(value):
    high = value.astype(BF16)
    return high, (value - high.astype(F32)).astype(BF16)


def halved_lower(matrix):
    order = matrix.shape[0]
    rows = lax.broadcasted_iota(jnp.int32, (order, order), 0)
    cols = lax.broadcasted_iota(jnp.int32, (order, order), 1)
    return jnp.where(rows > cols, matrix, jnp.where(rows == cols, 0.5 * matrix, 0))


def inverse_lower(blocks):
    order = blocks[0].shape[-1]
    rows = lax.broadcasted_iota(jnp.int32, (order, order), 0)
    cols = lax.broadcasted_iota(jnp.int32, (order, order), 1)
    equal = rows == cols
    inverses = []
    for block in blocks:
        recip_col = 1.0 / jnp.sum(jnp.where(equal, block, 0), 1, keepdims=True)
        recip_row = 1.0 / jnp.sum(jnp.where(equal, block, 0), 0, keepdims=True)
        pair = ((rows ^ cols) == 1) & (rows > cols)
        corner = jnp.where(pair, block, 0)
        inverses.append(jnp.where(equal, recip_col, 0) - recip_col * corner * recip_row)
    size = 2
    while size < order:
        below = ((rows ^ cols) & -size == size) & (rows > cols)
        below = below & ((rows ^ cols) < 2 * size)
        inner = [
            exact_dot(jnp.where(below, block, 0), inverse)
            for block, inverse in zip(blocks, inverses)
        ]
        inverses = [
            inverse - exact_dot(inverse, part) for inverse, part in zip(inverses, inner)
        ]
        size *= 2
    return inverses


def prepare_kernel(cuts, side_ref, one_ref, two_ref, rows_ref, inv_one_ref, inv_two_ref, *out_refs):
    inverse_one, inverse_two = inverse_lower([one_ref[...], two_ref[...]])
    inv_one_ref[...] = inverse_one
    inv_two_ref[...] = inverse_two
    chosen = jnp.where(side_ref[0] == 1, inverse_two, inverse_one)
    high, low = halves(chosen)
    for (start, size), out_ref in zip(cuts, out_refs):
        own_high, own_low = halves(rows_ref[start : start + size, :])
        product = wide_dot(own_high, high) + (
            wide_dot(own_high, low) + wide_dot(own_low, high)
        )
        out_ref[...] = product.astype(BF16)


def prepare(side, diag_one, diag_two, adj_trail, cuts):
    height, width = adj_trail.shape
    panel = diag_one.shape[0]
    square = pl.BlockSpec((panel, panel), lambda i: (0, 0))
    return pl.pallas_call(
        functools.partial(prepare_kernel, cuts),
        grid=(1,),
        in_specs=[
            pl.BlockSpec(memory_space=pltpu.SMEM),
            square,
            square,
            pl.BlockSpec((height, panel), lambda i: (0, width // panel - 1)),
        ],
        out_specs=[square, square]
        + [pl.BlockSpec((size, panel), lambda i: (0, 0)) for _, size in cuts],
        out_shape=[jax.ShapeDtypeStruct((panel, panel), F32)] * 2
        + [jax.ShapeDtypeStruct((size, panel), BF16) for _, size in cuts],
        compiler_params=pltpu.CompilerParams(vmem_limit_bytes=32 * 2**20),
        cost_estimate=pl.CostEstimate(
            flops=8 * height * panel * panel, bytes_accessed=6 * height * panel, transcendentals=0
        ),
        name="prepare",
    )(side, diag_one, diag_two, adj_trail)


def block_adjoint(block, inverse, seed_adj):
    inner = halved_lower(exact_dot(block.T, seed_adj))
    middle = exact_dot(inverse.T, inner)
    return halved_lower(exact_dot(middle, inverse))


def per_device(
    trail,
    row_one,
    row_two,
    diag_one,
    diag_two,
    adj_trail,
    adj_row_one,
    adj_row_two,
    adj_diag_one,
    adj_diag_two,
):
    panel = diag_one.shape[0]
    height, width = trail.shape
    band = row_one.shape[0]
    last = width - panel
    row_count = lax.axis_size("row")
    col_count = lax.axis_size("col")
    levels = col_count // 2
    top = levels - 1
    row_here = lax.axis_index("row")
    col_here = lax.axis_index("col")
    row_start = row_here * band
    level = col_here // 2
    is_two = col_here % 2 == 1
    here_one = col_here == col_count - 2
    here_two = col_here == col_count - 1
    step_rows = -(-height // (16 * PIECES)) * 16
    cuts = [(at, min(step_rows, height - at)) for at in range(0, height, step_rows)]

    def own_rows(matrix):
        return lax.dynamic_slice_in_dim(matrix, row_start, band, 0)

    def row_swap(value, step):
        return lax.ppermute(value, "row", [(i, i ^ step) for i in range(row_count)])

    def pair_swap(value, which):
        pairs = [(2 * k + s, 2 * k + 1 - s) for k in which for s in range(2)]
        return lax.ppermute(value, "col", pairs)

    def gather_rows(value):
        value = value[None]
        step = 1
        while step < row_count:
            other = row_swap(value, step)
            low = (row_here // step) % 2 == 0
            value = jnp.concatenate(
                [jnp.where(low, value, other), jnp.where(low, other, value)], 0
            )
            step *= 2
        return value.reshape(panel, width)

    def spread(value):
        held = {top: value}

        def pick(which):
            groups = []
            for k in which:
                for group in groups:
                    if group[0] is held[k]:
                        group[1].append(k)
                        break
                else:
                    groups.append((held[k], [k]))
            chosen = groups[0][0]
            for array, members in groups[1:]:
                at = functools.reduce(jnp.logical_or, [level == k for k in members])
                chosen = jnp.where(at, array, chosen)
            return chosen

        def send(hops):
            operand = pick([source for source, _ in hops])
            pairs = [(2 * a + s, 2 * b + s) for a, b in hops for s in range(2)]
            arrived = lax.ppermute(operand, "col", pairs)
            return {target: arrived for _, target in hops}

        if levels > 1:
            span = levels // 2
            held.update(send([(top, span - 1)]))
            fresh = [span - 1]
            span //= 2
            while span >= 1:
                up = send([(k, k + span) for k in fresh])
                down = send([(k, k - span) for k in fresh])
                held.update(up)
                held.update(down)
                fresh = [k + d * span for k in fresh for d in (1, -1)]
                span //= 2
        return pick(list(range(levels - 1))) if levels > 1 else value

    full_two = gather_rows(row_two)
    side = is_two.astype(jnp.int32)[None]
    inverse_one, inverse_two, *solved = prepare(side, diag_one, diag_two, adj_trail, cuts)
    cross_piece = min(1, len(cuts) - 1)
    packets = [
        jnp.concatenate([piece, full_two[:, last:]], 0) if k == cross_piece else piece
        for k, piece in enumerate(solved)
    ]

    def cross_factor(own, other):
        size = cuts[cross_piece][1]
        cross = jnp.where(is_two, other[size:], own[size:])
        return cross, jnp.concatenate(halves(exact_dot(cross.astype(F32), inverse_one)), 0)

    def panels_of(own, other, factor, size):
        solved_two = jnp.where(is_two, own[:size], other[:size])
        base_one = jnp.where(is_two, other[:size], own[:size])
        tail = base_one.astype(F32) - wide_dot(
            jnp.concatenate([solved_two, solved_two], 1), factor
        )
        return jnp.concatenate([solved_two, tail.astype(BF16)], 1)

    arrived = [spread(packet) for packet in packets]
    top_other = [pair_swap(packet, [top]) for packet in packets]
    low_other = [pair_swap(packet, range(levels - 1)) for packet in arrived]

    _, top_factor = cross_factor(packets[cross_piece], top_other[cross_piece])
    terms = 0
    for k, (start, size) in enumerate(cuts):
        top_both = panels_of(packets[k], top_other[k], top_factor, size)
        terms = terms + wide_dot(top_both.T, trail[start : start + size, last:])
    placed = lax.dynamic_update_slice_in_dim(
        jnp.zeros((2 * panel, panel), F32),
        jnp.where(is_two, 0, adj_row_two[:, last:]),
        row_start,
        0,
    )
    terms = terms - placed
    step = 1
    while step < row_count:
        terms = terms + row_swap(terms, step)
        step *= 2
    terms = terms.astype(BF16)
    terms = jnp.where(level == top, terms, spread(terms))
    terms_other = pair_swap(terms, range(levels))
    terms, terms_other = terms.astype(F32), terms_other.astype(F32)
    diag_term_two = jnp.where(is_two, terms[:panel], terms_other[:panel])
    crossing = jnp.where(is_two, terms_other[:panel], terms[:panel])
    diag_term_one = jnp.where(is_two, terms_other[panel:], terms[panel:])

    at_top = level == top
    own = [jnp.where(at_top, a, b) for a, b in zip(packets, arrived)]
    other = [jnp.where(at_top, a, b) for a, b in zip(top_other, low_other)]
    cross, factor = cross_factor(own[cross_piece], other[cross_piece])
    both = [
        panels_of(own[k], other[k], factor, size) for k, (_, size) in enumerate(cuts)
    ]
    sums = 0
    for (start, size), piece in zip(cuts, both):
        sums = sums + wide_dot(piece.T, trail[start : start + size])
    both = jnp.concatenate(both, 0)
    solved_two, tail = both[:, :panel], both[:, panel:]
    full_one = gather_rows(row_one)

    grad_diag_two = block_adjoint(
        diag_two, inverse_two, jnp.tril(adj_diag_two - diag_term_two)
    )
    mirror_two = grad_diag_two + grad_diag_two.T
    adj_two = -crossing - exact_dot(mirror_two, cross.astype(F32))
    head = exact_dot(adj_two, inverse_one).astype(BF16)
    seed_one = jnp.tril(adj_diag_one - wide_dot(head.T, cross) - diag_term_one)
    grad_diag_one = block_adjoint(diag_one, inverse_one, seed_one)
    mirror_one = grad_diag_one + grad_diag_one.T

    parts = sums.reshape(2, row_count, band, width)
    step = 1
    while step < row_count:
        low = (row_here // step) % 2 == 0
        parts = parts.reshape(2, -1, 2, band, width)
        keep = jnp.where(low, parts[:, :, 0], parts[:, :, 1])
        give = jnp.where(low, parts[:, :, 1], parts[:, :, 0])
        parts = keep + row_swap(give.astype(BF16), step).astype(F32)
        step *= 2
    parts = parts.reshape(2, band, width)

    head_wide = head.astype(F32)
    mix_two = jnp.concatenate([own_rows(mirror_two), own_rows(head_wide)], 1)
    mix_one = jnp.concatenate([own_rows(head_wide.T), own_rows(mirror_one)], 1)
    full_both = jnp.concatenate([full_two, full_one], 0)
    mix = jnp.concatenate([mix_two, mix_one], 0)
    mixed = wide_dot(
        jnp.concatenate(halves(mix), 1), jnp.concatenate([full_both, full_both], 0)
    )
    two_left = adj_row_two - mixed[:band] - parts[0]
    one_left = adj_row_one - mixed[band:] - parts[1]

    trail_left = adj_trail - wide_dot(both, full_both)
    column = lax.broadcasted_iota(jnp.int32, (1, width), 1)
    in_block = column >= last

    def put(matrix, block_one, block_two):
        block = jnp.where(here_one, block_one, block_two).astype(F32)
        block = jnp.pad(block, ((0, 0), (last, 0)))
        return jnp.where(in_block & (here_one | here_two), block, matrix)

    grad_trail = put(trail_left, tail, solved_two).astype(BF16)
    nothing = jnp.zeros((band, panel), F32)
    grad_row_one = put(one_left, nothing, nothing)
    grad_row_two = put(two_left, own_rows(head_wide), nothing)
    return (grad_trail, grad_row_one, grad_row_two, grad_diag_one, grad_diag_two)


def solution(mesh):
    split = P("row", "col")
    in_specs = (split, split, split, P(), P(), split, split, split, P(), P())
    out_specs = (split, split, split, P(), P())
    return jax.shard_map(
        per_device, mesh=mesh, in_specs=in_specs, out_specs=out_specs, check_vma=False
    )
```

```python
import functools

import jax
import jax.numpy as jnp
from jax import lax
from jax.experimental import pallas as pl
from jax.experimental.pallas import tpu as pltpu
from jax.sharding import PartitionSpec as P

EXACT = lax.Precision.HIGHEST
F32 = jnp.float32
BF16 = jnp.bfloat16
PIECES = 3


def exact_dot(a, b):
    return jnp.dot(a, b, precision=EXACT, preferred_element_type=F32)


def wide_dot(a, b):
    return jnp.dot(a, b, preferred_element_type=F32)


def halves(value):
    high = value.astype(BF16)
    return high, (value - high.astype(F32)).astype(BF16)


def halved_lower(matrix):
    order = matrix.shape[0]
    rows = lax.broadcasted_iota(jnp.int32, (order, order), 0)
    cols = lax.broadcasted_iota(jnp.int32, (order, order), 1)
    return jnp.where(rows > cols, matrix, jnp.where(rows == cols, 0.5 * matrix, 0))


def inverse_lower(blocks):
    order = blocks[0].shape[-1]
    rows = lax.broadcasted_iota(jnp.int32, (order, order), 0)
    cols = lax.broadcasted_iota(jnp.int32, (order, order), 1)
    equal = rows == cols
    inverses = []
    for block in blocks:
        recip_col = 1.0 / jnp.sum(jnp.where(equal, block, 0), 1, keepdims=True)
        recip_row = 1.0 / jnp.sum(jnp.where(equal, block, 0), 0, keepdims=True)
        pair = ((rows ^ cols) == 1) & (rows > cols)
        corner = jnp.where(pair, block, 0)
        inverses.append(jnp.where(equal, recip_col, 0) - recip_col * corner * recip_row)
    size = 2
    while size < order:
        below = ((rows ^ cols) & -size == size) & (rows > cols)
        below = below & ((rows ^ cols) < 2 * size)
        inner = [
            exact_dot(jnp.where(below, block, 0), inverse)
            for block, inverse in zip(blocks, inverses)
        ]
        inverses = [
            inverse - exact_dot(inverse, part) for inverse, part in zip(inverses, inner)
        ]
        size *= 2
    return inverses


def invert_kernel(one_ref, two_ref, inv_one_ref, inv_two_ref):
    inverse_one, inverse_two = inverse_lower([one_ref[...], two_ref[...]])
    inv_one_ref[...] = inverse_one
    inv_two_ref[...] = inverse_two


def invert(diag_one, diag_two):
    square = jax.ShapeDtypeStruct(diag_one.shape, F32)
    return pl.pallas_call(
        invert_kernel,
        out_shape=[square, square],
        cost_estimate=pl.CostEstimate(
            flops=12 * 12 * diag_one.shape[0] ** 3, bytes_accessed=2**18, transcendentals=0
        ),
        name="invert",
    )(diag_one, diag_two)


def solve_kernel(side_ref, one_ref, two_ref, rows_ref, cross_ref, out_ref):
    panel = one_ref.shape[0]
    chosen = jnp.where(side_ref[0] == 1, two_ref[...], one_ref[...])
    high, low = halves(chosen)
    own_high, own_low = halves(rows_ref[...])
    product = wide_dot(own_high, high) + (
        wide_dot(own_high, low) + wide_dot(own_low, high)
    )
    out_ref[:panel, :] = cross_ref[...]
    out_ref[panel:, :] = product.astype(BF16)


def solve(side, inverse_one, inverse_two, rows, cross):
    height, panel = rows.shape
    vmem = pl.BlockSpec(memory_space=pltpu.VMEM)
    return pl.pallas_call(
        solve_kernel,
        in_specs=[pl.BlockSpec(memory_space=pltpu.SMEM)] + [vmem] * 4,
        out_specs=vmem,
        out_shape=jax.ShapeDtypeStruct((panel + height, panel), BF16),
        compiler_params=pltpu.CompilerParams(vmem_limit_bytes=32 * 2**20),
        cost_estimate=pl.CostEstimate(
            flops=6 * height * panel * panel, bytes_accessed=6 * height * panel, transcendentals=0
        ),
        name="solve",
    )(side, inverse_one, inverse_two, rows, cross)


def cut_kernel(cuts, whole_ref, *out_refs):
    for (start, stop), out_ref in zip(cuts, out_refs):
        out_ref[...] = whole_ref[start:stop, :]


def cut(whole, cuts):
    panel = whole.shape[1]
    vmem = pl.BlockSpec(memory_space=pltpu.VMEM)
    return pl.pallas_call(
        functools.partial(cut_kernel, cuts),
        in_specs=[vmem],
        out_specs=[vmem] * len(cuts),
        out_shape=[jax.ShapeDtypeStruct((stop - start, panel), BF16) for start, stop in cuts],
        cost_estimate=pl.CostEstimate(
            flops=0, bytes_accessed=2 * whole.size, transcendentals=0
        ),
        name="cut",
    )(whole)


def after(value, *others):
    return lax.optimization_barrier((value, *others))[0]


def block_adjoint(block, inverse, seed_adj):
    inner = halved_lower(exact_dot(block.T, seed_adj))
    middle = exact_dot(inverse.T, inner)
    return halved_lower(exact_dot(middle, inverse))


def per_device(
    trail,
    row_one,
    row_two,
    diag_one,
    diag_two,
    adj_trail,
    adj_row_one,
    adj_row_two,
    adj_diag_one,
    adj_diag_two,
):
    panel = diag_one.shape[0]
    height, width = trail.shape
    band = row_one.shape[0]
    last = width - panel
    row_count = lax.axis_size("row")
    col_count = lax.axis_size("col")
    levels = col_count // 2
    top = levels - 1
    row_here = lax.axis_index("row")
    col_here = lax.axis_index("col")
    row_start = row_here * band
    level = col_here // 2
    is_two = col_here % 2 == 1
    here_one = col_here == col_count - 2
    here_two = col_here == col_count - 1
    step_rows = -(-(height + panel) // (16 * PIECES)) * 16
    bounds = list(range(step_rows, height + panel, step_rows)) + [height + panel]
    bounds = [panel] + bounds
    cuts = list(zip(bounds, bounds[1:]))

    def own_rows(matrix):
        return lax.dynamic_slice_in_dim(matrix, row_start, band, 0)

    def row_swap(value, step):
        return lax.ppermute(value, "row", [(i, i ^ step) for i in range(row_count)])

    def pair_swap(value, which):
        pairs = [(2 * k + s, 2 * k + 1 - s) for k in which for s in range(2)]
        return lax.ppermute(value, "col", pairs)

    def gather_rows(value):
        value = value[None]
        step = 1
        while step < row_count:
            other = row_swap(value, step)
            low = (row_here // step) % 2 == 0
            value = jnp.concatenate(
                [jnp.where(low, value, other), jnp.where(low, other, value)], 0
            )
            step *= 2
        return value.reshape(panel, width)

    def choose(options):
        merged = []
        for members, array in options:
            for entry in merged:
                if entry[1] is array:
                    entry[0].extend(members)
                    break
            else:
                merged.append((list(members), array))
        chosen = merged[0][1]
        for members, array in merged[1:]:
            at = functools.reduce(jnp.logical_or, [level == k for k in members])
            chosen = jnp.where(at, array, chosen)
        return chosen

    def hop(value, hops):
        pairs = [(2 * a + s, 2 * b + s) for a, b in hops for s in range(2)]
        return lax.ppermute(value, "col", pairs)

    def spread_first(value):
        return hop(value, [(top, levels // 2 - 1)]) if levels > 1 else value

    def spread_rest(first):
        held = {max(levels // 2 - 1, 0): first}
        span = levels // 4
        while span >= 1:
            fresh = list(held)
            operand = choose([([k], held[k]) for k in fresh])
            up = hop(operand, [(k, k + span) for k in fresh])
            down = hop(operand, [(k, k - span) for k in fresh if k >= span])
            for k in fresh:
                held[k + span] = up
                if k >= span:
                    held[k - span] = down
            span //= 2
        return choose([([k], held[k]) for k in sorted(held)])

    full_two = gather_rows(row_two)
    inverse_one, inverse_two = invert(diag_one, diag_two)
    side = is_two.astype(jnp.int32)[None]
    whole = solve(
        side, inverse_one, inverse_two, adj_trail[:, last:], full_two[:, last:]
    )
    packets = cut(whole, [(0, cuts[0][1])] + cuts[1:])

    def cross_factor(own, other):
        cross = jnp.where(is_two, other[:panel], own[:panel])
        return cross, jnp.concatenate(halves(exact_dot(cross.astype(F32), inverse_one)), 0)

    def panels_of(own, other, factor, size):
        solved_two = jnp.where(is_two, own[-size:], other[-size:])
        base_one = jnp.where(is_two, other[-size:], own[-size:])
        tail = base_one.astype(F32) - wide_dot(
            jnp.concatenate([solved_two, solved_two], 1), factor
        )
        return jnp.concatenate([solved_two, tail.astype(BF16)], 1)

    whole_other = pair_swap(whole, [top])
    first = [spread_first(packet) for packet in packets]
    final = len(first) - 1
    full_one = gather_rows(after(row_one, full_two, first[min(1, final)]))
    arrived, low_other = [], []
    for k, value in enumerate(first):
        arrived.append(spread_rest(value))
        low_other.append(
            pair_swap(after(arrived[k], first[min(k + 1, final)]), range(levels - 1))
        )

    whole_other = after(whole_other, first[final])
    _, top_factor = cross_factor(whole, whole_other)
    top_both = panels_of(whole, whole_other, top_factor, height)
    terms = wide_dot(top_both.T, trail[:, last:])
    placed = lax.dynamic_update_slice_in_dim(
        jnp.zeros((2 * panel, panel), F32),
        jnp.where(is_two, 0, adj_row_two[:, last:]),
        row_start,
        0,
    )
    terms = terms - placed
    step = 1
    while step < row_count:
        pairs = [
            (i * col_count + c, (i ^ step) * col_count + c)
            for i in range(row_count)
            for c in (col_count - 2, col_count - 1)
        ]
        terms = terms + lax.ppermute(terms, ("row", "col"), pairs)
        step *= 2
    terms = row_terms = terms.astype(BF16)
    terms = choose(
        [([top], terms)] + [([k], hop(terms, [(top, k)])) for k in range(levels - 1)]
    )
    terms_other = pair_swap(terms, range(levels))
    terms, terms_other = terms.astype(F32), terms_other.astype(F32)
    diag_term_two = jnp.where(is_two, terms[:panel], terms_other[:panel])
    crossing = jnp.where(is_two, terms_other[:panel], terms[:panel])
    diag_term_one = jnp.where(is_two, terms_other[panel:], terms[panel:])

    at_top = level == top
    own = [jnp.where(at_top, a, b) for a, b in zip(packets, arrived)]
    other = []
    for k, (start, stop) in enumerate(cuts):
        piece = whole_other[(0 if k == 0 else start) : stop]
        other.append(jnp.where(at_top, piece, after(low_other[k], row_terms)))
    cross, factor = cross_factor(own[0], other[0])
    both = [
        panels_of(own[k], other[k], factor, stop - start)
        for k, (start, stop) in enumerate(cuts)
    ]
    sums = 0
    for (start, stop), piece in zip(cuts, both):
        sums = sums + wide_dot(piece.T, trail[start - panel : stop - panel])
    both = jnp.concatenate(both, 0)
    solved_two, tail = both[:, :panel], both[:, panel:]

    grad_diag_two = block_adjoint(
        diag_two, inverse_two, jnp.tril(adj_diag_two - diag_term_two)
    )
    mirror_two = grad_diag_two + grad_diag_two.T
    adj_two = -crossing - exact_dot(mirror_two, cross.astype(F32))
    head = exact_dot(adj_two, inverse_one).astype(BF16)
    seed_one = jnp.tril(adj_diag_one - wide_dot(head.T, cross) - diag_term_one)
    grad_diag_one = block_adjoint(diag_one, inverse_one, seed_one)
    mirror_one = grad_diag_one + grad_diag_one.T

    parts = sums.reshape(2, row_count, band, width)
    step = 1
    while step < row_count:
        low = (row_here // step) % 2 == 0
        parts = parts.reshape(2, -1, 2, band, width)
        keep = jnp.where(low, parts[:, :, 0], parts[:, :, 1])
        give = jnp.where(low, parts[:, :, 1], parts[:, :, 0])
        parts = keep + row_swap(give.astype(BF16), step).astype(F32)
        step *= 2
    parts = parts.reshape(2, band, width)

    head_wide = head.astype(F32)
    mix_two = jnp.concatenate([own_rows(mirror_two), own_rows(head_wide)], 1)
    mix_one = jnp.concatenate([own_rows(head_wide.T), own_rows(mirror_one)], 1)
    full_both = jnp.concatenate([full_two, full_one], 0)
    mix = jnp.concatenate([mix_two, mix_one], 0)
    mixed = wide_dot(
        jnp.concatenate(halves(mix), 1), jnp.concatenate([full_both, full_both], 0)
    )
    two_left = adj_row_two - mixed[:band] - parts[0]
    one_left = adj_row_one - mixed[band:] - parts[1]

    trail_left = adj_trail - wide_dot(both, full_both)
    column = lax.broadcasted_iota(jnp.int32, (1, width), 1)
    in_block = column >= last

    def put(matrix, block_one, block_two):
        block = jnp.where(here_one, block_one, block_two).astype(F32)
        block = jnp.pad(block, ((0, 0), (last, 0)))
        return jnp.where(in_block & (here_one | here_two), block, matrix)

    grad_trail = put(trail_left, tail, solved_two).astype(BF16)
    nothing = jnp.zeros((band, panel), F32)
    grad_row_one = put(one_left, nothing, nothing)
    grad_row_two = put(two_left, own_rows(head_wide), nothing)
    return (grad_trail, grad_row_one, grad_row_two, grad_diag_one, grad_diag_two)


def solution(mesh):
    split = P("row", "col")
    in_specs = (split, split, split, P(), P(), split, split, split, P(), P())
    out_specs = (split, split, split, P(), P())
    return jax.shard_map(
        per_device, mesh=mesh, in_specs=in_specs, out_specs=out_specs, check_vma=False
    )
```

```python
import functools

import jax
import jax.numpy as jnp
from jax import lax
from jax.experimental import pallas as pl
from jax.experimental.pallas import tpu as pltpu
from jax.sharding import PartitionSpec as P

EXACT = lax.Precision.HIGHEST
F32 = jnp.float32
BF16 = jnp.bfloat16
PIECES = 3


def exact_dot(a, b):
    return jnp.dot(a, b, precision=EXACT, preferred_element_type=F32)


def wide_dot(a, b):
    return jnp.dot(a, b, preferred_element_type=F32)


def halves(value):
    high = value.astype(BF16)
    return high, (value - high.astype(F32)).astype(BF16)


def halved_lower(matrix):
    order = matrix.shape[0]
    rows = lax.broadcasted_iota(jnp.int32, (order, order), 0)
    cols = lax.broadcasted_iota(jnp.int32, (order, order), 1)
    return jnp.where(rows > cols, matrix, jnp.where(rows == cols, 0.5 * matrix, 0))


def inverse_lower(blocks):
    order = blocks[0].shape[-1]
    rows = lax.broadcasted_iota(jnp.int32, (order, order), 0)
    cols = lax.broadcasted_iota(jnp.int32, (order, order), 1)
    equal = rows == cols
    inverses = []
    for block in blocks:
        recip_col = 1.0 / jnp.sum(jnp.where(equal, block, 0), 1, keepdims=True)
        recip_row = 1.0 / jnp.sum(jnp.where(equal, block, 0), 0, keepdims=True)
        pair = ((rows ^ cols) == 1) & (rows > cols)
        corner = jnp.where(pair, block, 0)
        inverses.append(jnp.where(equal, recip_col, 0) - recip_col * corner * recip_row)
    size = 2
    while size < order:
        below = ((rows ^ cols) & -size == size) & (rows > cols)
        below = below & ((rows ^ cols) < 2 * size)
        inner = [
            exact_dot(jnp.where(below, block, 0), inverse)
            for block, inverse in zip(blocks, inverses)
        ]
        inverses = [
            inverse - exact_dot(inverse, part) for inverse, part in zip(inverses, inner)
        ]
        size *= 2
    return inverses


def prepare_kernel(
    cuts, side_ref, one_ref, two_ref, adj_ref, inv_one_ref, inv_two_ref, whole_ref, *rest
):
    *piece_refs, rows_ref, sem = rest
    height, panel = rows_ref.shape
    fetch = pltpu.make_async_copy(
        adj_ref.at[:, pl.ds(adj_ref.shape[1] - panel, panel)], rows_ref, sem
    )
    fetch.start()
    inverse_one, inverse_two = inverse_lower([one_ref[...], two_ref[...]])
    inv_one_ref[...] = inverse_one
    inv_two_ref[...] = inverse_two
    chosen = jnp.where(side_ref[0] == 1, inverse_two, inverse_one)
    high, low = halves(chosen)
    whole_ref[:panel, :] = jnp.zeros((panel, panel), BF16)
    piece_refs[0][:panel, :] = jnp.zeros((panel, panel), BF16)
    fetch.wait()
    for k, ((start, stop), piece_ref) in enumerate(zip(cuts, piece_refs)):
        own_high, own_low = halves(rows_ref[start:stop, :])
        product = wide_dot(own_high, high) + (
            wide_dot(own_high, low) + wide_dot(own_low, high)
        )
        product = product.astype(BF16)
        whole_ref[panel + start : panel + stop, :] = product
        piece_ref[(panel if k == 0 else 0) :, :] = product


def prepare(side, diag_one, diag_two, adj_trail, cuts):
    height = adj_trail.shape[0]
    panel = diag_one.shape[0]
    vmem = pl.BlockSpec(memory_space=pltpu.VMEM)
    sizes = [stop - start for start, stop in cuts]
    sizes[0] += panel
    return pl.pallas_call(
        functools.partial(prepare_kernel, cuts),
        in_specs=[
            pl.BlockSpec(memory_space=pltpu.SMEM),
            vmem,
            vmem,
            pl.BlockSpec(memory_space=pl.ANY),
        ],
        out_specs=[vmem] * (3 + len(cuts)),
        out_shape=[jax.ShapeDtypeStruct((panel, panel), F32)] * 2
        + [jax.ShapeDtypeStruct((size, panel), BF16) for size in [panel + height] + sizes],
        scratch_shapes=[pltpu.VMEM((height, panel), F32), pltpu.SemaphoreType.DMA],
        compiler_params=pltpu.CompilerParams(vmem_limit_bytes=60 * 2**20),
        cost_estimate=pl.CostEstimate(
            flops=8 * height * panel * panel, bytes_accessed=6 * height * panel, transcendentals=0
        ),
        name="prepare",
    )(side, diag_one, diag_two, adj_trail)


def update_kernel(flags_ref, both_ref, rows_ref, adj_ref, *rest):
    out_ref = rest[-1]
    panel = both_ref.shape[1] // 2
    last = out_ref.shape[1] - panel
    both = both_ref[...]
    left = adj_ref[...] - wide_dot(both, rows_ref[...])
    out_ref[:, :last] = left[:, :last].astype(BF16)
    block = jnp.where(flags_ref[0] == 1, both[:, panel:], left[:, last:].astype(BF16))
    out_ref[:, last:] = jnp.where(flags_ref[1] == 1, both[:, :panel], block)


def update(flags, both, full_both, adj_trail, start, previous):
    height, width = adj_trail.shape
    rows, depth = both.shape
    tile = depth // 2
    first = start // tile
    operands = [flags, both, full_both, adj_trail]
    in_specs = [
        pl.BlockSpec(memory_space=pltpu.SMEM),
        pl.BlockSpec((tile, depth), lambda i: (i, 0)),
        pl.BlockSpec((depth, width), lambda i: (0, 0)),
        pl.BlockSpec((tile, width), lambda i: (first + i, 0)),
    ]
    if previous is not None:
        operands.append(previous)
        in_specs.append(pl.BlockSpec(memory_space=pl.ANY))
    return pl.pallas_call(
        update_kernel,
        grid=(rows // tile,),
        in_specs=in_specs,
        out_specs=pl.BlockSpec((tile, width), lambda i: (first + i, 0)),
        out_shape=jax.ShapeDtypeStruct((height, width), BF16),
        input_output_aliases={} if previous is None else {4: 0},
        compiler_params=pltpu.CompilerParams(vmem_limit_bytes=16 * 2**20),
        cost_estimate=pl.CostEstimate(
            flops=2 * rows * depth * width, bytes_accessed=6 * rows * width, transcendentals=0
        ),
        name="update",
    )(*operands)


def after(value, *others):
    return lax.optimization_barrier((value, *others))[0]


def block_adjoint(block, inverse, seed_adj):
    inner = halved_lower(exact_dot(block.T, seed_adj))
    middle = exact_dot(inverse.T, inner)
    return halved_lower(exact_dot(middle, inverse))


def per_device(
    trail,
    row_one,
    row_two,
    diag_one,
    diag_two,
    adj_trail,
    adj_row_one,
    adj_row_two,
    adj_diag_one,
    adj_diag_two,
):
    panel = diag_one.shape[0]
    height, width = trail.shape
    band = row_one.shape[0]
    last = width - panel
    row_count = lax.axis_size("row")
    col_count = lax.axis_size("col")
    levels = col_count // 2
    top = levels - 1
    row_here = lax.axis_index("row")
    col_here = lax.axis_index("col")
    row_start = row_here * band
    level = col_here // 2
    is_two = col_here % 2 == 1
    here_one = col_here == col_count - 2
    here_two = col_here == col_count - 1
    tiles = height // panel
    marks = [(k * (tiles + 1) + PIECES - 1) // PIECES - 1 for k in range(1, PIECES)]
    marks = [0] + marks + [tiles]
    cuts = [(a * panel, b * panel) for a, b in zip(marks, marks[1:])]
    final = len(cuts) - 1

    def own_rows(matrix):
        return lax.dynamic_slice_in_dim(matrix, row_start, band, 0)

    def row_swap(value, step):
        return lax.ppermute(value, "row", [(i, i ^ step) for i in range(row_count)])

    def pair_swap(value, which):
        pairs = [(2 * k + s, 2 * k + 1 - s) for k in which for s in range(2)]
        return lax.ppermute(value, "col", pairs)

    def gather_step(value, step):
        other = row_swap(value, step)
        low = (row_here // step) % 2 == 0
        return jnp.concatenate(
            [jnp.where(low, value, other), jnp.where(low, other, value)], 1
        )

    def gather_rest(value):
        step = 2
        while step < row_count:
            value = gather_step(value, step)
            step *= 2
        return value.reshape(panel, width)

    def choose(options):
        merged = []
        for members, array in options:
            for entry in merged:
                if entry[1] is array:
                    entry[0].extend(members)
                    break
            else:
                merged.append((list(members), array))
        chosen = merged[0][1]
        for members, array in merged[1:]:
            at = functools.reduce(jnp.logical_or, [level == k for k in members])
            chosen = jnp.where(at, array, chosen)
        return chosen

    def hop(value, hops):
        pairs = [(2 * a + s, 2 * b + s) for a, b in hops for s in range(2)]
        return lax.ppermute(value, "col", pairs)

    def spread_first(value):
        return hop(value, [(top, levels // 2 - 1)]) if levels > 1 else value

    def spread_rest(first):
        held = {max(levels // 2 - 1, 0): first}
        span = levels // 4
        while span >= 1:
            fresh = list(held)
            operand = choose([([k], held[k]) for k in fresh])
            up = hop(operand, [(k, k + span) for k in fresh])
            down = hop(operand, [(k, k - span) for k in fresh if k >= span])
            for k in fresh:
                held[k + span] = up
                if k >= span:
                    held[k - span] = down
            span //= 2
        return choose([([k], held[k]) for k in sorted(held)])

    near = gather_step(jnp.stack([row_two, row_one])[:, None], 1)
    near_two, near_one = near[:1], near[1:]
    full_two = gather_rest(near_two)
    side = is_two.astype(jnp.int32)[None]
    inverse_one, inverse_two, whole, *packets = prepare(
        side, after(diag_one, near_two), diag_two, adj_trail, cuts
    )
    whole = lax.dynamic_update_slice(whole, full_two[:, last:], (0, 0))
    packets[0] = lax.dynamic_update_slice(packets[0], full_two[:, last:], (0, 0))

    def cross_factor(own, other):
        cross = jnp.where(is_two, other[:panel], own[:panel])
        return cross, jnp.concatenate(halves(exact_dot(cross.astype(F32), inverse_one)), 0)

    def panels_of(own, other, factor, size):
        solved_two = jnp.where(is_two, own[-size:], other[-size:])
        base_one = jnp.where(is_two, other[-size:], own[-size:])
        tail = base_one.astype(F32) - wide_dot(
            jnp.concatenate([solved_two, solved_two], 1), factor
        )
        return jnp.concatenate([solved_two, tail.astype(BF16)], 1)

    whole_other = pair_swap(whole, [top])
    first = [spread_first(packet) for packet in packets]
    full_one = gather_rest(after(near_one, whole))
    full_both = jnp.concatenate([full_two, full_one], 0)
    arrived, low_other = [], []
    for k, value in enumerate(first):
        value = after(value, *first[max(k - 1, 0) : k], *arrived[: max(k - 1, 0)])
        arrived.append(spread_rest(value))
    for k, value in enumerate(arrived):
        value = after(value, first[min(k + 1, final)], *arrived[:k])
        low_other.append(pair_swap(value, range(levels - 1)))

    whole_other = after(whole_other, arrived[min(1, final)])
    _, top_factor = cross_factor(whole, whole_other)
    top_both = panels_of(whole, whole_other, top_factor, height)
    terms = wide_dot(top_both.T, trail[:, last:])
    placed = lax.dynamic_update_slice_in_dim(
        jnp.zeros((2 * panel, panel), F32),
        jnp.where(is_two, 0, adj_row_two[:, last:]),
        row_start,
        0,
    )
    terms = terms - placed
    own_terms = terms
    step = 1
    while step < row_count:
        pairs = [
            (i * col_count + c, (i ^ step) * col_count + c)
            for i in range(row_count)
            for c in (col_count - 2, col_count - 1)
        ]
        terms = terms + lax.ppermute(terms, ("row", "col"), pairs)
        step *= 2
    terms = row_terms = terms.astype(BF16)
    terms = choose(
        [([top], terms)] + [([k], hop(terms, [(top, k)])) for k in range(levels - 1)]
    )
    terms_other = pair_swap(terms, range(levels))
    terms, terms_other = terms.astype(F32), terms_other.astype(F32)
    diag_term_two = jnp.where(is_two, terms[:panel], terms_other[:panel])
    crossing = jnp.where(is_two, terms_other[:panel], terms[:panel])
    diag_term_one = jnp.where(is_two, terms_other[panel:], terms[panel:])

    at_top = level == top
    flags = jnp.stack([here_one, here_two]).astype(jnp.int32)
    sums = 0
    grad_trail = cross = None
    for k, (start, stop) in enumerate(cuts):
        top_piece = whole_other[(0 if k == 0 else panel + start) : panel + stop]
        low = after(low_other[k], own_terms)
        if k == final:
            low = after(low, row_terms, grad_trail)
        own = jnp.where(at_top, packets[k], arrived[k])
        other = jnp.where(at_top, top_piece, low)
        if k == 0:
            cross, factor = cross_factor(own, other)
        both = panels_of(own, other, factor, stop - start)
        sums = sums + wide_dot(both.T, trail[start:stop])
        if k < final:
            grad_trail = update(flags, both, full_both, adj_trail, start, grad_trail)

    parts = sums.reshape(2, row_count, band, width)
    step = 1
    while step < row_count:
        low = (row_here // step) % 2 == 0
        parts = parts.reshape(2, -1, 2, band, width)
        keep = jnp.where(low, parts[:, :, 0], parts[:, :, 1])
        give = jnp.where(low, parts[:, :, 1], parts[:, :, 0])
        give = give.astype(BF16)
        if 2 * step >= row_count:
            start = cuts[final][0]
            grad_trail = update(flags, both, full_both, adj_trail, start, grad_trail)
            give = sent = after(give, grad_trail)
        parts = keep + row_swap(give, step).astype(F32)
        step *= 2
    parts = parts.reshape(2, band, width)

    grad_diag_two = block_adjoint(
        diag_two, inverse_two, jnp.tril(adj_diag_two - after(diag_term_two, sent))
    )
    mirror_two = grad_diag_two + grad_diag_two.T
    adj_two = -crossing - exact_dot(mirror_two, cross.astype(F32))
    head = exact_dot(adj_two, inverse_one).astype(BF16)
    seed_one = jnp.tril(adj_diag_one - wide_dot(head.T, cross) - diag_term_one)
    grad_diag_one = block_adjoint(diag_one, inverse_one, seed_one)
    mirror_one = grad_diag_one + grad_diag_one.T

    head_wide = head.astype(F32)
    mix_two = jnp.concatenate([own_rows(mirror_two), own_rows(head_wide)], 1)
    mix_one = jnp.concatenate([own_rows(head_wide.T), own_rows(mirror_one)], 1)
    mix = jnp.concatenate([mix_two, mix_one], 0)
    mixed = wide_dot(
        jnp.concatenate(halves(mix), 1), jnp.concatenate([full_both, full_both], 0)
    )
    two_left = adj_row_two - mixed[:band] - parts[0]
    one_left = adj_row_one - mixed[band:] - parts[1]

    column = lax.broadcasted_iota(jnp.int32, (1, width), 1)
    in_block = column >= last

    def put(matrix, block_one, block_two):
        block = jnp.where(here_one, block_one, block_two).astype(F32)
        block = jnp.pad(block, ((0, 0), (last, 0)))
        return jnp.where(in_block & (here_one | here_two), block, matrix)

    nothing = jnp.zeros((band, panel), F32)
    grad_row_one = put(one_left, nothing, nothing)
    grad_row_two = put(two_left, own_rows(head_wide), nothing)
    return (grad_trail, grad_row_one, grad_row_two, grad_diag_one, grad_diag_two)


def solution(mesh):
    split = P("row", "col")
    in_specs = (split, split, split, P(), P(), split, split, split, P(), P())
    out_specs = (split, split, split, P(), P())
    return jax.shard_map(
        per_device, mesh=mesh, in_specs=in_specs, out_specs=out_specs, check_vma=False
    )
```

```python
import functools

import jax
import jax.numpy as jnp
from jax import lax
from jax.experimental import pallas as pl
from jax.experimental.pallas import tpu as pltpu
from jax.sharding import PartitionSpec as P

EXACT = lax.Precision.HIGHEST
F32 = jnp.float32
BF16 = jnp.bfloat16
PIECES = 2


def exact_dot(a, b):
    return jnp.dot(a, b, precision=EXACT, preferred_element_type=F32)


def wide_dot(a, b):
    return jnp.dot(a, b, preferred_element_type=F32)


def halves(value):
    high = value.astype(BF16)
    return high, (value - high.astype(F32)).astype(BF16)


def halved_lower(matrix):
    order = matrix.shape[0]
    rows = lax.broadcasted_iota(jnp.int32, (order, order), 0)
    cols = lax.broadcasted_iota(jnp.int32, (order, order), 1)
    return jnp.where(rows > cols, matrix, jnp.where(rows == cols, 0.5 * matrix, 0))


def split_dot(left, right):
    (left_high, left_low), (right_high, right_low) = left, right
    return wide_dot(
        jnp.concatenate([left_high, left_high, left_low], 1),
        jnp.concatenate([right_high, right_low, right_high], 0),
    )


def inverse_lower(blocks):
    order = blocks[0].shape[-1]
    rows = lax.broadcasted_iota(jnp.int32, (order, order), 0)
    cols = lax.broadcasted_iota(jnp.int32, (order, order), 1)
    equal = rows == cols
    inverses = []
    for block in blocks:
        recip_col = 1.0 / jnp.sum(jnp.where(equal, block, 0), 1, keepdims=True)
        recip_row = 1.0 / jnp.sum(jnp.where(equal, block, 0), 0, keepdims=True)
        pair = ((rows ^ cols) == 1) & (rows > cols)
        corner = jnp.where(pair, block, 0)
        inverses.append(jnp.where(equal, recip_col, 0) - recip_col * corner * recip_row)
    size = 2
    while size < order:
        below = ((rows ^ cols) & -size == size) & (rows > cols)
        below = below & ((rows ^ cols) < 2 * size)
        known = [halves(inverse) for inverse in inverses]
        inner = [
            split_dot(halves(jnp.where(below, block, 0)), pair)
            for block, pair in zip(blocks, known)
        ]
        inverses = [
            inverse - split_dot(pair, halves(part))
            for inverse, pair, part in zip(inverses, known, inner)
        ]
        size *= 2
    return inverses


def prepare_kernel(
    cuts,
    side_ref,
    one_ref,
    two_ref,
    adj_ref,
    inv_one_ref,
    inv_two_ref,
    whole_ref,
    *rest,
):
    *piece_refs, rows_ref, sem = rest
    panel = one_ref.shape[0]
    block = pl.ds(adj_ref.shape[1] - panel, panel)
    fetch = pltpu.make_async_copy(adj_ref.at[:, block], rows_ref, sem)
    fetch.start()
    inverse_one, inverse_two = inverse_lower([one_ref[...], two_ref[...]])
    inv_one_ref[...] = inverse_one
    inv_two_ref[...] = inverse_two
    chosen = halves(jnp.where(side_ref[0] == 1, inverse_two, inverse_one))
    fetch.wait()
    for (start, stop), piece_ref in zip(cuts, piece_refs):
        product = split_dot(halves(rows_ref[start:stop, :]), chosen).astype(BF16)
        whole_ref[start:stop, :] = product
        piece_ref[:panel, :] = jnp.zeros((panel, panel), BF16)
        piece_ref[panel:, :] = product


def prepare(side, diag_one, diag_two, adj_trail, cuts):
    height = adj_trail.shape[0]
    panel = diag_one.shape[0]
    vmem = pl.BlockSpec(memory_space=pltpu.VMEM)
    hbm = pl.BlockSpec(memory_space=pl.ANY)
    sizes = [panel + stop - start for start, stop in cuts]
    return pl.pallas_call(
        functools.partial(prepare_kernel, cuts),
        in_specs=[pl.BlockSpec(memory_space=pltpu.SMEM), vmem, vmem, hbm],
        out_specs=[vmem] * (3 + len(cuts)),
        out_shape=[jax.ShapeDtypeStruct((panel, panel), F32)] * 2
        + [jax.ShapeDtypeStruct((size, panel), BF16) for size in [height] + sizes],
        scratch_shapes=[pltpu.VMEM((height, panel), F32), pltpu.SemaphoreType.DMA],
        compiler_params=pltpu.CompilerParams(vmem_limit_bytes=56 * 2**20),
        cost_estimate=pl.CostEstimate(
            flops=8 * height * panel * panel, bytes_accessed=6 * height * panel, transcendentals=0
        ),
        name="prepare",
    )(side, diag_one, diag_two, adj_trail)


def update_kernel(flags_ref, both_ref, rows_ref, adj_ref, *rest):
    out_ref = rest[-1]
    panel = both_ref.shape[1] // 2
    last = out_ref.shape[1] - panel
    both = both_ref[...]
    left = adj_ref[...] - wide_dot(both, rows_ref[...])
    out_ref[:, :last] = left[:, :last].astype(BF16)
    block = jnp.where(flags_ref[0] == 1, both[:, panel:], left[:, last:].astype(BF16))
    out_ref[:, last:] = jnp.where(flags_ref[1] == 1, both[:, :panel], block)


def update(flags, both, full_both, adj_trail, start, previous):
    height, width = adj_trail.shape
    rows, depth = both.shape
    tile = depth
    first = start // tile
    operands = [flags, both, full_both, adj_trail]
    in_specs = [
        pl.BlockSpec(memory_space=pltpu.SMEM),
        pl.BlockSpec((tile, depth), lambda i: (i, 0)),
        pl.BlockSpec((depth, width), lambda i: (0, 0)),
        pl.BlockSpec((tile, width), lambda i: (first + i, 0)),
    ]
    if previous is not None:
        operands.append(previous)
        in_specs.append(pl.BlockSpec(memory_space=pl.ANY))
    return pl.pallas_call(
        update_kernel,
        grid=(rows // tile,),
        in_specs=in_specs,
        out_specs=pl.BlockSpec((tile, width), lambda i: (first + i, 0)),
        out_shape=jax.ShapeDtypeStruct((height, width), BF16),
        input_output_aliases={} if previous is None else {4: 0},
        compiler_params=pltpu.CompilerParams(vmem_limit_bytes=16 * 2**20),
        cost_estimate=pl.CostEstimate(
            flops=2 * rows * depth * width, bytes_accessed=6 * rows * width, transcendentals=0
        ),
        name="update",
    )(*operands)


def after(value, *others):
    return lax.optimization_barrier((value, *others))[0]


def block_adjoint(block, inverse, seed_adj):
    inner = halved_lower(exact_dot(block.T, seed_adj))
    middle = exact_dot(inverse.T, inner)
    return halved_lower(exact_dot(middle, inverse))


def per_device(
    trail,
    row_one,
    row_two,
    diag_one,
    diag_two,
    adj_trail,
    adj_row_one,
    adj_row_two,
    adj_diag_one,
    adj_diag_two,
):
    panel = diag_one.shape[0]
    height, width = trail.shape
    band = row_one.shape[0]
    last = width - panel
    row_count = lax.axis_size("row")
    col_count = lax.axis_size("col")
    levels = col_count // 2
    top = levels - 1
    row_here = lax.axis_index("row")
    col_here = lax.axis_index("col")
    row_start = row_here * band
    level = col_here // 2
    is_two = col_here % 2 == 1
    here_one = col_here == col_count - 2
    here_two = col_here == col_count - 1
    tile = 2 * panel
    marks = [k * (height // tile) // PIECES * tile for k in range(PIECES + 1)]
    cuts = list(zip(marks, marks[1:]))
    final = len(cuts) - 1

    def own_rows(matrix):
        return lax.dynamic_slice_in_dim(matrix, row_start, band, 0)

    def row_swap(value, step):
        return lax.ppermute(value, "row", [(i, i ^ step) for i in range(row_count)])

    def pair_swap(value, which):
        pairs = [(2 * k + s, 2 * k + 1 - s) for k in which for s in range(2)]
        return lax.ppermute(value, "col", pairs)

    def gather_step(value, step):
        other = row_swap(value, step)
        low = (row_here // step) % 2 == 0
        return jnp.concatenate(
            [jnp.where(low, value, other), jnp.where(low, other, value)], 1
        )

    def gather_rest(value):
        step = 2
        while step < row_count:
            value = gather_step(value, step)
            step *= 2
        return value.reshape(panel, width)

    def choose(options):
        merged = []
        for members, array in options:
            for entry in merged:
                if entry[1] is array:
                    entry[0].extend(members)
                    break
            else:
                merged.append((list(members), array))
        chosen = merged[0][1]
        for members, array in merged[1:]:
            at = functools.reduce(jnp.logical_or, [level == k for k in members])
            chosen = jnp.where(at, array, chosen)
        return chosen

    def hop(value, hops):
        pairs = [(2 * a + s, 2 * b + s) for a, b in hops for s in range(2)]
        return lax.ppermute(value, "col", pairs)

    def spread(pieces, gate):
        middle, span = levels // 2 - 1, levels // 4
        first, down = [], []
        for k in range(len(pieces) + 1):
            if k == 0:
                operand, hops = pieces[0], [(top, middle)]
            elif k < len(pieces):
                operand = jnp.where(level == top, pieces[k], first[-1])
                hops = [(top, middle), (middle, middle - span)]
            else:
                operand, hops = first[-1], [(middle, middle - span)]
            moved = hop(operand, hops)
            if k > 0:
                down.append(moved)
            if k < len(pieces):
                first.append(after(moved, gate) if k == 0 else moved)
        held = [
            {middle: here, middle - span: low, middle + span: hop(here, [(middle, middle + span)])}
            for here, low in zip(first, down)
        ]
        span //= 2
        while span >= 1:
            for piece in held:
                fresh = list(piece)
                operand = choose([([k], piece[k]) for k in fresh])
                up = hop(operand, [(k, k + span) for k in fresh])
                low = hop(operand, [(k, k - span) for k in fresh if k >= span])
                for k in fresh:
                    piece[k + span] = up
                    if k >= span:
                        piece[k - span] = low
            span //= 2
        arrived = []
        for piece in held:
            options = [([k], after(piece[k], *arrived)) for k in sorted(piece)]
            arrived.append(choose(options))
        return first, arrived

    near_two = gather_step(row_two[None, None], 1)
    near_one = gather_step(row_one[None, None], 1)
    full_two = gather_rest(near_two)
    side = is_two.astype(jnp.int32)[None]
    inverse_one, inverse_two, whole, *packets = prepare(
        side, after(diag_one, near_two, near_one), diag_two, adj_trail, cuts
    )
    own_cross = full_two[:, last:]
    packets[0] = lax.dynamic_update_slice(packets[0], own_cross, (0, 0))
    full_one = gather_rest(after(near_one, packets[0]))
    full_both = jnp.concatenate([full_two, full_one], 0)
    edge = after(trail[:, last:], packets[0])

    def factor_of(cross):
        return jnp.concatenate(halves(exact_dot(cross.astype(F32), inverse_one)), 0)

    def panels_of(own, other, factor, size):
        solved_two = jnp.where(is_two, own[-size:], other[-size:])
        base_one = jnp.where(is_two, other[-size:], own[-size:])
        tail = base_one.astype(F32) - wide_dot(
            jnp.concatenate([solved_two, solved_two], 1), factor
        )
        return jnp.concatenate([solved_two, tail.astype(BF16)], 1)

    whole_other = pair_swap(whole, [top])
    first, arrived = spread(packets, full_one)
    at_top = level == top
    other = []
    own = [jnp.where(at_top, a, b) for a, b in zip(packets, arrived)]
    for k, value in enumerate(arrived):
        value = own[0] if k == 0 else value
        other.append(pair_swap(value, range(levels if k == 0 else levels - 1)))

    whole_other = after(whole_other, first[final])
    top_both = panels_of(whole, whole_other, factor_of(own_cross), height)
    terms = wide_dot(top_both.T, edge)
    placed = lax.dynamic_update_slice_in_dim(
        jnp.zeros((2 * panel, panel), F32),
        jnp.where(is_two, 0, adj_row_two[:, last:]),
        row_start,
        0,
    )
    terms = terms - placed
    own_terms = terms
    step = 1
    while step < row_count:
        pairs = [
            (i * col_count + c, (i ^ step) * col_count + c)
            for i in range(row_count)
            for c in (col_count - 2, col_count - 1)
        ]
        terms = terms + lax.ppermute(terms, ("row", "col"), pairs)
        if step == 1:
            terms = after(terms, other[0])
        step *= 2
    terms = row_terms = terms.astype(BF16)
    terms = choose(
        [([top], terms)] + [([k], hop(terms, [(top, k)])) for k in range(levels - 1)]
    )
    terms_other = pair_swap(terms, range(levels))
    terms, terms_other = terms.astype(F32), terms_other.astype(F32)
    diag_term_two = jnp.where(is_two, terms[:panel], terms_other[:panel])
    crossing = jnp.where(is_two, terms_other[:panel], terms[:panel])
    diag_term_one = jnp.where(is_two, terms_other[panel:], terms[panel:])

    flags = jnp.stack([here_one, here_two]).astype(jnp.int32)
    cross = jnp.where(is_two, other[0][:panel], own[0][:panel])
    factor = factor_of(cross)
    sums = 0
    grad_trail = None
    for k, (start, stop) in enumerate(cuts):
        theirs = after(other[k], own_terms)
        if k == final:
            theirs = after(theirs, row_terms, grad_trail)
        if k > 0:
            theirs = jnp.where(at_top, whole_other[start:stop], theirs[panel:])
        both = panels_of(own[k], theirs, factor, stop - start)
        sums = sums + wide_dot(both.T, trail[start:stop])
        if k < final:
            grad_trail = update(flags, both, full_both, adj_trail, start, grad_trail)

    parts = sums.reshape(2, row_count, band, width)
    step = 1
    while step < row_count:
        low = (row_here // step) % 2 == 0
        parts = parts.reshape(2, -1, 2, band, width)
        keep = jnp.where(low, parts[:, :, 0], parts[:, :, 1])
        give = jnp.where(low, parts[:, :, 1], parts[:, :, 0])
        give = give.astype(BF16)
        if 2 * step >= row_count:
            start = cuts[final][0]
            grad_trail = update(flags, both, full_both, adj_trail, start, grad_trail)
            give = sent = after(give, grad_trail)
        parts = keep + row_swap(give, step).astype(F32)
        step *= 2
    parts = parts.reshape(2, band, width)

    grad_diag_two = block_adjoint(
        diag_two, inverse_two, jnp.tril(adj_diag_two - after(diag_term_two, sent))
    )
    mirror_two = grad_diag_two + grad_diag_two.T
    adj_two = -crossing - exact_dot(mirror_two, cross.astype(F32))
    head = exact_dot(adj_two, inverse_one).astype(BF16)
    seed_one = jnp.tril(adj_diag_one - wide_dot(head.T, cross) - diag_term_one)
    grad_diag_one = block_adjoint(diag_one, inverse_one, seed_one)
    mirror_one = grad_diag_one + grad_diag_one.T

    head_wide = head.astype(F32)
    mix_two = jnp.concatenate([own_rows(mirror_two), own_rows(head_wide)], 1)
    mix_one = jnp.concatenate([own_rows(head_wide.T), own_rows(mirror_one)], 1)
    mix = jnp.concatenate([mix_two, mix_one], 0)
    mixed = wide_dot(
        jnp.concatenate(halves(mix), 1), jnp.concatenate([full_both, full_both], 0)
    )
    two_left = adj_row_two - mixed[:band] - parts[0]
    one_left = adj_row_one - mixed[band:] - parts[1]

    column = lax.broadcasted_iota(jnp.int32, (1, width), 1)
    in_block = column >= last

    def put(matrix, block_one, block_two):
        block = jnp.where(here_one, block_one, block_two).astype(F32)
        block = jnp.pad(block, ((0, 0), (last, 0)))
        return jnp.where(in_block & (here_one | here_two), block, matrix)

    nothing = jnp.zeros((band, panel), F32)
    grad_row_one = put(one_left, nothing, nothing)
    grad_row_two = put(two_left, own_rows(head_wide), nothing)
    return (grad_trail, grad_row_one, grad_row_two, grad_diag_one, grad_diag_two)


def solution(mesh):
    split = P("row", "col")
    in_specs = (split, split, split, P(), P(), split, split, split, P(), P())
    out_specs = (split, split, split, P(), P())
    return jax.shard_map(
        per_device, mesh=mesh, in_specs=in_specs, out_specs=out_specs, check_vma=False
    )
```

```python
import functools

import jax
import jax.numpy as jnp
from jax import lax
from jax.experimental import pallas as pl
from jax.experimental.pallas import tpu as pltpu
from jax.sharding import PartitionSpec as P

EXACT = lax.Precision.HIGHEST
F32 = jnp.float32
BF16 = jnp.bfloat16
PIECES = 2


def exact_dot(a, b):
    return jnp.dot(a, b, precision=EXACT, preferred_element_type=F32)


def wide_dot(a, b):
    return jnp.dot(a, b, preferred_element_type=F32)


def halves(value):
    high = value.astype(BF16)
    return high, (value - high.astype(F32)).astype(BF16)


def halved_lower(matrix):
    order = matrix.shape[0]
    rows = lax.broadcasted_iota(jnp.int32, (order, order), 0)
    cols = lax.broadcasted_iota(jnp.int32, (order, order), 1)
    return jnp.where(rows > cols, matrix, jnp.where(rows == cols, 0.5 * matrix, 0))


def split_dot(left, right):
    (left_high, left_low), (right_high, right_low) = left, right
    return wide_dot(
        jnp.concatenate([left_high, left_high, left_low], 1),
        jnp.concatenate([right_high, right_low, right_high], 0),
    )


def inverse_lower(blocks):
    order = blocks[0].shape[-1]
    rows = lax.broadcasted_iota(jnp.int32, (order, order), 0)
    cols = lax.broadcasted_iota(jnp.int32, (order, order), 1)
    equal = rows == cols
    inverses = []
    for block in blocks:
        recip_col = 1.0 / jnp.sum(jnp.where(equal, block, 0), 1, keepdims=True)
        recip_row = 1.0 / jnp.sum(jnp.where(equal, block, 0), 0, keepdims=True)
        pair = ((rows ^ cols) == 1) & (rows > cols)
        corner = jnp.where(pair, block, 0)
        inverses.append(jnp.where(equal, recip_col, 0) - recip_col * corner * recip_row)
    size = 2
    while size < order:
        below = ((rows ^ cols) & -size == size) & (rows > cols)
        below = below & ((rows ^ cols) < 2 * size)
        known = [halves(inverse) for inverse in inverses]
        inner = [
            split_dot(halves(jnp.where(below, block, 0)), pair)
            for block, pair in zip(blocks, known)
        ]
        inverses = [
            inverse - split_dot(pair, halves(part))
            for inverse, pair, part in zip(inverses, known, inner)
        ]
        size *= 2
    return inverses


def prepare_kernel(
    cuts,
    side_ref,
    one_ref,
    two_ref,
    adj_ref,
    trail_ref,
    inv_one_ref,
    inv_two_ref,
    edge_ref,
    whole_ref,
    *rest,
):
    *piece_refs, rows_ref, sem, edge_sem = rest
    panel = one_ref.shape[0]
    block = pl.ds(adj_ref.shape[1] - panel, panel)
    fetch = pltpu.make_async_copy(adj_ref.at[:, block], rows_ref, sem)
    fetch.start()
    fetch_edge = pltpu.make_async_copy(trail_ref.at[:, block], edge_ref, edge_sem)
    fetch_edge.start()
    inverse_one, inverse_two = inverse_lower([one_ref[...], two_ref[...]])
    inv_one_ref[...] = inverse_one
    inv_two_ref[...] = inverse_two
    chosen = halves(jnp.where(side_ref[0] == 1, inverse_two, inverse_one))
    fetch.wait()
    for (start, stop), piece_ref in zip(cuts, piece_refs):
        product = split_dot(halves(rows_ref[start:stop, :]), chosen).astype(BF16)
        whole_ref[start:stop, :] = product
        piece_ref[:panel, :] = jnp.zeros((panel, panel), BF16)
        piece_ref[panel:, :] = product
    fetch_edge.wait()


def prepare(side, diag_one, diag_two, adj_trail, trail, cuts):
    height = adj_trail.shape[0]
    panel = diag_one.shape[0]
    vmem = pl.BlockSpec(memory_space=pltpu.VMEM)
    hbm = pl.BlockSpec(memory_space=pltpu.HBM)
    sizes = [panel + stop - start for start, stop in cuts]
    return pl.pallas_call(
        functools.partial(prepare_kernel, cuts),
        in_specs=[pl.BlockSpec(memory_space=pltpu.SMEM), vmem, vmem, hbm, hbm],
        out_specs=[vmem] * (4 + len(cuts)),
        out_shape=[jax.ShapeDtypeStruct((panel, panel), F32)] * 2
        + [jax.ShapeDtypeStruct((size, panel), BF16) for size in [height, height] + sizes],
        scratch_shapes=[
            pltpu.VMEM((height, panel), F32),
            pltpu.SemaphoreType.DMA,
            pltpu.SemaphoreType.DMA,
        ],
        compiler_params=pltpu.CompilerParams(vmem_limit_bytes=60 * 2**20),
        cost_estimate=pl.CostEstimate(
            flops=8 * height * panel * panel, bytes_accessed=8 * height * panel, transcendentals=0
        ),
        name="prepare",
    )(side, diag_one, diag_two, adj_trail, trail)


def gather_sums_kernel(start, both_ref, trail_ref, past_ref, out_ref, rows_ref, sems):
    rows, depth = both_ref.shape
    steps = [pl.ds(at, depth) for at in range(0, rows, depth)]
    fetches = [
        pltpu.make_async_copy(
            trail_ref.at[pl.ds(start + k * depth, depth), :], rows_ref.at[step, :], sems.at[k]
        )
        for k, step in enumerate(steps)
    ]
    for fetch in fetches:
        fetch.start()
    total = past_ref[...]
    for fetch, step in zip(fetches, steps):
        fetch.wait()
        total += lax.dot_general(
            both_ref[step, :],
            rows_ref[step, :],
            (((0,), (0,)), ((), ())),
            preferred_element_type=F32,
        )
    out_ref[...] = total


def gather_sums(both, trail, start, past):
    width = trail.shape[1]
    rows, depth = both.shape
    vmem = pl.BlockSpec(memory_space=pltpu.VMEM)
    return pl.pallas_call(
        functools.partial(gather_sums_kernel, start),
        in_specs=[vmem, pl.BlockSpec(memory_space=pltpu.HBM), vmem],
        out_specs=vmem,
        out_shape=jax.ShapeDtypeStruct((depth, width), F32),
        scratch_shapes=[
            pltpu.VMEM((rows, width), BF16),
            pltpu.SemaphoreType.DMA((rows // depth,)),
        ],
        compiler_params=pltpu.CompilerParams(vmem_limit_bytes=60 * 2**20),
        cost_estimate=pl.CostEstimate(
            flops=2 * rows * depth * width, bytes_accessed=2 * rows * width, transcendentals=0
        ),
        name="gather_sums",
    )(both, trail, past)


def update_kernel(start, flags_ref, both_ref, rows_ref, adj_ref, *rest):
    out_ref, adj_rows, out_rows, in_sems, out_sems = rest[-5:]
    rows, depth = both_ref.shape
    panel = depth // 2
    last = out_ref.shape[1] - panel
    fetches, stores, steps = [], [], []
    for k in range(rows // depth):
        step = pl.ds(k * depth, depth)
        place = pl.ds(start + k * depth, depth)
        steps.append(step)
        fetches.append(
            pltpu.make_async_copy(adj_ref.at[place, :], adj_rows.at[step, :], in_sems.at[k])
        )
        stores.append(
            pltpu.make_async_copy(out_rows.at[step, :], out_ref.at[place, :], out_sems.at[k])
        )
    for fetch in fetches:
        fetch.start()
    for fetch, store, step in zip(fetches, stores, steps):
        both = both_ref[step, :]
        product = wide_dot(both, rows_ref[...])
        fetch.wait()
        left = (adj_rows[step, :] - product).astype(BF16)
        out_rows[step, :last] = left[:, :last]
        block = jnp.where(flags_ref[0] == 1, both[:, panel:], left[:, last:])
        out_rows[step, last:] = jnp.where(flags_ref[1] == 1, both[:, :panel], block)
        store.start()
    for store in stores:
        store.wait()


def update(flags, both, full_both, adj_trail, start, previous):
    height, width = adj_trail.shape
    rows, depth = both.shape
    operands = [flags, both, full_both, adj_trail]
    vmem = pl.BlockSpec(memory_space=pltpu.VMEM)
    hbm = pl.BlockSpec(memory_space=pltpu.HBM)
    in_specs = [pl.BlockSpec(memory_space=pltpu.SMEM), vmem, vmem, hbm]
    if previous is not None:
        operands.append(previous)
        in_specs.append(hbm)
    return pl.pallas_call(
        functools.partial(update_kernel, start),
        in_specs=in_specs,
        out_specs=hbm,
        out_shape=jax.ShapeDtypeStruct((height, width), BF16),
        input_output_aliases={} if previous is None else {4: 0},
        scratch_shapes=[
            pltpu.VMEM((rows, width), F32),
            pltpu.VMEM((rows, width), BF16),
            pltpu.SemaphoreType.DMA((rows // depth,)),
            pltpu.SemaphoreType.DMA((rows // depth,)),
        ],
        compiler_params=pltpu.CompilerParams(vmem_limit_bytes=60 * 2**20),
        cost_estimate=pl.CostEstimate(
            flops=2 * rows * depth * width, bytes_accessed=6 * rows * width, transcendentals=0
        ),
        name="update",
    )(*operands)


def after(value, *others):
    return lax.optimization_barrier((value, *others))[0]


def block_adjoint(block, inverse, seed_adj):
    inner = halved_lower(exact_dot(block.T, seed_adj))
    middle = exact_dot(inverse.T, inner)
    return halved_lower(exact_dot(middle, inverse))


def per_device(
    trail,
    row_one,
    row_two,
    diag_one,
    diag_two,
    adj_trail,
    adj_row_one,
    adj_row_two,
    adj_diag_one,
    adj_diag_two,
):
    panel = diag_one.shape[0]
    height, width = trail.shape
    band = row_one.shape[0]
    last = width - panel
    row_count = lax.axis_size("row")
    col_count = lax.axis_size("col")
    levels = col_count // 2
    top = levels - 1
    row_here = lax.axis_index("row")
    col_here = lax.axis_index("col")
    row_start = row_here * band
    level = col_here // 2
    is_two = col_here % 2 == 1
    here_one = col_here == col_count - 2
    here_two = col_here == col_count - 1
    tile = 2 * panel
    marks = [k * (height // tile) // PIECES * tile for k in range(PIECES + 1)]
    cuts = list(zip(marks, marks[1:]))
    final = len(cuts) - 1

    def own_rows(matrix):
        return lax.dynamic_slice_in_dim(matrix, row_start, band, 0)

    def row_swap(value, step):
        return lax.ppermute(value, "row", [(i, i ^ step) for i in range(row_count)])

    def pair_swap(value, which):
        pairs = [(2 * k + s, 2 * k + 1 - s) for k in which for s in range(2)]
        return lax.ppermute(value, "col", pairs)

    def gather_step(value, step):
        other = row_swap(value, step)
        low = (row_here // step) % 2 == 0
        return jnp.concatenate(
            [jnp.where(low, value, other), jnp.where(low, other, value)], 1
        )

    def gather_rest(value):
        step = 2
        while step < row_count:
            value = gather_step(value, step)
            step *= 2
        return value.reshape(panel, width)

    def choose(options):
        merged = []
        for members, array in options:
            for entry in merged:
                if entry[1] is array:
                    entry[0].extend(members)
                    break
            else:
                merged.append((list(members), array))
        chosen = merged[0][1]
        for members, array in merged[1:]:
            at = functools.reduce(jnp.logical_or, [level == k for k in members])
            chosen = jnp.where(at, array, chosen)
        return chosen

    def hop(value, hops):
        pairs = [(2 * a + s, 2 * b + s) for a, b in hops for s in range(2)]
        return lax.ppermute(value, "col", pairs)

    def spread(pieces, gate):
        middle, span = levels // 2 - 1, levels // 4
        first, down = [], []
        for k in range(len(pieces) + 1):
            if k == 0:
                operand, hops = pieces[0], [(top, middle)]
            elif k < len(pieces):
                operand = jnp.where(level == top, pieces[k], first[-1])
                hops = [(top, middle), (middle, middle - span)]
            else:
                operand, hops = first[-1], [(middle, middle - span)]
            moved = hop(operand, hops)
            if k > 0:
                down.append(moved)
            if k < len(pieces):
                first.append(after(moved, gate) if k == 0 else moved)
        held = [
            {middle: here, middle - span: low, middle + span: hop(here, [(middle, middle + span)])}
            for here, low in zip(first, down)
        ]
        span //= 2
        while span >= 1:
            for piece in held:
                fresh = list(piece)
                operand = choose([([k], piece[k]) for k in fresh])
                up = hop(operand, [(k, k + span) for k in fresh])
                low = hop(operand, [(k, k - span) for k in fresh if k >= span])
                for k in fresh:
                    piece[k + span] = up
                    if k >= span:
                        piece[k - span] = low
            span //= 2
        arrived = []
        for piece in held:
            options = [([k], after(piece[k], *arrived)) for k in sorted(piece)]
            arrived.append(choose(options))
        return first, arrived

    near_two = gather_step(row_two[None, None], 1)
    near_one = gather_step(row_one[None, None], 1)
    full_two = gather_rest(near_two)
    side = is_two.astype(jnp.int32)[None]
    inverse_one, inverse_two, edge, whole, *packets = prepare(
        side, after(diag_one, near_two, near_one), diag_two, adj_trail, trail, cuts
    )
    own_cross = full_two[:, last:]
    packets[0] = lax.dynamic_update_slice(packets[0], own_cross, (0, 0))
    full_one = gather_rest(after(near_one, packets[0]))
    full_both = jnp.concatenate([full_two, full_one], 0)

    def factor_of(cross):
        return jnp.concatenate(halves(exact_dot(cross.astype(F32), inverse_one)), 0)

    def panels_of(own, other, factor, size):
        solved_two = jnp.where(is_two, own[-size:], other[-size:])
        base_one = jnp.where(is_two, other[-size:], own[-size:])
        tail = base_one.astype(F32) - wide_dot(
            jnp.concatenate([solved_two, solved_two], 1), factor
        )
        return jnp.concatenate([solved_two, tail.astype(BF16)], 1)

    whole_other = lax.ppermute(whole, "col", [(col_count - 1, col_count - 2)])
    first, arrived = spread(packets, full_one)
    at_top = level == top
    other = []
    own = [jnp.where(at_top, a, b) for a, b in zip(packets, arrived)]
    for value in own:
        other.append(pair_swap(value, range(levels)))

    whole_other = after(whole_other, first[final])
    top_both = panels_of(whole, whole_other, factor_of(own_cross), height)
    terms = wide_dot(top_both.T, edge)
    placed = lax.dynamic_update_slice_in_dim(
        jnp.zeros((2 * panel, panel), F32),
        jnp.where(is_two, 0, adj_row_two[:, last:]),
        row_start,
        0,
    )
    terms = terms - placed
    own_terms = terms
    step = 1
    while step < row_count:
        pairs = [
            (i * col_count + c, (i ^ step) * col_count + c)
            for i in range(row_count)
            for c in (col_count - 2, col_count - 1)
        ]
        if step > 1:
            terms = terms.astype(BF16)
        moved = lax.ppermute(terms, ("row", "col"), pairs)
        terms = terms.astype(F32) + moved.astype(F32)
        if step == 1:
            terms = after(terms, other[0])
        step *= 2
    terms = terms.astype(BF16)

    flags = jnp.stack([here_one, here_two]).astype(jnp.int32)
    cross = jnp.where(is_two, other[0][:panel], own[0][:panel])
    factor = factor_of(cross)
    sums = jnp.zeros((2 * panel, width), F32)
    grad_trail = None
    for (start, stop), mine, theirs in zip(cuts[:-1], own, other):
        both = panels_of(mine, after(theirs, own_terms), factor, stop - start)
        sums = gather_sums(both, trail, start, sums)
        grad_trail = update(flags, both, full_both, adj_trail, start, grad_trail)
    terms = choose(
        [([top], terms)] + [([k], hop(terms, [(top, k)])) for k in range(levels - 1)]
    )
    terms_other = pair_swap(after(terms, grad_trail), range(levels))
    terms, terms_other = terms.astype(F32), terms_other.astype(F32)
    diag_term_two = jnp.where(is_two, terms[:panel], terms_other[:panel])
    crossing = jnp.where(is_two, terms_other[:panel], terms[:panel])
    diag_term_one = jnp.where(is_two, terms_other[panel:], terms[panel:])

    start, stop = cuts[-1]
    theirs = after(other[-1], terms, sums, grad_trail)
    both = panels_of(own[-1], theirs, factor, stop - start)
    sums = gather_sums(both, trail, start, sums)

    parts = sums.reshape(2, row_count, band, width)
    step = 1
    while step < row_count:
        low = (row_here // step) % 2 == 0
        parts = parts.reshape(2, -1, 2, band, width)
        keep = jnp.where(low, parts[:, :, 0], parts[:, :, 1])
        give = jnp.where(low, parts[:, :, 1], parts[:, :, 0])
        give = give.astype(BF16)
        if 2 * step >= row_count:
            grad_trail = update(flags, both, full_both, adj_trail, start, grad_trail)
            give = sent = after(give, grad_trail)
        parts = keep + row_swap(give, step).astype(F32)
        step *= 2
    parts = parts.reshape(2, band, width)

    grad_diag_two = block_adjoint(
        diag_two, inverse_two, jnp.tril(adj_diag_two - after(diag_term_two, sent))
    )
    mirror_two = grad_diag_two + grad_diag_two.T
    adj_two = -crossing - exact_dot(mirror_two, cross.astype(F32))
    head = exact_dot(adj_two, inverse_one).astype(BF16)
    seed_one = jnp.tril(adj_diag_one - wide_dot(head.T, cross) - diag_term_one)
    grad_diag_one = block_adjoint(diag_one, inverse_one, seed_one)
    mirror_one = grad_diag_one + grad_diag_one.T

    head_wide = head.astype(F32)
    mix_two = jnp.concatenate([own_rows(mirror_two), own_rows(head_wide)], 1)
    mix_one = jnp.concatenate([own_rows(head_wide.T), own_rows(mirror_one)], 1)
    mix = jnp.concatenate([mix_two, mix_one], 0)
    mixed = wide_dot(
        jnp.concatenate(halves(mix), 1), jnp.concatenate([full_both, full_both], 0)
    )
    two_left = adj_row_two - mixed[:band] - parts[0]
    one_left = adj_row_one - mixed[band:] - parts[1]

    column = lax.broadcasted_iota(jnp.int32, (1, width), 1)
    in_block = column >= last

    def put(matrix, block_one, block_two):
        block = jnp.where(here_one, block_one, block_two).astype(F32)
        block = jnp.pad(block, ((0, 0), (last, 0)))
        return jnp.where(in_block & (here_one | here_two), block, matrix)

    nothing = jnp.zeros((band, panel), F32)
    grad_row_one = put(one_left, nothing, nothing)
    grad_row_two = put(two_left, own_rows(head_wide), nothing)
    return (grad_trail, grad_row_one, grad_row_two, grad_diag_one, grad_diag_two)


def solution(mesh):
    split = P("row", "col")
    in_specs = (split, split, split, P(), P(), split, split, split, P(), P())
    out_specs = (split, split, split, P(), P())
    return jax.shard_map(
        per_device, mesh=mesh, in_specs=in_specs, out_specs=out_specs, check_vma=False
    )
```

```python
import functools

import jax
import jax.numpy as jnp
from jax import lax
from jax.experimental import pallas as pl
from jax.experimental.pallas import tpu as pltpu
from jax.sharding import PartitionSpec as P

EXACT = lax.Precision.HIGHEST
F32 = jnp.float32
BF16 = jnp.bfloat16
PIECES = 2


def exact_dot(a, b):
    return jnp.dot(a, b, precision=EXACT, preferred_element_type=F32)


def wide_dot(a, b):
    return jnp.dot(a, b, preferred_element_type=F32)


def halves(value):
    high = value.astype(BF16)
    return high, (value - high.astype(F32)).astype(BF16)


def halved_lower(matrix):
    order = matrix.shape[0]
    rows = lax.broadcasted_iota(jnp.int32, (order, order), 0)
    cols = lax.broadcasted_iota(jnp.int32, (order, order), 1)
    return jnp.where(rows > cols, matrix, jnp.where(rows == cols, 0.5 * matrix, 0))


def split_dot(left, right):
    (left_high, left_low), (right_high, right_low) = left, right
    return wide_dot(
        jnp.concatenate([left_high, left_high, left_low], 1),
        jnp.concatenate([right_high, right_low, right_high], 0),
    )


def inverse_lower(blocks):
    order = blocks[0].shape[-1]
    rows = lax.broadcasted_iota(jnp.int32, (order, order), 0)
    cols = lax.broadcasted_iota(jnp.int32, (order, order), 1)
    equal = rows == cols
    inverses = []
    for block in blocks:
        recip_col = 1.0 / jnp.sum(jnp.where(equal, block, 0), 1, keepdims=True)
        recip_row = 1.0 / jnp.sum(jnp.where(equal, block, 0), 0, keepdims=True)
        pair = ((rows ^ cols) == 1) & (rows > cols)
        corner = jnp.where(pair, block, 0)
        inverses.append(jnp.where(equal, recip_col, 0) - recip_col * corner * recip_row)
    size = 2
    while size < order:
        below = ((rows ^ cols) & -size == size) & (rows > cols)
        below = below & ((rows ^ cols) < 2 * size)
        known = [halves(inverse) for inverse in inverses]
        inner = [
            split_dot(halves(jnp.where(below, block, 0)), pair)
            for block, pair in zip(blocks, known)
        ]
        inverses = [
            inverse - split_dot(pair, halves(part))
            for inverse, pair, part in zip(inverses, known, inner)
        ]
        size *= 2
    return inverses


def prepare_kernel(
    cuts,
    side_ref,
    one_ref,
    two_ref,
    adj_ref,
    inv_one_ref,
    inv_two_ref,
    whole_ref,
    *rest,
):
    *piece_refs, rows_ref, sem = rest
    panel = one_ref.shape[0]
    block = pl.ds(adj_ref.shape[1] - panel, panel)
    fetch = pltpu.make_async_copy(adj_ref.at[:, block], rows_ref, sem)
    fetch.start()
    inverse_one, inverse_two = inverse_lower([one_ref[...], two_ref[...]])
    inv_one_ref[...] = inverse_one
    inv_two_ref[...] = inverse_two
    chosen = halves(jnp.where(side_ref[0] == 1, inverse_two, inverse_one))
    whole_ref[:panel, :] = jnp.zeros((panel, panel), BF16)
    fetch.wait()
    for (start, stop), piece_ref in zip(cuts, piece_refs):
        product = split_dot(halves(rows_ref[start:stop, :]), chosen).astype(BF16)
        whole_ref[panel + start : panel + stop, :] = product
        piece_ref[:panel, :] = jnp.zeros((panel, panel), BF16)
        piece_ref[panel:, :] = product


def prepare(side, diag_one, diag_two, adj_trail, cuts):
    height = adj_trail.shape[0]
    panel = diag_one.shape[0]
    vmem = pl.BlockSpec(memory_space=pltpu.VMEM)
    hbm = pl.BlockSpec(memory_space=pltpu.HBM)
    sizes = [panel + stop - start for start, stop in cuts]
    return pl.pallas_call(
        functools.partial(prepare_kernel, cuts),
        in_specs=[pl.BlockSpec(memory_space=pltpu.SMEM), vmem, vmem, hbm],
        out_specs=[vmem] * (3 + len(cuts)),
        out_shape=[jax.ShapeDtypeStruct((panel, panel), F32)] * 2
        + [jax.ShapeDtypeStruct((size, panel), BF16) for size in [panel + height] + sizes],
        scratch_shapes=[
            pltpu.VMEM((height, panel), F32),
            pltpu.SemaphoreType.DMA,
        ],
        compiler_params=pltpu.CompilerParams(vmem_limit_bytes=60 * 2**20),
        cost_estimate=pl.CostEstimate(
            flops=8 * height * panel * panel, bytes_accessed=8 * height * panel, transcendentals=0
        ),
        name="prepare",
    )(side, diag_one, diag_two, adj_trail)


def blank(shape):
    return pl.pallas_call(
        lambda out_ref: None,
        out_specs=pl.BlockSpec(memory_space=pltpu.HBM),
        out_shape=jax.ShapeDtypeStruct(shape, BF16),
        name="blank",
    )()


def after(value, *others):
    return lax.optimization_barrier((value, *others))[0]


def block_adjoint(block, inverse, seed_adj):
    inner = halved_lower(exact_dot(block.T, seed_adj))
    middle = exact_dot(inverse.T, inner)
    return halved_lower(exact_dot(middle, inverse))


def per_device(
    trail,
    row_one,
    row_two,
    diag_one,
    diag_two,
    adj_trail,
    adj_row_one,
    adj_row_two,
    adj_diag_one,
    adj_diag_two,
):
    panel = diag_one.shape[0]
    height, width = trail.shape
    band = row_one.shape[0]
    last = width - panel
    row_count = lax.axis_size("row")
    col_count = lax.axis_size("col")
    levels = col_count // 2
    top = levels - 1
    row_here = lax.axis_index("row")
    col_here = lax.axis_index("col")
    row_start = row_here * band
    level = col_here // 2
    is_two = col_here % 2 == 1
    here_one = col_here == col_count - 2
    here_two = col_here == col_count - 1
    tile = 2 * panel
    marks = [k * (height // tile) // PIECES * tile for k in range(PIECES + 1)]
    cuts = list(zip(marks, marks[1:]))
    final = len(cuts) - 1

    def own_rows(matrix):
        return lax.dynamic_slice_in_dim(matrix, row_start, band, 0)

    def row_swap(value, step):
        return lax.ppermute(value, "row", [(i, i ^ step) for i in range(row_count)])

    def pair_swap(value, which):
        pairs = [(2 * k + s, 2 * k + 1 - s) for k in which for s in range(2)]
        return lax.ppermute(value, "col", pairs)

    def gather_step(value, step):
        other = row_swap(value, step)
        low = (row_here // step) % 2 == 0
        return jnp.concatenate(
            [jnp.where(low, value, other), jnp.where(low, other, value)], 1
        )

    def gather_rest(value):
        step = 2
        while step < row_count:
            value = gather_step(value, step)
            step *= 2
        return value.reshape(panel, width)

    def choose(options):
        merged = []
        for members, array in options:
            for entry in merged:
                if entry[1] is array:
                    entry[0].extend(members)
                    break
            else:
                merged.append((list(members), array))
        chosen = merged[0][1]
        for members, array in merged[1:]:
            at = functools.reduce(jnp.logical_or, [level == k for k in members])
            chosen = jnp.where(at, array, chosen)
        return chosen

    def hop(value, hops):
        pairs = [(2 * a + s, 2 * b + s) for a, b in hops for s in range(2)]
        return lax.ppermute(value, "col", pairs)

    def spread(pieces, gate):
        middle, span = levels // 2 - 1, levels // 4
        first, down = [], []
        for k in range(len(pieces) + 1):
            if k == 0:
                operand, hops = pieces[0], [(top, middle)]
            elif k < len(pieces):
                operand = jnp.where(level == top, pieces[k], first[-1])
                hops = [(top, middle), (middle, middle - span)]
            else:
                operand, hops = first[-1], [(middle, middle - span)]
            moved = hop(operand, hops)
            if k > 0:
                down.append(moved)
            if k < len(pieces):
                first.append(after(moved, gate) if k == 0 else moved)
        held = [
            {middle: here, middle - span: low, middle + span: hop(here, [(middle, middle + span)])}
            for here, low in zip(first, down)
        ]
        span //= 2
        while span >= 1:
            for piece in held:
                fresh = list(piece)
                operand = choose([([k], piece[k]) for k in fresh])
                up = hop(operand, [(k, k + span) for k in fresh])
                low = hop(operand, [(k, k - span) for k in fresh if k >= span])
                for k in fresh:
                    piece[k + span] = up
                    if k >= span:
                        piece[k - span] = low
            span //= 2
        arrived = []
        for piece in held:
            options = [([k], after(piece[k], *arrived)) for k in sorted(piece)]
            arrived.append(choose(options))
        return first, arrived

    near_two = gather_step(row_two[None, None], 1)
    near_one = gather_step(row_one[None, None], 1)
    full_two = gather_rest(near_two)
    side = is_two.astype(jnp.int32)[None]
    inverse_one, inverse_two, whole, *packets = prepare(
        side, after(diag_one, near_two, near_one), diag_two, adj_trail, cuts
    )
    own_cross = full_two[:, last:]
    whole = lax.dynamic_update_slice(whole, own_cross, (0, 0))
    packets[0] = lax.dynamic_update_slice(packets[0], own_cross, (0, 0))
    full_one = gather_rest(after(near_one, packets[0]))

    def factor_of(cross):
        return jnp.concatenate(halves(exact_dot(cross.astype(F32), inverse_one)), 0)

    def panels_of(own, other, factor, size):
        solved_two = jnp.where(is_two, own[-size:], other[-size:])
        base_one = jnp.where(is_two, other[-size:], own[-size:])
        tail = base_one.astype(F32) - wide_dot(
            jnp.concatenate([solved_two, solved_two], 1), factor
        )
        return jnp.concatenate([solved_two, tail.astype(BF16)], 1)

    one_owner, two_owner = col_count - 2, col_count - 1
    early_two = lax.ppermute(whole, "col", [(two_owner, one_owner)])
    first, arrived = spread(packets, full_one)
    early_one = lax.ppermute(after(whole, first[0]), "col", [(one_owner, two_owner)])
    at_top = level == top
    own = [jnp.where(at_top, a, b) for a, b in zip(packets, arrived)]
    other = [pair_swap(value, range(levels - 1)) for value in arrived]
    full_both = jnp.concatenate([full_two, after(full_one, arrived[0])], 0)

    early_two = after(early_two, arrived[final], other[0])
    top_both = panels_of(whole, early_two, factor_of(own_cross), height)
    terms = wide_dot(top_both.T, trail[:, last:])
    placed = lax.dynamic_update_slice_in_dim(
        jnp.zeros((2 * panel, panel), F32),
        jnp.where(is_two, 0, after(adj_row_two, first[final])[:, last:]),
        row_start,
        0,
    )
    terms = terms - placed
    own_terms = terms
    step = 1
    while step < row_count:
        pairs = [
            (i * col_count + c, (i ^ step) * col_count + c)
            for i in range(row_count)
            for c in (col_count - 2, col_count - 1)
        ]
        if step > 1:
            terms = terms.astype(BF16)
        moved = lax.ppermute(terms, ("row", "col"), pairs)
        terms = terms.astype(F32) + moved.astype(F32)
        step *= 2
    terms = terms.astype(BF16)

    whole_other = jnp.where(is_two, early_one, early_two)
    for k, (start, stop) in enumerate(cuts):
        piece = whole_other[(0 if k == 0 else panel + start) : panel + stop]
        low = other[k][-piece.shape[0] :]
        other[k] = jnp.where(at_top, piece, after(low, own_terms))
    cross = jnp.where(is_two, other[0][:panel], own[0][:panel])
    factor = factor_of(cross)
    column = lax.broadcasted_iota(jnp.int32, (1, width), 1)
    in_block = column >= last

    def put(matrix, block_one, block_two):
        block = jnp.where(here_one, block_one, block_two).astype(matrix.dtype)
        block = jnp.pad(block, ((0, 0), (last, 0)))
        return jnp.where(in_block & (here_one | here_two), block, matrix)

    def updated(both, start, previous):
        rows = adj_trail[start : start + both.shape[0]]
        left = (rows - wide_dot(both, full_both)).astype(BF16)
        left = put(left, both[:, panel:], both[:, :panel])
        return lax.dynamic_update_slice(previous, left, (start, 0))

    sums = 0
    grad_trail = blank((height, width))
    for (start, stop), mine, theirs in zip(cuts[:-1], own, other):
        both = panels_of(mine, theirs, factor, stop - start)
        sums = sums + wide_dot(both.T, trail[start:stop])
        grad_trail = updated(both, start, grad_trail)
    terms = choose(
        [([top], terms)] + [([k], hop(terms, [(top, k)])) for k in range(levels - 1)]
    )
    terms_other = pair_swap(after(terms, sums), range(levels))
    terms, terms_other = terms.astype(F32), terms_other.astype(F32)
    diag_term_two = jnp.where(is_two, terms[:panel], terms_other[:panel])
    crossing = jnp.where(is_two, terms_other[:panel], terms[:panel])
    diag_term_one = jnp.where(is_two, terms_other[panel:], terms[panel:])

    start, stop = cuts[-1]
    theirs = after(other[-1], terms, sums)
    both = panels_of(own[-1], theirs, factor, stop - start)
    sums = (sums + wide_dot(both.T, trail[start:stop])).astype(BF16)

    parts = sums.reshape(2, row_count, band, width)
    step = 1
    while step < row_count:
        low = (row_here // step) % 2 == 0
        parts = parts.reshape(2, -1, 2, band, width)
        keep = jnp.where(low, parts[:, :, 0], parts[:, :, 1])
        give = jnp.where(low, parts[:, :, 1], parts[:, :, 0])
        give = give.astype(BF16)
        sent = give
        parts = keep + row_swap(give, step).astype(F32)
        step *= 2
    parts = parts.reshape(2, band, width)
    grad_trail = updated(after(both, sent), start, grad_trail)

    grad_diag_two = block_adjoint(
        diag_two, inverse_two, jnp.tril(adj_diag_two - after(diag_term_two, sums))
    )
    mirror_two = grad_diag_two + grad_diag_two.T
    adj_two = -crossing - exact_dot(mirror_two, cross.astype(F32))
    head = exact_dot(adj_two, inverse_one).astype(BF16)
    seed_one = jnp.tril(adj_diag_one - wide_dot(head.T, cross) - diag_term_one)
    grad_diag_one = block_adjoint(diag_one, inverse_one, seed_one)
    mirror_one = grad_diag_one + grad_diag_one.T

    head_wide = head.astype(F32)
    mix_two = jnp.concatenate([own_rows(mirror_two), own_rows(head_wide)], 1)
    mix_one = jnp.concatenate([own_rows(head_wide.T), own_rows(mirror_one)], 1)
    mix = jnp.concatenate([mix_two, mix_one], 0)
    mixed = wide_dot(
        jnp.concatenate(halves(mix), 1), jnp.concatenate([full_both, full_both], 0)
    )
    two_left = adj_row_two - mixed[:band] - parts[0]
    one_left = adj_row_one - mixed[band:] - parts[1]

    nothing = jnp.zeros((band, panel), F32)
    grad_row_one = put(one_left, nothing, nothing)
    grad_row_two = put(two_left, own_rows(head_wide), nothing)
    return (grad_trail, grad_row_one, grad_row_two, grad_diag_one, grad_diag_two)


def solution(mesh):
    split = P("row", "col")
    in_specs = (split, split, split, P(), P(), split, split, split, P(), P())
    out_specs = (split, split, split, P(), P())
    return jax.shard_map(
        per_device, mesh=mesh, in_specs=in_specs, out_specs=out_specs, check_vma=False
    )
```

```python
import functools

import jax
import jax.numpy as jnp
from jax import lax
from jax.experimental import pallas as pl
from jax.experimental.pallas import tpu as pltpu
from jax.sharding import PartitionSpec as P

EXACT = lax.Precision.HIGHEST
F32 = jnp.float32
BF16 = jnp.bfloat16
PIECES = 2


def exact_dot(a, b):
    return jnp.dot(a, b, precision=EXACT, preferred_element_type=F32)


def wide_dot(a, b):
    return jnp.dot(a, b, preferred_element_type=F32)


def halves(value):
    high = value.astype(BF16)
    return high, (value - high.astype(F32)).astype(BF16)


def halved_lower(matrix):
    order = matrix.shape[0]
    rows = lax.broadcasted_iota(jnp.int32, (order, order), 0)
    cols = lax.broadcasted_iota(jnp.int32, (order, order), 1)
    return jnp.where(rows > cols, matrix, jnp.where(rows == cols, 0.5 * matrix, 0))


def split_dot(left, right):
    (left_high, left_low), (right_high, right_low) = left, right
    return wide_dot(
        jnp.concatenate([left_high, left_high, left_low], 1),
        jnp.concatenate([right_high, right_low, right_high], 0),
    )


def inverse_lower(blocks):
    order = blocks[0].shape[-1]
    rows = lax.broadcasted_iota(jnp.int32, (order, order), 0)
    cols = lax.broadcasted_iota(jnp.int32, (order, order), 1)
    equal = rows == cols
    inverses = []
    for block in blocks:
        recip_col = 1.0 / jnp.sum(jnp.where(equal, block, 0), 1, keepdims=True)
        recip_row = 1.0 / jnp.sum(jnp.where(equal, block, 0), 0, keepdims=True)
        pair = ((rows ^ cols) == 1) & (rows > cols)
        corner = jnp.where(pair, block, 0)
        inverses.append(jnp.where(equal, recip_col, 0) - recip_col * corner * recip_row)
    size = 2
    while size < order:
        below = ((rows ^ cols) & -size == size) & (rows > cols)
        below = below & ((rows ^ cols) < 2 * size)
        known = [halves(inverse) for inverse in inverses]
        inner = [
            split_dot(halves(jnp.where(below, block, 0)), pair)
            for block, pair in zip(blocks, known)
        ]
        inverses = [
            inverse - split_dot(pair, halves(part))
            for inverse, pair, part in zip(inverses, known, inner)
        ]
        size *= 2
    return inverses


def prepare_kernel(
    cuts,
    side_ref,
    one_ref,
    two_ref,
    adj_ref,
    inv_one_ref,
    inv_two_ref,
    whole_ref,
    *rest,
):
    *piece_refs, rows_ref, sem = rest
    panel = one_ref.shape[0]
    block = pl.ds(adj_ref.shape[1] - panel, panel)
    fetch = pltpu.make_async_copy(adj_ref.at[:, block], rows_ref, sem)
    fetch.start()
    inverse_one, inverse_two = inverse_lower([one_ref[...], two_ref[...]])
    inv_one_ref[...] = inverse_one
    inv_two_ref[...] = inverse_two
    chosen = halves(jnp.where(side_ref[0] == 1, inverse_two, inverse_one))
    fetch.wait()
    for (start, stop), piece_ref in zip(cuts, piece_refs):
        product = split_dot(halves(rows_ref[start:stop, :]), chosen).astype(BF16)
        whole_ref[start:stop, :] = product
        piece_ref[:panel, :] = jnp.zeros((panel, panel), BF16)
        piece_ref[panel:, :] = product


def prepare(side, diag_one, diag_two, adj_trail, cuts):
    height = adj_trail.shape[0]
    panel = diag_one.shape[0]
    vmem = pl.BlockSpec(memory_space=pltpu.VMEM)
    hbm = pl.BlockSpec(memory_space=pltpu.HBM)
    sizes = [panel + stop - start for start, stop in cuts]
    return pl.pallas_call(
        functools.partial(prepare_kernel, cuts),
        in_specs=[pl.BlockSpec(memory_space=pltpu.SMEM), vmem, vmem, hbm],
        out_specs=[vmem] * (3 + len(cuts)),
        out_shape=[jax.ShapeDtypeStruct((panel, panel), F32)] * 2
        + [jax.ShapeDtypeStruct((size, panel), BF16) for size in [height] + sizes],
        scratch_shapes=[
            pltpu.VMEM((height, panel), F32),
            pltpu.SemaphoreType.DMA,
        ],
        compiler_params=pltpu.CompilerParams(vmem_limit_bytes=60 * 2**20),
        cost_estimate=pl.CostEstimate(
            flops=8 * height * panel * panel, bytes_accessed=8 * height * panel, transcendentals=0
        ),
        name="prepare",
    )(side, diag_one, diag_two, adj_trail)


def blank(shape):
    return pl.pallas_call(
        lambda out_ref: None,
        out_specs=pl.BlockSpec(memory_space=pltpu.HBM),
        out_shape=jax.ShapeDtypeStruct(shape, BF16),
        name="blank",
    )()


def after(value, *others):
    return lax.optimization_barrier((value, *others))[0]


def block_adjoint(block, inverse, seed_adj):
    inner = halved_lower(exact_dot(block.T, seed_adj))
    middle = exact_dot(inverse.T, inner)
    return halved_lower(exact_dot(middle, inverse))


def per_device(
    trail,
    row_one,
    row_two,
    diag_one,
    diag_two,
    adj_trail,
    adj_row_one,
    adj_row_two,
    adj_diag_one,
    adj_diag_two,
):
    panel = diag_one.shape[0]
    height, width = trail.shape
    band = row_one.shape[0]
    last = width - panel
    row_count = lax.axis_size("row")
    col_count = lax.axis_size("col")
    levels = col_count // 2
    top = levels - 1
    row_here = lax.axis_index("row")
    col_here = lax.axis_index("col")
    row_start = row_here * band
    level = col_here // 2
    is_two = col_here % 2 == 1
    here_one = col_here == col_count - 2
    here_two = col_here == col_count - 1
    tile = 2 * panel
    marks = [k * (height // tile) // PIECES * tile for k in range(PIECES + 1)]
    cuts = list(zip(marks, marks[1:]))
    final = len(cuts) - 1

    def own_rows(matrix):
        return lax.dynamic_slice_in_dim(matrix, row_start, band, 0)

    def row_swap(value, step):
        return lax.ppermute(value, "row", [(i, i ^ step) for i in range(row_count)])

    def pair_swap(value, which):
        pairs = [(2 * k + s, 2 * k + 1 - s) for k in which for s in range(2)]
        return lax.ppermute(value, "col", pairs)

    def gather_step(value, step):
        other = row_swap(value, step)
        low = (row_here // step) % 2 == 0
        return jnp.concatenate(
            [jnp.where(low, value, other), jnp.where(low, other, value)], 1
        )

    def gather_rest(value):
        step = 2
        while step < row_count:
            value = gather_step(value, step)
            step *= 2
        return value.reshape(panel, width)

    def choose(options):
        merged = []
        for members, array in options:
            for entry in merged:
                if entry[1] is array:
                    entry[0].extend(members)
                    break
            else:
                merged.append((list(members), array))
        chosen = merged[0][1]
        for members, array in merged[1:]:
            at = functools.reduce(jnp.logical_or, [level == k for k in members])
            chosen = jnp.where(at, array, chosen)
        return chosen

    def hop(value, hops):
        pairs = [(2 * a + s, 2 * b + s) for a, b in hops for s in range(2)]
        return lax.ppermute(value, "col", pairs)

    def spread(pieces, gate):
        middle, span = levels // 2 - 1, levels // 4
        first, down = [], []
        for k in range(len(pieces) + 1):
            if k == 0:
                operand, hops = pieces[0], [(top, middle)]
            elif k < len(pieces):
                operand = jnp.where(level == top, pieces[k], first[-1])
                hops = [(top, middle), (middle, middle - span)]
            else:
                operand, hops = first[-1], [(middle, middle - span)]
            moved = hop(operand, hops)
            if k > 0:
                down.append(moved)
            if k < len(pieces):
                first.append(after(moved, gate) if k == 0 else moved)
        held = [
            {middle: here, middle - span: low, middle + span: hop(here, [(middle, middle + span)])}
            for here, low in zip(first, down)
        ]
        span //= 2
        while span >= 1:
            for piece in held:
                fresh = list(piece)
                operand = choose([([k], piece[k]) for k in fresh])
                up = hop(operand, [(k, k + span) for k in fresh])
                low = hop(operand, [(k, k - span) for k in fresh if k >= span])
                for k in fresh:
                    piece[k + span] = up
                    if k >= span:
                        piece[k - span] = low
            span //= 2
        arrived = []
        for piece in held:
            options = [([k], after(piece[k], *arrived)) for k in sorted(piece)]
            arrived.append(choose(options))
        return first, arrived

    near_two = gather_step(row_two[None, None], 1)
    near_one = gather_step(row_one[None, None], 1)
    full_two = gather_rest(near_two)
    side = is_two.astype(jnp.int32)[None]
    inverse_one, inverse_two, whole, *packets = prepare(
        side, diag_one, diag_two, adj_trail, cuts
    )
    own_cross = full_two[:, last:]
    one_owner, two_owner = col_count - 2, col_count - 1
    lent_cross = lax.ppermute(own_cross, "col", [(one_owner, two_owner)])
    packets[final] = lax.dynamic_update_slice(
        packets[final], jnp.where(is_two, lent_cross, own_cross), (0, 0)
    )

    def factor_of(cross):
        return jnp.concatenate(halves(exact_dot(cross.astype(F32), inverse_one)), 0)

    def panels_of(own, other, factor, size):
        solved_two = jnp.where(is_two, own[-size:], other[-size:])
        base_one = jnp.where(is_two, other[-size:], own[-size:])
        tail = base_one.astype(F32) - wide_dot(
            jnp.concatenate([solved_two, solved_two], 1), factor
        )
        return jnp.concatenate([solved_two, tail.astype(BF16)], 1)

    early_two = [
        lax.ppermute(packet, "col", [(two_owner, one_owner)]) for packet in packets
    ]
    first, arrived = spread(packets, early_two[0])
    full_one = gather_rest(after(near_one, first[0]))
    early_one = lax.ppermute(after(whole, first[0]), "col", [(one_owner, two_owner)])
    at_top = level == top
    own = [jnp.where(at_top, a, b) for a, b in zip(packets, arrived)]
    other = [pair_swap(value, range(levels - 1)) for value in arrived]
    full_both = jnp.concatenate([full_two, after(full_one, arrived[0])], 0)

    early_two = jnp.concatenate([piece[panel:] for piece in early_two], 0)
    early_two = after(early_two, arrived[final], other[0])
    top_both = panels_of(whole, early_two, factor_of(own_cross), height)
    terms = wide_dot(top_both.T, trail[:, last:])
    placed = lax.dynamic_update_slice_in_dim(
        jnp.zeros((2 * panel, panel), F32),
        jnp.where(is_two, 0, after(adj_row_two, first[final])[:, last:]),
        row_start,
        0,
    )
    terms = terms - placed
    own_terms = terms
    step = 1
    while step < row_count:
        pairs = [
            (i * col_count + c, (i ^ step) * col_count + c)
            for i in range(row_count)
            for c in (col_count - 2, col_count - 1)
        ]
        if step > 1:
            terms = terms.astype(BF16)
        moved = lax.ppermute(terms, ("row", "col"), pairs)
        terms = terms.astype(F32) + moved.astype(F32)
        step *= 2
    terms = terms.astype(BF16)

    whole_other = jnp.where(is_two, after(early_one, own_terms), early_two)
    for k, (start, stop) in enumerate(cuts):
        low = after(other[k][panel:], own_terms, *other[:k])
        other[k] = jnp.where(at_top, whole_other[start:stop], low)
    cross = own[final][:panel]
    factor = factor_of(cross)
    column = lax.broadcasted_iota(jnp.int32, (1, width), 1)
    in_block = column >= last

    def put(matrix, block_one, block_two):
        block = jnp.where(here_one, block_one, block_two).astype(matrix.dtype)
        block = jnp.pad(block, ((0, 0), (last, 0)))
        return jnp.where(in_block & (here_one | here_two), block, matrix)

    def updated(both, start, previous):
        rows = adj_trail[start : start + both.shape[0]]
        left = (rows - wide_dot(both, full_both)).astype(BF16)
        left = put(left, both[:, panel:], both[:, :panel])
        return lax.dynamic_update_slice(previous, left, (start, 0))

    sums = 0
    grad_trail = blank((height, width))
    for (start, stop), mine, theirs in zip(cuts[:-1], own, other):
        both = panels_of(mine, theirs, factor, stop - start)
        sums = sums + wide_dot(both.T, trail[start:stop])
        grad_trail = updated(both, start, grad_trail)
    terms = choose(
        [([top], terms)] + [([k], hop(terms, [(top, k)])) for k in range(levels - 1)]
    )
    terms_other = pair_swap(after(terms, sums), range(levels))
    terms, terms_other = terms.astype(F32), terms_other.astype(F32)
    diag_term_two = jnp.where(is_two, terms[:panel], terms_other[:panel])
    crossing = jnp.where(is_two, terms_other[:panel], terms[:panel])
    diag_term_one = jnp.where(is_two, terms_other[panel:], terms[panel:])

    start, stop = cuts[-1]
    theirs = after(other[-1], terms, sums)
    both = panels_of(own[-1], theirs, factor, stop - start)
    sums = (sums + wide_dot(both.T, trail[start:stop])).astype(BF16)

    parts = sums.reshape(2, row_count, band, width)
    step = 1
    while step < row_count:
        low = (row_here // step) % 2 == 0
        parts = parts.reshape(2, -1, 2, band, width)
        keep = jnp.where(low, parts[:, :, 0], parts[:, :, 1])
        give = jnp.where(low, parts[:, :, 1], parts[:, :, 0])
        give = give.astype(BF16)
        sent = give
        parts = keep + row_swap(give, step).astype(F32)
        step *= 2
    parts = parts.reshape(2, band, width)
    grad_trail = updated(after(both, sent), start, grad_trail)

    grad_diag_two = block_adjoint(
        diag_two, inverse_two, jnp.tril(adj_diag_two - diag_term_two)
    )
    mirror_two = grad_diag_two + grad_diag_two.T
    adj_two = -crossing - exact_dot(mirror_two, cross.astype(F32))
    head = exact_dot(adj_two, inverse_one).astype(BF16)
    seed_one = jnp.tril(adj_diag_one - wide_dot(head.T, cross) - diag_term_one)
    grad_diag_one = block_adjoint(diag_one, inverse_one, seed_one)
    mirror_one = grad_diag_one + grad_diag_one.T

    head_wide = head.astype(F32)
    mix_two = jnp.concatenate([own_rows(mirror_two), own_rows(head_wide)], 1)
    mix_one = jnp.concatenate([own_rows(head_wide.T), own_rows(mirror_one)], 1)
    mix = jnp.concatenate([mix_two, mix_one], 0)
    mixed = wide_dot(
        jnp.concatenate(halves(mix), 1), jnp.concatenate([full_both, full_both], 0)
    )
    two_left = adj_row_two - mixed[:band] - parts[0]
    one_left = adj_row_one - mixed[band:] - parts[1]

    nothing = jnp.zeros((band, panel), F32)
    grad_row_one = put(one_left, nothing, nothing)
    grad_row_two = put(two_left, own_rows(head_wide), nothing)
    return (grad_trail, grad_row_one, grad_row_two, grad_diag_one, grad_diag_two)


def solution(mesh):
    split = P("row", "col")
    in_specs = (split, split, split, P(), P(), split, split, split, P(), P())
    out_specs = (split, split, split, P(), P())
    return jax.shard_map(
        per_device, mesh=mesh, in_specs=in_specs, out_specs=out_specs, check_vma=False
    )
```

```python
import functools

import jax
import jax.numpy as jnp
from jax import lax
from jax.experimental import pallas as pl
from jax.experimental.pallas import tpu as pltpu
from jax.sharding import PartitionSpec as P

EXACT = lax.Precision.HIGHEST
F32 = jnp.float32
BF16 = jnp.bfloat16
PIECES = 2


def exact_dot(a, b):
    return jnp.dot(a, b, precision=EXACT, preferred_element_type=F32)


def wide_dot(a, b):
    return jnp.dot(a, b, preferred_element_type=F32)


def halves(value):
    high = value.astype(BF16)
    return high, (value - high.astype(F32)).astype(BF16)


def halved_lower(matrix):
    order = matrix.shape[0]
    rows = lax.broadcasted_iota(jnp.int32, (order, order), 0)
    cols = lax.broadcasted_iota(jnp.int32, (order, order), 1)
    return jnp.where(rows > cols, matrix, jnp.where(rows == cols, 0.5 * matrix, 0))


def split_dot(left, right):
    (left_high, left_low), (right_high, right_low) = left, right
    return wide_dot(
        jnp.concatenate([left_high, left_high, left_low], 1),
        jnp.concatenate([right_high, right_low, right_high], 0),
    )


def inverse_lower(blocks):
    order = blocks[0].shape[-1]
    rows = lax.broadcasted_iota(jnp.int32, (order, order), 0)
    cols = lax.broadcasted_iota(jnp.int32, (order, order), 1)
    equal = rows == cols
    inverses = []
    for block in blocks:
        recip_col = 1.0 / jnp.sum(jnp.where(equal, block, 0), 1, keepdims=True)
        recip_row = 1.0 / jnp.sum(jnp.where(equal, block, 0), 0, keepdims=True)
        pair = ((rows ^ cols) == 1) & (rows > cols)
        corner = jnp.where(pair, block, 0)
        inverses.append(jnp.where(equal, recip_col, 0) - recip_col * corner * recip_row)
    size = 2
    while size < order:
        below = ((rows ^ cols) & -size == size) & (rows > cols)
        below = below & ((rows ^ cols) < 2 * size)
        known = [halves(inverse) for inverse in inverses]
        inner = [
            split_dot(halves(jnp.where(below, block, 0)), pair)
            for block, pair in zip(blocks, known)
        ]
        inverses = [
            inverse - split_dot(pair, halves(part))
            for inverse, pair, part in zip(inverses, known, inner)
        ]
        size *= 2
    return inverses


def prepare_kernel(
    cuts,
    side_ref,
    one_ref,
    two_ref,
    adj_ref,
    inv_one_ref,
    inv_two_ref,
    whole_ref,
    *rest,
):
    *piece_refs, rows_ref, sem = rest
    panel = one_ref.shape[0]
    block = pl.ds(adj_ref.shape[1] - panel, panel)
    fetch = pltpu.make_async_copy(adj_ref.at[:, block], rows_ref, sem)
    fetch.start()
    inverse_one, inverse_two = inverse_lower([one_ref[...], two_ref[...]])
    inv_one_ref[...] = inverse_one
    inv_two_ref[...] = inverse_two
    chosen = halves(jnp.where(side_ref[0] == 1, inverse_two, inverse_one))
    fetch.wait()
    for (start, stop), piece_ref in zip(cuts, piece_refs):
        product = split_dot(halves(rows_ref[start:stop, :]), chosen).astype(BF16)
        whole_ref[start:stop, :] = product
        piece_ref[:panel, :] = jnp.zeros((panel, panel), BF16)
        piece_ref[panel:, :] = product


def prepare(side, diag_one, diag_two, adj_trail, cuts):
    height = adj_trail.shape[0]
    panel = diag_one.shape[0]
    vmem = pl.BlockSpec(memory_space=pltpu.VMEM)
    hbm = pl.BlockSpec(memory_space=pltpu.HBM)
    sizes = [panel + stop - start for start, stop in cuts]
    return pl.pallas_call(
        functools.partial(prepare_kernel, cuts),
        in_specs=[pl.BlockSpec(memory_space=pltpu.SMEM), vmem, vmem, hbm],
        out_specs=[vmem] * (3 + len(cuts)),
        out_shape=[jax.ShapeDtypeStruct((panel, panel), F32)] * 2
        + [jax.ShapeDtypeStruct((size, panel), BF16) for size in [height] + sizes],
        scratch_shapes=[
            pltpu.VMEM((height, panel), F32),
            pltpu.SemaphoreType.DMA,
        ],
        compiler_params=pltpu.CompilerParams(vmem_limit_bytes=60 * 2**20),
        cost_estimate=pl.CostEstimate(
            flops=8 * height * panel * panel, bytes_accessed=8 * height * panel, transcendentals=0
        ),
        name="prepare",
    )(side, diag_one, diag_two, adj_trail)


def blank(shape):
    return pl.pallas_call(
        lambda out_ref: None,
        out_specs=pl.BlockSpec(memory_space=pltpu.HBM),
        out_shape=jax.ShapeDtypeStruct(shape, BF16),
        name="blank",
    )()


def after(value, *others):
    return lax.optimization_barrier((value, *others))[0]


def block_adjoint(block, inverse, seed_adj):
    inner = halved_lower(exact_dot(block.T, seed_adj))
    middle = exact_dot(inverse.T, inner)
    return halved_lower(exact_dot(middle, inverse))


def per_device(
    trail,
    row_one,
    row_two,
    diag_one,
    diag_two,
    adj_trail,
    adj_row_one,
    adj_row_two,
    adj_diag_one,
    adj_diag_two,
):
    panel = diag_one.shape[0]
    height, width = trail.shape
    band = row_one.shape[0]
    last = width - panel
    row_count = lax.axis_size("row")
    col_count = lax.axis_size("col")
    levels = col_count // 2
    top = levels - 1
    row_here = lax.axis_index("row")
    col_here = lax.axis_index("col")
    row_start = row_here * band
    level = col_here // 2
    is_two = col_here % 2 == 1
    here_one = col_here == col_count - 2
    here_two = col_here == col_count - 1
    tile = 2 * panel
    marks = [k * (height // tile) // PIECES * tile for k in range(PIECES + 1)]
    cuts = list(zip(marks, marks[1:]))
    final = len(cuts) - 1

    def own_rows(matrix):
        return lax.dynamic_slice_in_dim(matrix, row_start, band, 0)

    def row_swap(value, step):
        return lax.ppermute(value, "row", [(i, i ^ step) for i in range(row_count)])

    def pair_swap(value, which):
        pairs = [(2 * k + s, 2 * k + 1 - s) for k in which for s in range(2)]
        return lax.ppermute(value, "col", pairs)

    def gather_step(value, step):
        other = row_swap(value, step)
        low = (row_here // step) % 2 == 0
        return jnp.concatenate(
            [jnp.where(low, value, other), jnp.where(low, other, value)], 1
        )

    def gather_rest(value):
        step = 2
        while step < row_count:
            value = gather_step(value, step)
            step *= 2
        return value.reshape(panel, width)

    def choose(options):
        merged = []
        for members, array in options:
            for entry in merged:
                if entry[1] is array:
                    entry[0].extend(members)
                    break
            else:
                merged.append((list(members), array))
        chosen = merged[0][1]
        for members, array in merged[1:]:
            at = functools.reduce(jnp.logical_or, [level == k for k in members])
            chosen = jnp.where(at, array, chosen)
        return chosen

    def hop(value, hops):
        pairs = [(2 * a + s, 2 * b + s) for a, b in hops for s in range(2)]
        return lax.ppermute(value, "col", pairs)

    def spread(pieces, gates, extra):
        middle, span = levels // 2 - 1, levels // 4
        first, down = [], []
        extra_moved = hop(extra, [(top, middle)])
        for k in range(len(pieces) + 1):
            if k == 0:
                operand, hops = pieces[0], [(top, middle)]
            elif k < len(pieces):
                operand = jnp.where(level == top, pieces[k], first[-1])
                hops = [(top, middle), (middle, middle - span)]
            else:
                operand, hops = first[-1], [(middle, middle - span)]
            moved = hop(operand, hops)
            if k > 0:
                down.append(moved)
            if k < len(pieces):
                moved = after(moved, gates[k]) if k < len(gates) else moved
                if k == len(pieces) - 1:
                    moved = lax.dynamic_update_slice(moved, extra_moved, (0, 0))
                first.append(moved)
        held = [
            {middle: here, middle - span: low, middle + span: hop(here, [(middle, middle + span)])}
            for here, low in zip(first, down)
        ]
        span //= 2
        while span >= 1:
            for piece in held:
                fresh = list(piece)
                operand = choose([([k], piece[k]) for k in fresh])
                up = hop(operand, [(k, k + span) for k in fresh])
                low = hop(operand, [(k, k - span) for k in fresh if k >= span])
                for k in fresh:
                    piece[k + span] = up
                    if k >= span:
                        piece[k - span] = low
            span //= 2
        arrived = []
        for piece in held:
            options = [([k], after(piece[k], *arrived)) for k in sorted(piece)]
            arrived.append(choose(options))
        return first, arrived

    near_two = gather_step(row_two[None, None], 1)
    near_one = gather_step(row_one[None, None], 1)
    full_two = gather_rest(near_two)
    side = is_two.astype(jnp.int32)[None]
    inverse_one, inverse_two, whole, *packets = prepare(
        side, diag_one, diag_two, adj_trail, cuts
    )
    own_cross = full_two[:, last:]
    one_owner, two_owner = col_count - 2, col_count - 1
    lent_cross = lax.ppermute(own_cross, "col", [(one_owner, two_owner)])
    side_cross = jnp.where(is_two, lent_cross, own_cross)

    def factor_of(cross):
        return jnp.concatenate(halves(exact_dot(cross.astype(F32), inverse_one)), 0)

    def panels_of(own, other, factor, size):
        solved_two = jnp.where(is_two, own[-size:], other[-size:])
        base_one = jnp.where(is_two, other[-size:], own[-size:])
        tail = base_one.astype(F32) - wide_dot(
            jnp.concatenate([solved_two, solved_two], 1), factor
        )
        return jnp.concatenate([solved_two, tail.astype(BF16)], 1)

    early_two = [
        lax.ppermute(packet, "col", [(two_owner, one_owner)]) for packet in packets
    ]
    full_one = gather_rest(after(near_one, full_two))
    first, arrived = spread(packets, [early_two[0], full_one], side_cross)
    early_one = lax.ppermute(after(whole, first[0]), "col", [(one_owner, two_owner)])
    at_top = level == top
    own = [jnp.where(at_top, a, b) for a, b in zip(packets, arrived)]
    other = [pair_swap(value, range(levels - 1)) for value in arrived]
    full_both = jnp.concatenate([full_two, after(full_one, arrived[0])], 0)

    early_two = jnp.concatenate([piece[panel:] for piece in early_two], 0)
    early_two = after(early_two, arrived[final], other[0])
    top_both = panels_of(whole, early_two, factor_of(own_cross), height)
    terms = wide_dot(top_both.T, trail[:, last:])
    placed = lax.dynamic_update_slice_in_dim(
        jnp.zeros((2 * panel, panel), F32),
        jnp.where(is_two, 0, after(adj_row_two, first[final])[:, last:]),
        row_start,
        0,
    )
    terms = terms - placed
    own_terms = terms
    step = 1
    while step < row_count:
        pairs = [
            (i * col_count + c, (i ^ step) * col_count + c)
            for i in range(row_count)
            for c in (col_count - 2, col_count - 1)
        ]
        if step > 1:
            terms = terms.astype(BF16)
        moved = lax.ppermute(terms, ("row", "col"), pairs)
        terms = terms.astype(F32) + moved.astype(F32)
        step *= 2
    terms = terms.astype(BF16)
    terms_other = pair_swap(terms, [top])

    whole_other = jnp.where(is_two, after(early_one, own_terms), early_two)
    for k, (start, stop) in enumerate(cuts):
        low = after(other[k][panel:], own_terms, *other[:k])
        other[k] = jnp.where(at_top, whole_other[start:stop], low)
    cross = jnp.where(at_top, side_cross, own[final][:panel])
    factor = factor_of(cross)
    column = lax.broadcasted_iota(jnp.int32, (1, width), 1)
    in_block = column >= last

    def put(matrix, block_one, block_two):
        block = jnp.where(here_one, block_one, block_two).astype(matrix.dtype)
        block = jnp.pad(block, ((0, 0), (last, 0)))
        return jnp.where(in_block & (here_one | here_two), block, matrix)

    def updated(both, start, previous):
        rows = adj_trail[start : start + both.shape[0]]
        left = (rows - wide_dot(both, full_both)).astype(BF16)
        left = put(left, both[:, panel:], both[:, :panel])
        return lax.dynamic_update_slice(previous, left, (start, 0))

    sums = 0
    grad_trail = blank((height, width))
    for (start, stop), mine, theirs in zip(cuts[:-1], own, other):
        both = panels_of(mine, theirs, factor, stop - start)
        sums = sums + wide_dot(both.T, trail[start:stop])
        grad_trail = updated(both, start, grad_trail)
    diag_term_two = jnp.where(is_two, terms, terms_other)[:panel]
    terms = jnp.concatenate([diag_term_two, jnp.where(is_two, terms_other, terms)], 0)
    terms = choose(
        [([top], terms)] + [([k], hop(terms, [(top, k)])) for k in range(levels - 1)]
    )
    whole_terms = terms.astype(F32)
    diag_term_two = whole_terms[:panel]
    crossing = whole_terms[panel : 2 * panel]
    diag_term_one = whole_terms[2 * panel :]

    start, stop = cuts[-1]
    theirs = after(other[-1], terms, sums)
    both = panels_of(own[-1], theirs, factor, stop - start)
    sums = (sums + wide_dot(both.T, trail[start:stop])).astype(BF16)

    parts = sums.reshape(2, row_count, band, width)
    step = 1
    while step < row_count:
        low = (row_here // step) % 2 == 0
        parts = parts.reshape(2, -1, 2, band, width)
        keep = jnp.where(low, parts[:, :, 0], parts[:, :, 1])
        give = jnp.where(low, parts[:, :, 1], parts[:, :, 0])
        give = give.astype(BF16)
        sent = give
        parts = keep + row_swap(give, step).astype(F32)
        step *= 2
    parts = parts.reshape(2, band, width)
    grad_trail = updated(after(both, sent), start, grad_trail)

    grad_diag_two = block_adjoint(
        diag_two, inverse_two, jnp.tril(adj_diag_two - after(diag_term_two, sums))
    )
    mirror_two = grad_diag_two + grad_diag_two.T
    adj_two = -crossing - exact_dot(mirror_two, cross.astype(F32))
    head = exact_dot(adj_two, inverse_one).astype(BF16)
    seed_one = jnp.tril(adj_diag_one - wide_dot(head.T, cross) - diag_term_one)
    grad_diag_one = block_adjoint(diag_one, inverse_one, seed_one)
    mirror_one = grad_diag_one + grad_diag_one.T

    head_wide = head.astype(F32)
    mix_two = jnp.concatenate([own_rows(mirror_two), own_rows(head_wide)], 1)
    mix_one = jnp.concatenate([own_rows(head_wide.T), own_rows(mirror_one)], 1)
    mix = jnp.concatenate([mix_two, mix_one], 0)
    mixed = wide_dot(
        jnp.concatenate(halves(mix), 1), jnp.concatenate([full_both, full_both], 0)
    )
    two_left = adj_row_two - mixed[:band] - parts[0]
    one_left = adj_row_one - mixed[band:] - parts[1]

    nothing = jnp.zeros((band, panel), F32)
    grad_row_one = put(one_left, nothing, nothing)
    grad_row_two = put(two_left, own_rows(head_wide), nothing)
    return (grad_trail, grad_row_one, grad_row_two, grad_diag_one, grad_diag_two)


def solution(mesh):
    split = P("row", "col")
    in_specs = (split, split, split, P(), P(), split, split, split, P(), P())
    out_specs = (split, split, split, P(), P())
    return jax.shard_map(
        per_device, mesh=mesh, in_specs=in_specs, out_specs=out_specs, check_vma=False
    )
```

```python
import functools

import jax
import jax.numpy as jnp
from jax import lax
from jax.experimental import pallas as pl
from jax.experimental.pallas import tpu as pltpu
from jax.sharding import PartitionSpec as P

EXACT = lax.Precision.HIGHEST
F32 = jnp.float32
BF16 = jnp.bfloat16
PIECES = 2


def exact_dot(a, b):
    return jnp.dot(a, b, precision=EXACT, preferred_element_type=F32)


def wide_dot(a, b):
    return jnp.dot(a, b, preferred_element_type=F32)


def halves(value):
    high = value.astype(BF16)
    return high, (value - high.astype(F32)).astype(BF16)


def halved_lower(matrix):
    order = matrix.shape[0]
    rows = lax.broadcasted_iota(jnp.int32, (order, order), 0)
    cols = lax.broadcasted_iota(jnp.int32, (order, order), 1)
    return jnp.where(rows > cols, matrix, jnp.where(rows == cols, 0.5 * matrix, 0))


def split_dot(left, right):
    (left_high, left_low), (right_high, right_low) = left, right
    return wide_dot(
        jnp.concatenate([left_high, left_high, left_low], 1),
        jnp.concatenate([right_high, right_low, right_high], 0),
    )


def inverse_lower(blocks):
    order = blocks[0].shape[-1]
    rows = lax.broadcasted_iota(jnp.int32, (order, order), 0)
    cols = lax.broadcasted_iota(jnp.int32, (order, order), 1)
    equal = rows == cols
    inverses = []
    for block in blocks:
        recip_col = 1.0 / jnp.sum(jnp.where(equal, block, 0), 1, keepdims=True)
        recip_row = 1.0 / jnp.sum(jnp.where(equal, block, 0), 0, keepdims=True)
        pair = ((rows ^ cols) == 1) & (rows > cols)
        corner = jnp.where(pair, block, 0)
        inverses.append(jnp.where(equal, recip_col, 0) - recip_col * corner * recip_row)
    size = 2
    while size < order:
        below = ((rows ^ cols) & -size == size) & (rows > cols)
        below = below & ((rows ^ cols) < 2 * size)
        known = [halves(inverse) for inverse in inverses]
        inner = [
            split_dot(halves(jnp.where(below, block, 0)), pair)
            for block, pair in zip(blocks, known)
        ]
        inverses = [
            inverse - split_dot(pair, halves(part))
            for inverse, pair, part in zip(inverses, known, inner)
        ]
        size *= 2
    return inverses


def prepare_kernel(
    cuts,
    side_ref,
    one_ref,
    two_ref,
    adj_ref,
    inv_one_ref,
    inv_two_ref,
    whole_ref,
    *rest,
):
    *piece_refs, rows_ref, sem = rest
    panel = one_ref.shape[0]
    block = pl.ds(adj_ref.shape[1] - panel, panel)
    fetch = pltpu.make_async_copy(adj_ref.at[:, block], rows_ref, sem)
    fetch.start()
    inverse_one, inverse_two = inverse_lower([one_ref[...], two_ref[...]])
    inv_one_ref[...] = inverse_one
    inv_two_ref[...] = inverse_two
    chosen = halves(jnp.where(side_ref[0] == 1, inverse_two, inverse_one))
    fetch.wait()
    for (start, stop), piece_ref in zip(cuts, piece_refs):
        product = split_dot(halves(rows_ref[start:stop, :]), chosen).astype(BF16)
        whole_ref[start:stop, :] = product
        piece_ref[:panel, :] = jnp.zeros((panel, panel), BF16)
        piece_ref[panel:, :] = product


def prepare(side, diag_one, diag_two, adj_trail, cuts):
    height = adj_trail.shape[0]
    panel = diag_one.shape[0]
    vmem = pl.BlockSpec(memory_space=pltpu.VMEM)
    hbm = pl.BlockSpec(memory_space=pltpu.HBM)
    sizes = [panel + stop - start for start, stop in cuts]
    return pl.pallas_call(
        functools.partial(prepare_kernel, cuts),
        in_specs=[pl.BlockSpec(memory_space=pltpu.SMEM), vmem, vmem, hbm],
        out_specs=[vmem] * (3 + len(cuts)),
        out_shape=[jax.ShapeDtypeStruct((panel, panel), F32)] * 2
        + [jax.ShapeDtypeStruct((size, panel), BF16) for size in [height] + sizes],
        scratch_shapes=[
            pltpu.VMEM((height, panel), F32),
            pltpu.SemaphoreType.DMA,
        ],
        compiler_params=pltpu.CompilerParams(vmem_limit_bytes=60 * 2**20),
        cost_estimate=pl.CostEstimate(
            flops=8 * height * panel * panel, bytes_accessed=8 * height * panel, transcendentals=0
        ),
        name="prepare",
    )(side, diag_one, diag_two, adj_trail)


def blank(shape):
    return pl.pallas_call(
        lambda out_ref: None,
        out_specs=pl.BlockSpec(memory_space=pltpu.HBM),
        out_shape=jax.ShapeDtypeStruct(shape, BF16),
        name="blank",
    )()


def after(value, *others):
    return lax.optimization_barrier((value, *others))[0]


def block_adjoint(block, inverse, seed_adj):
    inner = halved_lower(exact_dot(block.T, seed_adj))
    middle = exact_dot(inverse.T, inner)
    return halved_lower(exact_dot(middle, inverse))


def per_device(
    trail,
    row_one,
    row_two,
    diag_one,
    diag_two,
    adj_trail,
    adj_row_one,
    adj_row_two,
    adj_diag_one,
    adj_diag_two,
):
    panel = diag_one.shape[0]
    height, width = trail.shape
    band = row_one.shape[0]
    last = width - panel
    row_count = lax.axis_size("row")
    col_count = lax.axis_size("col")
    levels = col_count // 2
    top = levels - 1
    row_here = lax.axis_index("row")
    col_here = lax.axis_index("col")
    row_start = row_here * band
    level = col_here // 2
    is_two = col_here % 2 == 1
    here_one = col_here == col_count - 2
    here_two = col_here == col_count - 1
    tile = 2 * panel
    marks = [k * (height // tile) // PIECES * tile for k in range(PIECES + 1)]
    cuts = list(zip(marks, marks[1:]))
    final = len(cuts) - 1

    def own_rows(matrix):
        return lax.dynamic_slice_in_dim(matrix, row_start, band, 0)

    def row_swap(value, step):
        return lax.ppermute(value, "row", [(i, i ^ step) for i in range(row_count)])

    def pair_swap(value, which):
        pairs = [(2 * k + s, 2 * k + 1 - s) for k in which for s in range(2)]
        return lax.ppermute(value, "col", pairs)

    def gather_step(value, step):
        other = row_swap(value, step)
        low = (row_here // step) % 2 == 0
        return jnp.concatenate(
            [jnp.where(low, value, other), jnp.where(low, other, value)], 1
        )

    def gather_rest(value):
        step = 2
        while step < row_count:
            value = gather_step(value, step)
            step *= 2
        return value.reshape(panel, width)

    def choose(options):
        merged = []
        for members, array in options:
            for entry in merged:
                if entry[1] is array:
                    entry[0].extend(members)
                    break
            else:
                merged.append((list(members), array))
        chosen = merged[0][1]
        for members, array in merged[1:]:
            at = functools.reduce(jnp.logical_or, [level == k for k in members])
            chosen = jnp.where(at, array, chosen)
        return chosen

    def hop(value, hops):
        pairs = [(2 * a + s, 2 * b + s) for a, b in hops for s in range(2)]
        return lax.ppermute(value, "col", pairs)

    def spread(pieces, gates, lend):
        middle, span = levels // 2 - 1, levels // 4
        first, down, up = [], [], []
        for k in range(len(pieces) + 1):
            if k == 0:
                operand, hops = pieces[0], [(top, middle)]
            elif k < len(pieces):
                operand = jnp.where(level == top, pieces[k], first[-1])
                hops = [(top, middle), (middle, middle - span)]
            else:
                operand, hops = first[-1], [(middle, middle - span)]
            moved = hop(operand, hops)
            if k == len(pieces) - 1:
                block = lend(up[0])
                block_moved = hop(block, [(top, middle)])
                moved = after(moved, block_moved)
            if k > 0:
                down.append(moved)
            if k < len(pieces):
                moved = after(moved, *gates[k]) if k < len(gates) else moved
                if k == len(pieces) - 1:
                    moved = lax.dynamic_update_slice(moved, block_moved, (0, 0))
                first.append(moved)
                up.append(hop(moved, [(middle, middle + span)]))
        held = [
            {middle: here, middle - span: low, middle + span: high}
            for here, low, high in zip(first, down, up)
        ]
        span //= 2
        while span >= 1:
            for piece in held:
                fresh = list(piece)
                operand = choose([([k], piece[k]) for k in fresh])
                up = hop(operand, [(k, k + span) for k in fresh])
                low = hop(operand, [(k, k - span) for k in fresh if k >= span])
                for k in fresh:
                    piece[k + span] = up
                    if k >= span:
                        piece[k - span] = low
            span //= 2
        arrived = []
        for piece in held:
            options = [([k], after(piece[k], *arrived)) for k in sorted(piece)]
            arrived.append(choose(options))
        return block, first, arrived

    near_two = gather_step(row_two[None, None], 1)
    near_one = gather_step(row_one[None, None], 1)
    full_two = gather_rest(near_two)
    side = is_two.astype(jnp.int32)[None]
    inverse_one, inverse_two, whole, *packets = prepare(
        side, diag_one, diag_two, adj_trail, cuts
    )
    own_cross = full_two[:, last:]
    one_owner, two_owner = col_count - 2, col_count - 1

    def lend(gate):
        lent = lax.ppermute(after(own_cross, gate), "col", [(one_owner, two_owner)])
        return jnp.where(is_two, lent, own_cross)

    def factor_of(cross):
        return jnp.concatenate(halves(exact_dot(cross.astype(F32), inverse_one)), 0)

    def panels_of(own, other, factor, size):
        solved_two = jnp.where(is_two, own[-size:], other[-size:])
        base_one = jnp.where(is_two, other[-size:], own[-size:])
        tail = base_one.astype(F32) - wide_dot(
            jnp.concatenate([solved_two, solved_two], 1), factor
        )
        return jnp.concatenate([solved_two, tail.astype(BF16)], 1)

    early_two = [
        lax.ppermute(packet, "col", [(two_owner, one_owner)]) for packet in packets
    ]
    full_one = gather_rest(after(near_one, full_two))
    gates = [(early_two[0],), (full_one,)]
    side_cross, first, arrived = spread(packets, gates, lend)
    early_one = lax.ppermute(after(whole, first[0]), "col", [(one_owner, two_owner)])
    at_top = level == top
    own = [jnp.where(at_top, a, b) for a, b in zip(packets, arrived)]
    other = [pair_swap(value, range(levels - 1)) for value in arrived]
    full_both = jnp.concatenate([full_two, after(full_one, arrived[0])], 0)

    early_two = jnp.concatenate(
        [after(piece, arrived[final], other[0])[panel:] for piece in early_two], 0
    )
    top_both = panels_of(whole, early_two, factor_of(own_cross), height)
    terms = wide_dot(top_both.T, trail[:, last:])
    placed = lax.dynamic_update_slice_in_dim(
        jnp.zeros((2 * panel, panel), F32),
        jnp.where(is_two, 0, after(adj_row_two, first[final])[:, last:]),
        row_start,
        0,
    )
    terms = terms - placed
    own_terms = terms
    step = 1
    while step < row_count:
        pairs = [
            (i * col_count + c, (i ^ step) * col_count + c)
            for i in range(row_count)
            for c in (col_count - 2, col_count - 1)
        ]
        if step > 1:
            terms = terms.astype(BF16)
        moved = lax.ppermute(terms, ("row", "col"), pairs)
        terms = terms.astype(F32) + moved.astype(F32)
        step *= 2
    terms = terms.astype(BF16)
    terms_other = pair_swap(terms, [top])

    diag_term_two = jnp.where(is_two, terms, terms_other)[:panel]
    terms = jnp.concatenate([diag_term_two, jnp.where(is_two, terms_other, terms)], 0)

    whole_other = jnp.where(is_two, after(early_one, own_terms), early_two)
    for k, (start, stop) in enumerate(cuts):
        low = after(other[k][panel:], own_terms, *other[:k])
        other[k] = jnp.where(at_top, whole_other[start:stop], low)
    cross = jnp.where(at_top, side_cross, own[final][:panel])
    factor = factor_of(cross)
    column = lax.broadcasted_iota(jnp.int32, (1, width), 1)
    in_block = column >= last

    def put(matrix, block_one, block_two):
        block = jnp.where(here_one, block_one, block_two).astype(matrix.dtype)
        block = jnp.pad(block, ((0, 0), (last, 0)))
        return jnp.where(in_block & (here_one | here_two), block, matrix)

    def updated(both, start, previous):
        rows = adj_trail[start : start + both.shape[0]]
        left = (rows - wide_dot(both, full_both)).astype(BF16)
        left = put(left, both[:, panel:], both[:, :panel])
        return lax.dynamic_update_slice(previous, left, (start, 0))

    sums = 0
    grad_trail = blank((height, width))
    for (start, stop), mine, theirs in zip(cuts[:-1], own, other):
        both = panels_of(mine, theirs, factor, stop - start)
        sums = sums + wide_dot(both.T, trail[start:stop])
        grad_trail = updated(after(both, terms), start, grad_trail)
    terms = choose(
        [([top], terms)] + [([k], hop(terms, [(top, k)])) for k in range(levels - 1)]
    )
    whole_terms = terms.astype(F32)
    diag_term_two = whole_terms[:panel]
    crossing = whole_terms[panel : 2 * panel]
    diag_term_one = whole_terms[2 * panel :]

    start, stop = cuts[-1]
    theirs = after(other[-1], terms, sums)
    both = panels_of(own[-1], theirs, factor, stop - start)
    sums = (sums + wide_dot(both.T, trail[start:stop])).astype(BF16)

    parts = sums.reshape(2, row_count, band, width)
    step = 1
    while step < row_count:
        low = (row_here // step) % 2 == 0
        parts = parts.reshape(2, -1, 2, band, width)
        keep = jnp.where(low, parts[:, :, 0], parts[:, :, 1])
        give = jnp.where(low, parts[:, :, 1], parts[:, :, 0])
        give = give.astype(BF16)
        sent = give
        parts = keep + row_swap(give, step).astype(F32)
        step *= 2
    parts = parts.reshape(2, band, width)
    grad_trail = updated(after(both, sent), start, grad_trail)

    grad_diag_two = block_adjoint(
        diag_two, inverse_two, jnp.tril(adj_diag_two - after(diag_term_two, sums))
    )
    mirror_two = grad_diag_two + grad_diag_two.T
    adj_two = -crossing - exact_dot(mirror_two, cross.astype(F32))
    head = exact_dot(adj_two, inverse_one).astype(BF16)
    seed_one = jnp.tril(adj_diag_one - wide_dot(head.T, cross) - diag_term_one)
    grad_diag_one = block_adjoint(diag_one, inverse_one, seed_one)
    mirror_one = grad_diag_one + grad_diag_one.T

    head_wide = head.astype(F32)
    mix_two = jnp.concatenate([own_rows(mirror_two), own_rows(head_wide)], 1)
    mix_one = jnp.concatenate([own_rows(head_wide.T), own_rows(mirror_one)], 1)
    mix = jnp.concatenate([mix_two, mix_one], 0)
    mixed = wide_dot(
        jnp.concatenate(halves(mix), 1), jnp.concatenate([full_both, full_both], 0)
    )
    two_left = adj_row_two - mixed[:band] - parts[0]
    one_left = adj_row_one - mixed[band:] - parts[1]

    nothing = jnp.zeros((band, panel), F32)
    grad_row_one = put(one_left, nothing, nothing)
    grad_row_two = put(two_left, own_rows(head_wide), nothing)
    return (grad_trail, grad_row_one, grad_row_two, grad_diag_one, grad_diag_two)


def solution(mesh):
    split = P("row", "col")
    in_specs = (split, split, split, P(), P(), split, split, split, P(), P())
    out_specs = (split, split, split, P(), P())
    return jax.shard_map(
        per_device, mesh=mesh, in_specs=in_specs, out_specs=out_specs, check_vma=False
    )
```

```python
import functools

import jax
import jax.numpy as jnp
from jax import lax
from jax.experimental import pallas as pl
from jax.experimental.pallas import tpu as pltpu
from jax.sharding import PartitionSpec as P

EXACT = lax.Precision.HIGHEST
F32 = jnp.float32
BF16 = jnp.bfloat16
PIECES = 2


def exact_dot(a, b):
    return jnp.dot(a, b, precision=EXACT, preferred_element_type=F32)


def wide_dot(a, b):
    return jnp.dot(a, b, preferred_element_type=F32)


def halves(value):
    high = value.astype(BF16)
    return high, (value - high.astype(F32)).astype(BF16)


def halved_lower(matrix):
    order = matrix.shape[0]
    rows = lax.broadcasted_iota(jnp.int32, (order, order), 0)
    cols = lax.broadcasted_iota(jnp.int32, (order, order), 1)
    return jnp.where(rows > cols, matrix, jnp.where(rows == cols, 0.5 * matrix, 0))


def split_dot(left, right):
    (left_high, left_low), (right_high, right_low) = left, right
    return wide_dot(
        jnp.concatenate([left_high, left_high, left_low], 1),
        jnp.concatenate([right_high, right_low, right_high], 0),
    )


def inverse_lower(blocks):
    order = blocks[0].shape[-1]
    rows = lax.broadcasted_iota(jnp.int32, (order, order), 0)
    cols = lax.broadcasted_iota(jnp.int32, (order, order), 1)
    equal = rows == cols
    inverses = []
    for block in blocks:
        recip_col = 1.0 / jnp.sum(jnp.where(equal, block, 0), 1, keepdims=True)
        recip_row = 1.0 / jnp.sum(jnp.where(equal, block, 0), 0, keepdims=True)
        pair = ((rows ^ cols) == 1) & (rows > cols)
        corner = jnp.where(pair, block, 0)
        inverses.append(jnp.where(equal, recip_col, 0) - recip_col * corner * recip_row)
    size = 2
    while size < order:
        below = ((rows ^ cols) & -size == size) & (rows > cols)
        below = below & ((rows ^ cols) < 2 * size)
        known = [halves(inverse) for inverse in inverses]
        inner = [
            split_dot(halves(jnp.where(below, block, 0)), pair)
            for block, pair in zip(blocks, known)
        ]
        inverses = [
            inverse - split_dot(pair, halves(part))
            for inverse, pair, part in zip(inverses, known, inner)
        ]
        size *= 2
    return inverses


def prepare_kernel(
    cuts,
    side_ref,
    one_ref,
    two_ref,
    adj_ref,
    inv_one_ref,
    inv_two_ref,
    whole_ref,
    *rest,
):
    *piece_refs, rows_ref, sem = rest
    panel = one_ref.shape[0]
    block = pl.ds(adj_ref.shape[1] - panel, panel)
    fetch = pltpu.make_async_copy(adj_ref.at[:, block], rows_ref, sem)
    fetch.start()
    inverse_one, inverse_two = inverse_lower([one_ref[...], two_ref[...]])
    inv_one_ref[...] = inverse_one
    inv_two_ref[...] = inverse_two
    chosen = halves(jnp.where(side_ref[0] == 1, inverse_two, inverse_one))
    fetch.wait()
    for (start, stop), piece_ref in zip(cuts, piece_refs):
        product = split_dot(halves(rows_ref[start:stop, :]), chosen).astype(BF16)
        whole_ref[start:stop, :] = product
        piece_ref[:panel, :] = jnp.zeros((panel, panel), BF16)
        piece_ref[panel:, :] = product


def prepare(side, diag_one, diag_two, adj_trail, cuts):
    height = adj_trail.shape[0]
    panel = diag_one.shape[0]
    vmem = pl.BlockSpec(memory_space=pltpu.VMEM)
    hbm = pl.BlockSpec(memory_space=pltpu.HBM)
    sizes = [panel + stop - start for start, stop in cuts]
    return pl.pallas_call(
        functools.partial(prepare_kernel, cuts),
        in_specs=[pl.BlockSpec(memory_space=pltpu.SMEM), vmem, vmem, hbm],
        out_specs=[vmem] * (3 + len(cuts)),
        out_shape=[jax.ShapeDtypeStruct((panel, panel), F32)] * 2
        + [jax.ShapeDtypeStruct((size, panel), BF16) for size in [height] + sizes],
        scratch_shapes=[
            pltpu.VMEM((height, panel), F32),
            pltpu.SemaphoreType.DMA,
        ],
        compiler_params=pltpu.CompilerParams(vmem_limit_bytes=60 * 2**20),
        cost_estimate=pl.CostEstimate(
            flops=8 * height * panel * panel, bytes_accessed=8 * height * panel, transcendentals=0
        ),
        name="prepare",
    )(side, diag_one, diag_two, adj_trail)


def blank(shape):
    return pl.pallas_call(
        lambda out_ref: None,
        out_specs=pl.BlockSpec(memory_space=pltpu.HBM),
        out_shape=jax.ShapeDtypeStruct(shape, BF16),
        name="blank",
    )()


def after(value, *others):
    return lax.optimization_barrier((value, *others))[0]


def block_adjoint(block, inverse, seed_adj):
    inner = halved_lower(exact_dot(block.T, seed_adj))
    middle = exact_dot(inverse.T, inner)
    return halved_lower(exact_dot(middle, inverse))


def per_device(
    trail,
    row_one,
    row_two,
    diag_one,
    diag_two,
    adj_trail,
    adj_row_one,
    adj_row_two,
    adj_diag_one,
    adj_diag_two,
):
    panel = diag_one.shape[0]
    height, width = trail.shape
    band = row_one.shape[0]
    last = width - panel
    row_count = lax.axis_size("row")
    col_count = lax.axis_size("col")
    levels = col_count // 2
    top = levels - 1
    row_here = lax.axis_index("row")
    col_here = lax.axis_index("col")
    row_start = row_here * band
    level = col_here // 2
    is_two = col_here % 2 == 1
    here_one = col_here == col_count - 2
    here_two = col_here == col_count - 1
    tile = 2 * panel
    marks = [k * (height // tile) // PIECES * tile for k in range(PIECES + 1)]
    cuts = list(zip(marks, marks[1:]))
    final = len(cuts) - 1

    def own_rows(matrix):
        return lax.dynamic_slice_in_dim(matrix, row_start, band, 0)

    def row_swap(value, step):
        return lax.ppermute(value, "row", [(i, i ^ step) for i in range(row_count)])

    def pair_swap(value, which):
        pairs = [(2 * k + s, 2 * k + 1 - s) for k in which for s in range(2)]
        return lax.ppermute(value, "col", pairs)

    def gather_step(value, step):
        other = row_swap(value, step)
        low = (row_here // step) % 2 == 0
        return jnp.concatenate(
            [jnp.where(low, value, other), jnp.where(low, other, value)], 1
        )

    def gather_rest(value):
        step = 2
        while step < row_count:
            value = gather_step(value, step)
            step *= 2
        return value.reshape(panel, value.shape[-1])

    def choose(options):
        merged = []
        for members, array in options:
            for entry in merged:
                if entry[1] is array:
                    entry[0].extend(members)
                    break
            else:
                merged.append((list(members), array))
        chosen = merged[0][1]
        for members, array in merged[1:]:
            at = functools.reduce(jnp.logical_or, [level == k for k in members])
            chosen = jnp.where(at, array, chosen)
        return chosen

    def hop(value, hops):
        pairs = [(2 * a + s, 2 * b + s) for a, b in hops for s in range(2)]
        return lax.ppermute(value, "col", pairs)

    def spread(pieces, gates, extra):
        middle, span = levels // 2 - 1, levels // 4
        first, down = [], []
        extra_moved = hop(extra, [(top, middle)])
        for k in range(len(pieces) + 1):
            if k == 0:
                operand, hops = pieces[0], [(top, middle)]
            elif k < len(pieces):
                operand = jnp.where(level == top, pieces[k], first[-1])
                hops = [(top, middle), (middle, middle - span)]
            else:
                operand, hops = first[-1], [(middle, middle - span)]
            moved = hop(operand, hops)
            if k > 0:
                down.append(moved)
            if k < len(pieces):
                moved = after(moved, gates[k]) if k < len(gates) else moved
                if k == len(pieces) - 1:
                    moved = lax.dynamic_update_slice(moved, extra_moved, (0, 0))
                first.append(moved)
        held = [
            {middle: here, middle - span: low, middle + span: hop(here, [(middle, middle + span)])}
            for here, low in zip(first, down)
        ]
        span //= 2
        while span >= 1:
            for piece in held:
                fresh = list(piece)
                operand = choose([([k], piece[k]) for k in fresh])
                up = hop(operand, [(k, k + span) for k in fresh])
                low = hop(operand, [(k, k - span) for k in fresh if k >= span])
                for k in fresh:
                    piece[k + span] = up
                    if k >= span:
                        piece[k - span] = low
            span //= 2
        arrived = []
        for piece in held:
            options = [([k], after(piece[k], *arrived)) for k in sorted(piece)]
            arrived.append(choose(options))
        return first, arrived

    one_owner, two_owner = col_count - 2, col_count - 1
    own_rows_cross = row_two[:, last:]
    lent_rows = lax.ppermute(own_rows_cross, "col", [(one_owner, two_owner)])
    rows_cross = jnp.where(is_two, lent_rows, own_rows_cross)
    near_two = gather_step(jnp.concatenate([row_two, rows_cross], 1)[None, None], 1)
    near_one = gather_step(row_one[None, None], 1)
    extended = gather_rest(near_two)
    full_two, side_cross = extended[:, :width], extended[:, width:]
    side = is_two.astype(jnp.int32)[None]
    inverse_one, inverse_two, whole, *packets = prepare(
        side, after(diag_one, rows_cross), diag_two, adj_trail, cuts
    )
    own_cross = side_cross

    def factor_of(cross):
        return jnp.concatenate(halves(exact_dot(cross.astype(F32), inverse_one)), 0)

    def panels_of(own, other, factor, size):
        solved_two = jnp.where(is_two, own[-size:], other[-size:])
        base_one = jnp.where(is_two, other[-size:], own[-size:])
        tail = base_one.astype(F32) - wide_dot(
            jnp.concatenate([solved_two, solved_two], 1), factor
        )
        return jnp.concatenate([solved_two, tail.astype(BF16)], 1)

    early_two = [
        lax.ppermute(packet, "col", [(two_owner, one_owner)]) for packet in packets
    ]
    full_one = gather_rest(after(near_one, side_cross))
    first, arrived = spread(packets, [early_two[0], full_one], side_cross)
    early_one = lax.ppermute(after(whole, first[0]), "col", [(one_owner, two_owner)])
    at_top = level == top
    own = [jnp.where(at_top, a, b) for a, b in zip(packets, arrived)]
    other = [pair_swap(value, range(levels - 1)) for value in arrived]
    full_both = jnp.concatenate([full_two, after(full_one, arrived[0])], 0)

    early_two = jnp.concatenate([piece[panel:] for piece in early_two], 0)
    early_two = after(early_two, arrived[final], other[0])
    top_both = panels_of(whole, early_two, factor_of(own_cross), height)
    terms = wide_dot(top_both.T, trail[:, last:])
    placed = lax.dynamic_update_slice_in_dim(
        jnp.zeros((2 * panel, panel), F32),
        jnp.where(is_two, 0, after(adj_row_two, first[final])[:, last:]),
        row_start,
        0,
    )
    terms = terms - placed
    own_terms = terms
    step = 1
    while step < row_count:
        pairs = [
            (i * col_count + c, (i ^ step) * col_count + c)
            for i in range(row_count)
            for c in (col_count - 2, col_count - 1)
        ]
        if step > 1:
            terms = terms.astype(BF16)
        moved = lax.ppermute(terms, ("row", "col"), pairs)
        terms = terms.astype(F32) + moved.astype(F32)
        step *= 2
    terms = terms.astype(BF16)
    terms_other = pair_swap(terms, [top])

    whole_other = jnp.where(is_two, after(early_one, own_terms), early_two)
    for k, (start, stop) in enumerate(cuts):
        low = after(other[k][panel:], own_terms, *other[:k])
        other[k] = jnp.where(at_top, whole_other[start:stop], low)
    cross = jnp.where(at_top, side_cross, own[final][:panel])
    factor = factor_of(cross)
    column = lax.broadcasted_iota(jnp.int32, (1, width), 1)
    in_block = column >= last

    def put(matrix, block_one, block_two):
        block = jnp.where(here_one, block_one, block_two).astype(matrix.dtype)
        block = jnp.pad(block, ((0, 0), (last, 0)))
        return jnp.where(in_block & (here_one | here_two), block, matrix)

    def updated(both, start, previous):
        rows = adj_trail[start : start + both.shape[0]]
        left = (rows - wide_dot(both, full_both)).astype(BF16)
        left = put(left, both[:, panel:], both[:, :panel])
        return lax.dynamic_update_slice(previous, left, (start, 0))

    sums = 0
    grad_trail = blank((height, width))
    for (start, stop), mine, theirs in zip(cuts[:-1], own, other):
        both = panels_of(mine, theirs, factor, stop - start)
        sums = sums + wide_dot(both.T, trail[start:stop])
        grad_trail = updated(after(both, terms), start, grad_trail)
    diag_term_two = jnp.where(is_two, terms, terms_other)[:panel]
    terms = jnp.concatenate([diag_term_two, jnp.where(is_two, terms_other, terms)], 0)
    terms = choose(
        [([top], terms)] + [([k], hop(terms, [(top, k)])) for k in range(levels - 1)]
    )
    whole_terms = terms.astype(F32)
    diag_term_two = whole_terms[:panel]
    crossing = whole_terms[panel : 2 * panel]
    diag_term_one = whole_terms[2 * panel :]

    start, stop = cuts[-1]
    theirs = after(other[-1], terms, sums)
    both = panels_of(own[-1], theirs, factor, stop - start)
    sums = (sums + wide_dot(both.T, trail[start:stop])).astype(BF16)

    parts = sums.reshape(2, row_count, band, width)
    step = 1
    while step < row_count:
        low = (row_here // step) % 2 == 0
        parts = parts.reshape(2, -1, 2, band, width)
        keep = jnp.where(low, parts[:, :, 0], parts[:, :, 1])
        give = jnp.where(low, parts[:, :, 1], parts[:, :, 0])
        give = give.astype(BF16)
        sent = give
        parts = keep + row_swap(give, step).astype(F32)
        step *= 2
    parts = parts.reshape(2, band, width)
    grad_trail = updated(after(both, sent), start, grad_trail)

    grad_diag_two = block_adjoint(
        diag_two, inverse_two, jnp.tril(adj_diag_two - after(diag_term_two, sums))
    )
    mirror_two = grad_diag_two + grad_diag_two.T
    adj_two = -crossing - exact_dot(mirror_two, cross.astype(F32))
    head = exact_dot(adj_two, inverse_one).astype(BF16)
    seed_one = jnp.tril(adj_diag_one - wide_dot(head.T, cross) - diag_term_one)
    grad_diag_one = block_adjoint(diag_one, inverse_one, seed_one)
    mirror_one = grad_diag_one + grad_diag_one.T

    head_wide = head.astype(F32)
    mix_two = jnp.concatenate([own_rows(mirror_two), own_rows(head_wide)], 1)
    mix_one = jnp.concatenate([own_rows(head_wide.T), own_rows(mirror_one)], 1)
    mix = jnp.concatenate([mix_two, mix_one], 0)
    mixed = wide_dot(
        jnp.concatenate(halves(mix), 1), jnp.concatenate([full_both, full_both], 0)
    )
    two_left = adj_row_two - mixed[:band] - parts[0]
    one_left = adj_row_one - mixed[band:] - parts[1]

    nothing = jnp.zeros((band, panel), F32)
    grad_row_one = put(one_left, nothing, nothing)
    grad_row_two = put(two_left, own_rows(head_wide), nothing)
    return (grad_trail, grad_row_one, grad_row_two, grad_diag_one, grad_diag_two)


def solution(mesh):
    split = P("row", "col")
    in_specs = (split, split, split, P(), P(), split, split, split, P(), P())
    out_specs = (split, split, split, P(), P())
    return jax.shard_map(
        per_device, mesh=mesh, in_specs=in_specs, out_specs=out_specs, check_vma=False
    )
```

```python
import functools

import jax
import jax.numpy as jnp
from jax import lax
from jax.experimental import pallas as pl
from jax.experimental.pallas import tpu as pltpu
from jax.sharding import PartitionSpec as P

EXACT = lax.Precision.HIGHEST
F32 = jnp.float32
BF16 = jnp.bfloat16
PIECES = 2


def exact_dot(a, b):
    return jnp.dot(a, b, precision=EXACT, preferred_element_type=F32)


def wide_dot(a, b):
    return jnp.dot(a, b, preferred_element_type=F32)


def halves(value):
    high = value.astype(BF16)
    return high, (value - high.astype(F32)).astype(BF16)


def halved_lower(matrix):
    order = matrix.shape[0]
    rows = lax.broadcasted_iota(jnp.int32, (order, order), 0)
    cols = lax.broadcasted_iota(jnp.int32, (order, order), 1)
    return jnp.where(rows > cols, matrix, jnp.where(rows == cols, 0.5 * matrix, 0))


def split_dot(left, right):
    (left_high, left_low), (right_high, right_low) = left, right
    return wide_dot(
        jnp.concatenate([left_high, left_high, left_low], 1),
        jnp.concatenate([right_high, right_low, right_high], 0),
    )


def inverse_lower(blocks):
    order = blocks[0].shape[-1]
    rows = lax.broadcasted_iota(jnp.int32, (order, order), 0)
    cols = lax.broadcasted_iota(jnp.int32, (order, order), 1)
    equal = rows == cols
    inverses = []
    for block in blocks:
        recip_col = 1.0 / jnp.sum(jnp.where(equal, block, 0), 1, keepdims=True)
        recip_row = 1.0 / jnp.sum(jnp.where(equal, block, 0), 0, keepdims=True)
        pair = ((rows ^ cols) == 1) & (rows > cols)
        corner = jnp.where(pair, block, 0)
        inverses.append(jnp.where(equal, recip_col, 0) - recip_col * corner * recip_row)
    size = 2
    while size < order:
        below = ((rows ^ cols) & -size == size) & (rows > cols)
        below = below & ((rows ^ cols) < 2 * size)
        known = [halves(inverse) for inverse in inverses]
        inner = [
            split_dot(halves(jnp.where(below, block, 0)), pair)
            for block, pair in zip(blocks, known)
        ]
        inverses = [
            inverse - split_dot(pair, halves(part))
            for inverse, pair, part in zip(inverses, known, inner)
        ]
        size *= 2
    return inverses


def prepare_kernel(
    cuts,
    side_ref,
    one_ref,
    two_ref,
    adj_ref,
    inv_one_ref,
    inv_two_ref,
    whole_ref,
    *rest,
):
    *piece_refs, rows_ref, sem = rest
    panel = one_ref.shape[0]
    block = pl.ds(adj_ref.shape[1] - panel, panel)
    fetch = pltpu.make_async_copy(adj_ref.at[:, block], rows_ref, sem)
    fetch.start()
    inverse_one, inverse_two = inverse_lower([one_ref[...], two_ref[...]])
    inv_one_ref[...] = inverse_one
    inv_two_ref[...] = inverse_two
    chosen = halves(jnp.where(side_ref[0] == 1, inverse_two, inverse_one))
    fetch.wait()
    for (start, stop), piece_ref in zip(cuts, piece_refs):
        product = split_dot(halves(rows_ref[start:stop, :]), chosen).astype(BF16)
        whole_ref[start:stop, :] = product
        piece_ref[:panel, :] = jnp.zeros((panel, panel), BF16)
        piece_ref[panel:, :] = product


def prepare(side, diag_one, diag_two, adj_trail, cuts):
    height = adj_trail.shape[0]
    panel = diag_one.shape[0]
    vmem = pl.BlockSpec(memory_space=pltpu.VMEM)
    hbm = pl.BlockSpec(memory_space=pltpu.HBM)
    sizes = [panel + stop - start for start, stop in cuts]
    return pl.pallas_call(
        functools.partial(prepare_kernel, cuts),
        in_specs=[pl.BlockSpec(memory_space=pltpu.SMEM), vmem, vmem, hbm],
        out_specs=[vmem] * (3 + len(cuts)),
        out_shape=[jax.ShapeDtypeStruct((panel, panel), F32)] * 2
        + [jax.ShapeDtypeStruct((size, panel), BF16) for size in [height] + sizes],
        scratch_shapes=[
            pltpu.VMEM((height, panel), F32),
            pltpu.SemaphoreType.DMA,
        ],
        compiler_params=pltpu.CompilerParams(vmem_limit_bytes=60 * 2**20),
        cost_estimate=pl.CostEstimate(
            flops=8 * height * panel * panel, bytes_accessed=8 * height * panel, transcendentals=0
        ),
        name="prepare",
    )(side, diag_one, diag_two, adj_trail)


def blank(shape):
    return pl.pallas_call(
        lambda out_ref: None,
        out_specs=pl.BlockSpec(memory_space=pltpu.HBM),
        out_shape=jax.ShapeDtypeStruct(shape, BF16),
        name="blank",
    )()


def after(value, *others):
    return lax.optimization_barrier((value, *others))[0]


def block_adjoint(block, inverse, seed_adj):
    inner = halved_lower(exact_dot(block.T, seed_adj))
    middle = exact_dot(inverse.T, inner)
    return halved_lower(exact_dot(middle, inverse))


def per_device(
    trail,
    row_one,
    row_two,
    diag_one,
    diag_two,
    adj_trail,
    adj_row_one,
    adj_row_two,
    adj_diag_one,
    adj_diag_two,
):
    panel = diag_one.shape[0]
    height, width = trail.shape
    band = row_one.shape[0]
    last = width - panel
    row_count = lax.axis_size("row")
    col_count = lax.axis_size("col")
    levels = col_count // 2
    top = levels - 1
    row_here = lax.axis_index("row")
    col_here = lax.axis_index("col")
    row_start = row_here * band
    level = col_here // 2
    is_two = col_here % 2 == 1
    here_one = col_here == col_count - 2
    here_two = col_here == col_count - 1
    tile = 2 * panel
    marks = [k * (height // tile) // PIECES * tile for k in range(PIECES + 1)]
    cuts = list(zip(marks, marks[1:]))
    final = len(cuts) - 1

    def own_rows(matrix):
        return lax.dynamic_slice_in_dim(matrix, row_start, band, 0)

    def row_swap(value, step):
        return lax.ppermute(value, "row", [(i, i ^ step) for i in range(row_count)])

    def pair_swap(value, which):
        pairs = [(2 * k + s, 2 * k + 1 - s) for k in which for s in range(2)]
        return lax.ppermute(value, "col", pairs)

    def gather_step(value, step):
        other = row_swap(value, step)
        low = (row_here // step) % 2 == 0
        return jnp.concatenate(
            [jnp.where(low, value, other), jnp.where(low, other, value)], 1
        )

    def gather_rest(value):
        step = 2
        while step < row_count:
            value = gather_step(value, step)
            step *= 2
        return value.reshape(panel, width)

    def choose(options):
        merged = []
        for members, array in options:
            for entry in merged:
                if entry[1] is array:
                    entry[0].extend(members)
                    break
            else:
                merged.append((list(members), array))
        chosen = merged[0][1]
        for members, array in merged[1:]:
            at = functools.reduce(jnp.logical_or, [level == k for k in members])
            chosen = jnp.where(at, array, chosen)
        return chosen

    def hop(value, hops):
        pairs = [(2 * a + s, 2 * b + s) for a, b in hops for s in range(2)]
        return lax.ppermute(value, "col", pairs)

    def spread(pieces, gates, extra):
        middle, span = levels // 2 - 1, levels // 4
        first, down = [], []
        extra_moved = hop(extra, [(top, middle)])
        for k in range(len(pieces) + 1):
            if k == 0:
                operand, hops = pieces[0], [(top, middle)]
            elif k < len(pieces):
                operand = jnp.where(level == top, pieces[k], first[-1])
                hops = [(top, middle), (middle, middle - span)]
            else:
                operand, hops = first[-1], [(middle, middle - span)]
            moved = hop(operand, hops)
            if k > 0:
                down.append(moved)
            if k < len(pieces):
                moved = after(moved, gates[k]) if k < len(gates) else moved
                if k == len(pieces) - 1:
                    moved = lax.dynamic_update_slice(moved, extra_moved, (0, 0))
                first.append(moved)
        held = [
            {middle: here, middle - span: low, middle + span: hop(here, [(middle, middle + span)])}
            for here, low in zip(first, down)
        ]
        span //= 2
        while span >= 1:
            for piece in held:
                fresh = list(piece)
                operand = choose([([k], piece[k]) for k in fresh])
                up = hop(operand, [(k, k + span) for k in fresh])
                low = hop(operand, [(k, k - span) for k in fresh if k >= span])
                for k in fresh:
                    piece[k + span] = up
                    if k >= span:
                        piece[k - span] = low
            span //= 2
        arrived = []
        for piece in held:
            options = [([k], after(piece[k], *arrived)) for k in sorted(piece)]
            arrived.append(choose(options))
        return first, arrived

    near_two = gather_step(row_two[None, None], 1)
    near_one = gather_step(row_one[None, None], 1)
    full_two = gather_rest(near_two)
    side = is_two.astype(jnp.int32)[None]
    inverse_one, inverse_two, whole, *packets = prepare(
        side, diag_one, diag_two, adj_trail, cuts
    )
    own_cross = full_two[:, last:]
    one_owner, two_owner = col_count - 2, col_count - 1
    lent_cross = lax.ppermute(own_cross, "col", [(one_owner, two_owner)])
    side_cross = jnp.where(is_two, lent_cross, own_cross)

    def factor_of(cross):
        return jnp.concatenate(halves(exact_dot(cross.astype(F32), inverse_one)), 0)

    def panels_of(own, other, factor, size):
        solved_two = jnp.where(is_two, own[-size:], other[-size:])
        base_one = jnp.where(is_two, other[-size:], own[-size:])
        tail = base_one.astype(F32) - wide_dot(
            jnp.concatenate([solved_two, solved_two], 1), factor
        )
        return jnp.concatenate([solved_two, tail.astype(BF16)], 1)

    early_two = [
        lax.ppermute(
            packet if k == 0 else after(packet, side_cross), "col", [(two_owner, one_owner)]
        )
        for k, packet in enumerate(packets)
    ]
    full_one = gather_rest(after(near_one, full_two))
    first, arrived = spread(packets, [early_two[0], full_one], side_cross)
    early_one = lax.ppermute(after(whole, first[0]), "col", [(one_owner, two_owner)])
    at_top = level == top
    own = [jnp.where(at_top, a, b) for a, b in zip(packets, arrived)]
    other = [pair_swap(value, range(levels - 1)) for value in arrived]
    full_both = jnp.concatenate([full_two, after(full_one, arrived[0])], 0)

    early_two = jnp.concatenate([piece[panel:] for piece in early_two], 0)
    early_two = after(early_two, arrived[final], other[0])
    top_both = panels_of(whole, early_two, factor_of(own_cross), height)
    terms = wide_dot(top_both.T, trail[:, last:])
    placed = lax.dynamic_update_slice_in_dim(
        jnp.zeros((2 * panel, panel), F32),
        jnp.where(is_two, 0, after(adj_row_two, first[final])[:, last:]),
        row_start,
        0,
    )
    terms = terms - placed
    own_terms = terms
    step = 1
    while step < row_count:
        pairs = [
            (i * col_count + c, (i ^ step) * col_count + c)
            for i in range(row_count)
            for c in (col_count - 2, col_count - 1)
        ]
        if step > 1:
            terms = terms.astype(BF16)
        moved = lax.ppermute(terms, ("row", "col"), pairs)
        terms = terms.astype(F32) + moved.astype(F32)
        step *= 2
    terms = terms.astype(BF16)
    terms_other = pair_swap(terms, [top])

    whole_other = jnp.where(is_two, after(early_one, own_terms), early_two)
    for k, (start, stop) in enumerate(cuts):
        low = after(other[k][panel:], own_terms, *other[:k])
        other[k] = jnp.where(at_top, whole_other[start:stop], low)
    cross = jnp.where(at_top, side_cross, own[final][:panel])
    factor = factor_of(cross)
    column = lax.broadcasted_iota(jnp.int32, (1, width), 1)
    in_block = column >= last

    def put(matrix, block_one, block_two):
        block = jnp.where(here_one, block_one, block_two).astype(matrix.dtype)
        block = jnp.pad(block, ((0, 0), (last, 0)))
        return jnp.where(in_block & (here_one | here_two), block, matrix)

    def updated(both, start, previous):
        rows = adj_trail[start : start + both.shape[0]]
        left = (rows - wide_dot(both, full_both)).astype(BF16)
        left = put(left, both[:, panel:], both[:, :panel])
        return lax.dynamic_update_slice(previous, left, (start, 0))

    sums = 0
    grad_trail = blank((height, width))
    for (start, stop), mine, theirs in zip(cuts[:-1], own, other):
        both = panels_of(mine, theirs, factor, stop - start)
        sums = sums + wide_dot(both.T, trail[start:stop])
        grad_trail = updated(both, start, grad_trail)
    diag_term_two = jnp.where(is_two, terms, terms_other)[:panel]
    terms = jnp.concatenate([diag_term_two, jnp.where(is_two, terms_other, terms)], 0)
    terms = choose(
        [([top], terms)] + [([k], hop(terms, [(top, k)])) for k in range(levels - 1)]
    )
    whole_terms = terms.astype(F32)
    diag_term_two = whole_terms[:panel]
    crossing = whole_terms[panel : 2 * panel]
    diag_term_one = whole_terms[2 * panel :]

    start, stop = cuts[-1]
    theirs = after(other[-1], terms, sums)
    both = panels_of(own[-1], theirs, factor, stop - start)
    sums = (sums + wide_dot(both.T, trail[start:stop])).astype(BF16)

    parts = sums.reshape(2, row_count, band, width)
    step = 1
    while step < row_count:
        low = (row_here // step) % 2 == 0
        parts = parts.reshape(2, -1, 2, band, width)
        keep = jnp.where(low, parts[:, :, 0], parts[:, :, 1])
        give = jnp.where(low, parts[:, :, 1], parts[:, :, 0])
        give = give.astype(BF16)
        sent = give
        parts = keep + row_swap(give, step).astype(F32)
        step *= 2
    parts = parts.reshape(2, band, width)
    grad_trail = updated(after(both, sent), start, grad_trail)

    grad_diag_two = block_adjoint(
        diag_two, inverse_two, jnp.tril(adj_diag_two - after(diag_term_two, sums))
    )
    mirror_two = grad_diag_two + grad_diag_two.T
    adj_two = -crossing - exact_dot(mirror_two, cross.astype(F32))
    head = exact_dot(adj_two, inverse_one).astype(BF16)
    seed_one = jnp.tril(adj_diag_one - wide_dot(head.T, cross) - diag_term_one)
    grad_diag_one = block_adjoint(diag_one, inverse_one, seed_one)
    mirror_one = grad_diag_one + grad_diag_one.T

    head_wide = head.astype(F32)
    mix_two = jnp.concatenate([own_rows(mirror_two), own_rows(head_wide)], 1)
    mix_one = jnp.concatenate([own_rows(head_wide.T), own_rows(mirror_one)], 1)
    mix = jnp.concatenate([mix_two, mix_one], 0)
    mixed = wide_dot(
        jnp.concatenate(halves(mix), 1), jnp.concatenate([full_both, full_both], 0)
    )
    two_left = adj_row_two - mixed[:band] - parts[0]
    one_left = adj_row_one - mixed[band:] - parts[1]

    nothing = jnp.zeros((band, panel), F32)
    grad_row_one = put(one_left, nothing, nothing)
    grad_row_two = put(two_left, own_rows(head_wide), nothing)
    return (grad_trail, grad_row_one, grad_row_two, grad_diag_one, grad_diag_two)


def solution(mesh):
    split = P("row", "col")
    in_specs = (split, split, split, P(), P(), split, split, split, P(), P())
    out_specs = (split, split, split, P(), P())
    return jax.shard_map(
        per_device, mesh=mesh, in_specs=in_specs, out_specs=out_specs, check_vma=False
    )
```

```python
import functools

import jax
import jax.numpy as jnp
from jax import lax
from jax.experimental import pallas as pl
from jax.experimental.pallas import tpu as pltpu
from jax.sharding import PartitionSpec as P

EXACT = lax.Precision.HIGHEST
F32 = jnp.float32
BF16 = jnp.bfloat16
PIECES = 2


def exact_dot(a, b):
    return jnp.dot(a, b, precision=EXACT, preferred_element_type=F32)


def wide_dot(a, b):
    return jnp.dot(a, b, preferred_element_type=F32)


def halves(value):
    high = value.astype(BF16)
    return high, (value - high.astype(F32)).astype(BF16)


def halved_lower(matrix):
    order = matrix.shape[0]
    rows = lax.broadcasted_iota(jnp.int32, (order, order), 0)
    cols = lax.broadcasted_iota(jnp.int32, (order, order), 1)
    return jnp.where(rows > cols, matrix, jnp.where(rows == cols, 0.5 * matrix, 0))


def split_dot(left, right):
    (left_high, left_low), (right_high, right_low) = left, right
    return wide_dot(
        jnp.concatenate([left_high, left_high, left_low], 1),
        jnp.concatenate([right_high, right_low, right_high], 0),
    )


def inverse_lower(blocks):
    order = blocks[0].shape[-1]
    rows = lax.broadcasted_iota(jnp.int32, (order, order), 0)
    cols = lax.broadcasted_iota(jnp.int32, (order, order), 1)
    equal = rows == cols
    inverses = []
    for block in blocks:
        recip_col = 1.0 / jnp.sum(jnp.where(equal, block, 0), 1, keepdims=True)
        recip_row = 1.0 / jnp.sum(jnp.where(equal, block, 0), 0, keepdims=True)
        pair = ((rows ^ cols) == 1) & (rows > cols)
        corner = jnp.where(pair, block, 0)
        inverses.append(jnp.where(equal, recip_col, 0) - recip_col * corner * recip_row)
    size = 2
    while size < order:
        below = ((rows ^ cols) & -size == size) & (rows > cols)
        below = below & ((rows ^ cols) < 2 * size)
        known = [halves(inverse) for inverse in inverses]
        inner = [
            split_dot(halves(jnp.where(below, block, 0)), pair)
            for block, pair in zip(blocks, known)
        ]
        inverses = [
            inverse - split_dot(pair, halves(part))
            for inverse, pair, part in zip(inverses, known, inner)
        ]
        size *= 2
    return inverses


def prepare_kernel(
    cuts,
    side_ref,
    one_ref,
    two_ref,
    adj_ref,
    inv_one_ref,
    inv_two_ref,
    whole_ref,
    *rest,
):
    *piece_refs, rows_ref, sem = rest
    panel = one_ref.shape[0]
    block = pl.ds(adj_ref.shape[1] - panel, panel)
    fetch = pltpu.make_async_copy(adj_ref.at[:, block], rows_ref, sem)
    fetch.start()
    inverse_one, inverse_two = inverse_lower([one_ref[...], two_ref[...]])
    inv_one_ref[...] = inverse_one
    inv_two_ref[...] = inverse_two
    chosen = halves(jnp.where(side_ref[0] == 1, inverse_two, inverse_one))
    fetch.wait()
    for (start, stop), piece_ref in zip(cuts, piece_refs):
        product = split_dot(halves(rows_ref[start:stop, :]), chosen).astype(BF16)
        whole_ref[start:stop, :] = product
        piece_ref[:panel, :] = jnp.zeros((panel, panel), BF16)
        piece_ref[panel:, :] = product


def prepare(side, diag_one, diag_two, adj_trail, cuts):
    height = adj_trail.shape[0]
    panel = diag_one.shape[0]
    vmem = pl.BlockSpec(memory_space=pltpu.VMEM)
    hbm = pl.BlockSpec(memory_space=pltpu.HBM)
    sizes = [panel + stop - start for start, stop in cuts]
    return pl.pallas_call(
        functools.partial(prepare_kernel, cuts),
        in_specs=[pl.BlockSpec(memory_space=pltpu.SMEM), vmem, vmem, hbm],
        out_specs=[vmem] * (3 + len(cuts)),
        out_shape=[jax.ShapeDtypeStruct((panel, panel), F32)] * 2
        + [jax.ShapeDtypeStruct((size, panel), BF16) for size in [height] + sizes],
        scratch_shapes=[
            pltpu.VMEM((height, panel), F32),
            pltpu.SemaphoreType.DMA,
        ],
        compiler_params=pltpu.CompilerParams(vmem_limit_bytes=60 * 2**20),
        cost_estimate=pl.CostEstimate(
            flops=8 * height * panel * panel, bytes_accessed=8 * height * panel, transcendentals=0
        ),
        name="prepare",
    )(side, diag_one, diag_two, adj_trail)


def blank(shape):
    return pl.pallas_call(
        lambda out_ref: None,
        out_specs=pl.BlockSpec(memory_space=pltpu.HBM),
        out_shape=jax.ShapeDtypeStruct(shape, BF16),
        name="blank",
    )()


def after(value, *others):
    return lax.optimization_barrier((value, *others))[0]


def block_adjoint(block, inverse, seed_adj):
    inner = halved_lower(exact_dot(block.T, seed_adj))
    middle = exact_dot(inverse.T, inner)
    return halved_lower(exact_dot(middle, inverse))


def per_device(
    trail,
    row_one,
    row_two,
    diag_one,
    diag_two,
    adj_trail,
    adj_row_one,
    adj_row_two,
    adj_diag_one,
    adj_diag_two,
):
    panel = diag_one.shape[0]
    height, width = trail.shape
    band = row_one.shape[0]
    last = width - panel
    row_count = lax.axis_size("row")
    col_count = lax.axis_size("col")
    levels = col_count // 2
    top = levels - 1
    row_here = lax.axis_index("row")
    col_here = lax.axis_index("col")
    row_start = row_here * band
    level = col_here // 2
    is_two = col_here % 2 == 1
    here_one = col_here == col_count - 2
    here_two = col_here == col_count - 1
    tile = 2 * panel
    marks = [k * (height // tile) // PIECES * tile for k in range(PIECES + 1)]
    cuts = list(zip(marks, marks[1:]))
    final = len(cuts) - 1

    def own_rows(matrix):
        return lax.dynamic_slice_in_dim(matrix, row_start, band, 0)

    def row_swap(value, step):
        return lax.ppermute(value, "row", [(i, i ^ step) for i in range(row_count)])

    def pair_swap(value, which):
        pairs = [(2 * k + s, 2 * k + 1 - s) for k in which for s in range(2)]
        return lax.ppermute(value, "col", pairs)

    def gather_step(value, step):
        other = row_swap(value, step)
        low = (row_here // step) % 2 == 0
        return jnp.concatenate(
            [jnp.where(low, value, other), jnp.where(low, other, value)], 1
        )

    def gather_rest(value):
        step = 2
        while step < row_count:
            value = gather_step(value, step)
            step *= 2
        return value.reshape(panel, width)

    def choose(options):
        merged = []
        for members, array in options:
            for entry in merged:
                if entry[1] is array:
                    entry[0].extend(members)
                    break
            else:
                merged.append((list(members), array))
        chosen = merged[0][1]
        for members, array in merged[1:]:
            at = functools.reduce(jnp.logical_or, [level == k for k in members])
            chosen = jnp.where(at, array, chosen)
        return chosen

    def hop(value, hops):
        pairs = [(2 * a + s, 2 * b + s) for a, b in hops for s in range(2)]
        return lax.ppermute(value, "col", pairs)

    def spread(pieces, gates, extra):
        middle, span = levels // 2 - 1, levels // 4
        first, down = [], []
        extra_moved = hop(extra, [(top, middle)])
        for k in range(len(pieces) + 1):
            if k == 0:
                operand, hops = pieces[0], [(top, middle)]
            elif k < len(pieces):
                operand = jnp.where(level == top, pieces[k], first[-1])
                hops = [(top, middle), (middle, middle - span)]
            else:
                operand, hops = first[-1], [(middle, middle - span)]
            moved = hop(operand, hops)
            if k > 0:
                down.append(moved)
            if k < len(pieces):
                moved = after(moved, gates[k]) if k < len(gates) else moved
                if k == len(pieces) - 1:
                    moved = lax.dynamic_update_slice(moved, extra_moved, (0, 0))
                first.append(moved)
        held = [
            {middle: here, middle - span: low, middle + span: hop(here, [(middle, middle + span)])}
            for here, low in zip(first, down)
        ]
        span //= 2
        while span >= 1:
            for piece in held:
                fresh = list(piece)
                operand = choose([([k], piece[k]) for k in fresh])
                up = hop(operand, [(k, k + span) for k in fresh])
                low = hop(operand, [(k, k - span) for k in fresh if k >= span])
                for k in fresh:
                    piece[k + span] = up
                    if k >= span:
                        piece[k - span] = low
            span //= 2
        arrived = []
        for piece in held:
            options = [([k], after(piece[k], *arrived)) for k in sorted(piece)]
            arrived.append(choose(options))
        return first, arrived

    near_two = gather_step(row_two[None, None], 1)
    near_one = gather_step(row_one[None, None], 1)
    full_two = gather_rest(near_two)
    side = is_two.astype(jnp.int32)[None]
    inverse_one, inverse_two, whole, *packets = prepare(
        side, diag_one, diag_two, adj_trail, cuts
    )
    own_cross = full_two[:, last:]
    one_owner, two_owner = col_count - 2, col_count - 1
    lent_cross = lax.ppermute(own_cross, "col", [(one_owner, two_owner)])
    side_cross = jnp.where(is_two, lent_cross, own_cross)

    def factor_of(cross):
        return jnp.concatenate(halves(exact_dot(cross.astype(F32), inverse_one)), 0)

    def panels_of(own, other, factor, size):
        solved_two = jnp.where(is_two, own[-size:], other[-size:])
        base_one = jnp.where(is_two, other[-size:], own[-size:])
        tail = base_one.astype(F32) - wide_dot(
            jnp.concatenate([solved_two, solved_two], 1), factor
        )
        return jnp.concatenate([solved_two, tail.astype(BF16)], 1)

    early_two = [
        lax.ppermute(packet, "col", [(two_owner, one_owner)]) for packet in packets
    ]
    full_one = gather_rest(after(near_one, full_two))
    first, arrived = spread(packets, [early_two[0], full_one], side_cross)
    early_one = lax.ppermute(after(whole, first[0]), "col", [(one_owner, two_owner)])
    at_top = level == top
    own = [jnp.where(at_top, a, b) for a, b in zip(packets, arrived)]
    other = [pair_swap(value, range(levels - 1)) for value in arrived]
    full_both = jnp.concatenate([full_two, after(full_one, arrived[0])], 0)

    early_two = jnp.concatenate([piece[panel:] for piece in early_two], 0)
    early_two = after(early_two, arrived[final], other[0])
    top_both = panels_of(whole, early_two, factor_of(own_cross), height)
    terms = wide_dot(top_both.T, trail[:, last:])
    placed = lax.dynamic_update_slice_in_dim(
        jnp.zeros((2 * panel, panel), F32),
        jnp.where(is_two, 0, after(adj_row_two, first[final])[:, last:]),
        row_start,
        0,
    )
    terms = terms - placed
    own_terms = terms
    step = 1
    while step < row_count:
        pairs = [
            (i * col_count + c, (i ^ step) * col_count + c)
            for i in range(row_count)
            for c in (col_count - 2, col_count - 1)
        ]
        if step > 1:
            terms = terms.astype(BF16)
        moved = lax.ppermute(terms, ("row", "col"), pairs)
        terms = terms.astype(F32) + moved.astype(F32)
        step *= 2
    terms = terms.astype(BF16)
    terms_other = pair_swap(terms, [top])

    whole_other = jnp.where(is_two, after(early_one, own_terms), early_two)
    for k, (start, stop) in enumerate(cuts):
        low = after(other[k][panel:], own_terms, *other[:k])
        other[k] = jnp.where(at_top, whole_other[start:stop], low)
    cross = jnp.where(at_top, side_cross, own[final][:panel])
    factor = factor_of(cross)
    column = lax.broadcasted_iota(jnp.int32, (1, width), 1)
    in_block = column >= last

    def put(matrix, block_one, block_two):
        block = jnp.where(here_one, block_one, block_two).astype(matrix.dtype)
        block = jnp.pad(block, ((0, 0), (last, 0)))
        return jnp.where(in_block & (here_one | here_two), block, matrix)

    def updated(both, start, previous):
        rows = adj_trail[start : start + both.shape[0]]
        left = (rows - wide_dot(both, full_both)).astype(BF16)
        left = put(left, both[:, panel:], both[:, :panel])
        return lax.dynamic_update_slice(previous, left, (start, 0))

    sums = 0
    grad_trail = blank((height, width))
    for (start, stop), mine, theirs in zip(cuts[:-1], own, other):
        both = panels_of(mine, theirs, factor, stop - start)
        sums = sums + wide_dot(both.T, trail[start:stop])
        grad_trail = updated(both, start, grad_trail)
    diag_term_two = jnp.where(is_two, terms, terms_other)[:panel]
    terms = jnp.concatenate([diag_term_two, jnp.where(is_two, terms_other, terms)], 0)
    terms = choose(
        [([top], terms)] + [([k], hop(terms, [(top, k)])) for k in range(levels - 1)]
    )
    whole_terms = terms.astype(F32)
    diag_term_two = whole_terms[:panel]
    crossing = whole_terms[panel : 2 * panel]
    diag_term_one = whole_terms[2 * panel :]

    start, stop = cuts[-1]
    theirs = after(other[-1], sums)
    both = panels_of(own[-1], theirs, factor, stop - start)
    sums = (sums + wide_dot(both.T, trail[start:stop])).astype(BF16)

    parts = sums.reshape(2, row_count, band, width)
    step = 1
    while step < row_count:
        low = (row_here // step) % 2 == 0
        parts = parts.reshape(2, -1, 2, band, width)
        keep = jnp.where(low, parts[:, :, 0], parts[:, :, 1])
        give = jnp.where(low, parts[:, :, 1], parts[:, :, 0])
        give = give.astype(BF16)
        sent = give
        parts = keep + row_swap(give, step).astype(F32)
        step *= 2
    parts = parts.reshape(2, band, width)
    grad_trail = updated(after(both, sent), start, grad_trail)

    grad_diag_two = block_adjoint(
        diag_two, inverse_two, jnp.tril(adj_diag_two - after(diag_term_two, sums))
    )
    mirror_two = grad_diag_two + grad_diag_two.T
    adj_two = -crossing - exact_dot(mirror_two, cross.astype(F32))
    head = exact_dot(adj_two, inverse_one).astype(BF16)
    seed_one = jnp.tril(adj_diag_one - wide_dot(head.T, cross) - diag_term_one)
    grad_diag_one = block_adjoint(diag_one, inverse_one, seed_one)
    mirror_one = grad_diag_one + grad_diag_one.T

    head_wide = head.astype(F32)
    mix_two = jnp.concatenate([own_rows(mirror_two), own_rows(head_wide)], 1)
    mix_one = jnp.concatenate([own_rows(head_wide.T), own_rows(mirror_one)], 1)
    mix = jnp.concatenate([mix_two, mix_one], 0)
    mixed = wide_dot(
        jnp.concatenate(halves(mix), 1), jnp.concatenate([full_both, full_both], 0)
    )
    two_left = adj_row_two - mixed[:band] - parts[0]
    one_left = adj_row_one - mixed[band:] - parts[1]

    nothing = jnp.zeros((band, panel), F32)
    grad_row_one = put(one_left, nothing, nothing)
    grad_row_two = put(two_left, own_rows(head_wide), nothing)
    return (grad_trail, grad_row_one, grad_row_two, grad_diag_one, grad_diag_two)


def solution(mesh):
    split = P("row", "col")
    in_specs = (split, split, split, P(), P(), split, split, split, P(), P())
    out_specs = (split, split, split, P(), P())
    return jax.shard_map(
        per_device, mesh=mesh, in_specs=in_specs, out_specs=out_specs, check_vma=False
    )
```

```python
import functools

import jax
import jax.numpy as jnp
from jax import lax
from jax.experimental import pallas as pl
from jax.experimental.pallas import tpu as pltpu
from jax.sharding import PartitionSpec as P

EXACT = lax.Precision.HIGHEST
F32 = jnp.float32
BF16 = jnp.bfloat16
PIECES = 2


def exact_dot(a, b):
    return jnp.dot(a, b, precision=EXACT, preferred_element_type=F32)


def wide_dot(a, b):
    return jnp.dot(a, b, preferred_element_type=F32)


def halves(value):
    high = value.astype(BF16)
    return high, (value - high.astype(F32)).astype(BF16)


def halved_lower(matrix):
    order = matrix.shape[0]
    rows = lax.broadcasted_iota(jnp.int32, (order, order), 0)
    cols = lax.broadcasted_iota(jnp.int32, (order, order), 1)
    return jnp.where(rows > cols, matrix, jnp.where(rows == cols, 0.5 * matrix, 0))


def split_dot(left, right):
    (left_high, left_low), (right_high, right_low) = left, right
    return wide_dot(
        jnp.concatenate([left_high, left_high, left_low], 1),
        jnp.concatenate([right_high, right_low, right_high], 0),
    )


def inverse_lower(blocks):
    order = blocks[0].shape[-1]
    rows = lax.broadcasted_iota(jnp.int32, (order, order), 0)
    cols = lax.broadcasted_iota(jnp.int32, (order, order), 1)
    equal = rows == cols
    inverses = []
    for block in blocks:
        recip_col = 1.0 / jnp.sum(jnp.where(equal, block, 0), 1, keepdims=True)
        recip_row = 1.0 / jnp.sum(jnp.where(equal, block, 0), 0, keepdims=True)
        pair = ((rows ^ cols) == 1) & (rows > cols)
        corner = jnp.where(pair, block, 0)
        inverses.append(jnp.where(equal, recip_col, 0) - recip_col * corner * recip_row)
    size = 2
    while size < order:
        below = ((rows ^ cols) & -size == size) & (rows > cols)
        below = below & ((rows ^ cols) < 2 * size)
        known = [halves(inverse) for inverse in inverses]
        inner = [
            split_dot(halves(jnp.where(below, block, 0)), pair)
            for block, pair in zip(blocks, known)
        ]
        inverses = [
            inverse - split_dot(pair, halves(part))
            for inverse, pair, part in zip(inverses, known, inner)
        ]
        size *= 2
    return inverses


def prepare_kernel(
    cuts,
    side_ref,
    one_ref,
    two_ref,
    adj_ref,
    inv_one_ref,
    inv_two_ref,
    whole_ref,
    *rest,
):
    *piece_refs, rows_ref, sem = rest
    panel = one_ref.shape[0]
    block = pl.ds(adj_ref.shape[1] - panel, panel)
    fetch = pltpu.make_async_copy(adj_ref.at[:, block], rows_ref, sem)
    fetch.start()
    inverse_one, inverse_two = inverse_lower([one_ref[...], two_ref[...]])
    inv_one_ref[...] = inverse_one
    inv_two_ref[...] = inverse_two
    chosen = halves(jnp.where(side_ref[0] == 1, inverse_two, inverse_one))
    fetch.wait()
    for (start, stop), piece_ref in zip(cuts, piece_refs):
        product = split_dot(halves(rows_ref[start:stop, :]), chosen).astype(BF16)
        whole_ref[start:stop, :] = product
        piece_ref[:panel, :] = jnp.zeros((panel, panel), BF16)
        piece_ref[panel:, :] = product


def prepare(side, diag_one, diag_two, adj_trail, cuts):
    height = adj_trail.shape[0]
    panel = diag_one.shape[0]
    vmem = pl.BlockSpec(memory_space=pltpu.VMEM)
    hbm = pl.BlockSpec(memory_space=pltpu.HBM)
    sizes = [panel + stop - start for start, stop in cuts]
    return pl.pallas_call(
        functools.partial(prepare_kernel, cuts),
        in_specs=[pl.BlockSpec(memory_space=pltpu.SMEM), vmem, vmem, hbm],
        out_specs=[vmem] * (3 + len(cuts)),
        out_shape=[jax.ShapeDtypeStruct((panel, panel), F32)] * 2
        + [jax.ShapeDtypeStruct((size, panel), BF16) for size in [height] + sizes],
        scratch_shapes=[
            pltpu.VMEM((height, panel), F32),
            pltpu.SemaphoreType.DMA,
        ],
        compiler_params=pltpu.CompilerParams(vmem_limit_bytes=60 * 2**20),
        cost_estimate=pl.CostEstimate(
            flops=8 * height * panel * panel, bytes_accessed=8 * height * panel, transcendentals=0
        ),
        name="prepare",
    )(side, diag_one, diag_two, adj_trail)


def blank(shape):
    return pl.pallas_call(
        lambda out_ref: None,
        out_specs=pl.BlockSpec(memory_space=pltpu.HBM),
        out_shape=jax.ShapeDtypeStruct(shape, BF16),
        name="blank",
    )()


def after(value, *others):
    return lax.optimization_barrier((value, *others))[0]


def block_adjoint(block, inverse, seed_adj):
    inner = halved_lower(exact_dot(block.T, seed_adj))
    middle = exact_dot(inverse.T, inner)
    return halved_lower(exact_dot(middle, inverse))


def per_device(
    trail,
    row_one,
    row_two,
    diag_one,
    diag_two,
    adj_trail,
    adj_row_one,
    adj_row_two,
    adj_diag_one,
    adj_diag_two,
):
    panel = diag_one.shape[0]
    height, width = trail.shape
    band = row_one.shape[0]
    last = width - panel
    row_count = lax.axis_size("row")
    col_count = lax.axis_size("col")
    levels = col_count // 2
    top = levels - 1
    row_here = lax.axis_index("row")
    col_here = lax.axis_index("col")
    row_start = row_here * band
    level = col_here // 2
    is_two = col_here % 2 == 1
    here_one = col_here == col_count - 2
    here_two = col_here == col_count - 1
    tile = 2 * panel
    marks = [k * (height // tile) // PIECES * tile for k in range(PIECES + 1)]
    cuts = list(zip(marks, marks[1:]))
    final = len(cuts) - 1

    def own_rows(matrix):
        return lax.dynamic_slice_in_dim(matrix, row_start, band, 0)

    def row_swap(value, step):
        return lax.ppermute(value, "row", [(i, i ^ step) for i in range(row_count)])

    def pair_swap(value, which):
        pairs = [(2 * k + s, 2 * k + 1 - s) for k in which for s in range(2)]
        return lax.ppermute(value, "col", pairs)

    def gather_step(value, step):
        other = row_swap(value, step)
        low = (row_here // step) % 2 == 0
        return jnp.concatenate(
            [jnp.where(low, value, other), jnp.where(low, other, value)], 1
        )

    def gather_rest(value):
        step = 2
        while step < row_count:
            value = gather_step(value, step)
            step *= 2
        return value.reshape(panel, width)

    def choose(options):
        merged = []
        for members, array in options:
            for entry in merged:
                if entry[1] is array:
                    entry[0].extend(members)
                    break
            else:
                merged.append((list(members), array))
        chosen = merged[0][1]
        for members, array in merged[1:]:
            at = functools.reduce(jnp.logical_or, [level == k for k in members])
            chosen = jnp.where(at, array, chosen)
        return chosen

    def hop(value, hops):
        pairs = [(2 * a + s, 2 * b + s) for a, b in hops for s in range(2)]
        return lax.ppermute(value, "col", pairs)

    def spread(pieces, gates, extra):
        middle, span = levels // 2 - 1, levels // 4
        first, down = [], []
        extra_moved = hop(extra, [(top, middle)])
        for k in range(len(pieces) + 1):
            if k == 0:
                operand, hops = pieces[0], [(top, middle)]
            elif k < len(pieces):
                operand = jnp.where(level == top, pieces[k], first[-1])
                hops = [(top, middle), (middle, middle - span)]
            else:
                operand, hops = first[-1], [(middle, middle - span)]
            moved = hop(operand, hops)
            if k > 0:
                down.append(moved)
            if k < len(pieces):
                moved = after(moved, gates[k]) if k < len(gates) else moved
                if k == len(pieces) - 1:
                    moved = lax.dynamic_update_slice(moved, extra_moved, (0, 0))
                first.append(moved)
        held = [
            {middle: here, middle - span: low, middle + span: hop(here, [(middle, middle + span)])}
            for here, low in zip(first, down)
        ]
        span //= 2
        while span >= 1:
            for piece in held:
                fresh = list(piece)
                operand = choose([([k], piece[k]) for k in fresh])
                up = hop(operand, [(k, k + span) for k in fresh])
                low = hop(operand, [(k, k - span) for k in fresh if k >= span])
                for k in fresh:
                    piece[k + span] = up
                    if k >= span:
                        piece[k - span] = low
            span //= 2
        arrived = []
        for piece in held:
            options = [([k], after(piece[k], *arrived)) for k in sorted(piece)]
            arrived.append(choose(options))
        return first, arrived

    near_two = gather_step(row_two[None, None], 1)
    near_one = gather_step(row_one[None, None], 1)
    full_two = gather_rest(near_two)
    side = is_two.astype(jnp.int32)[None]
    inverse_one, inverse_two, whole, *packets = prepare(
        side, diag_one, diag_two, adj_trail, cuts
    )
    own_cross = full_two[:, last:]
    one_owner, two_owner = col_count - 2, col_count - 1
    lent_cross = lax.ppermute(own_cross, "col", [(one_owner, two_owner)])
    side_cross = jnp.where(is_two, lent_cross, own_cross)

    def factor_of(cross):
        return jnp.concatenate(halves(exact_dot(cross.astype(F32), inverse_one)), 0)

    def panels_of(own, other, factor, size):
        solved_two = jnp.where(is_two, own[-size:], other[-size:])
        base_one = jnp.where(is_two, other[-size:], own[-size:])
        tail = base_one.astype(F32) - wide_dot(
            jnp.concatenate([solved_two, solved_two], 1), factor
        )
        return jnp.concatenate([solved_two, tail.astype(BF16)], 1)

    early_two = [
        lax.ppermute(packet, "col", [(two_owner, one_owner)]) for packet in packets
    ]
    full_one = gather_rest(after(near_one, full_two))
    first, arrived = spread(packets, [early_two[0], full_one], side_cross)
    early_one = lax.ppermute(after(whole, first[0]), "col", [(one_owner, two_owner)])
    at_top = level == top
    own = [jnp.where(at_top, a, b) for a, b in zip(packets, arrived)]
    other = [pair_swap(value, range(levels - 1)) for value in arrived]
    full_both = jnp.concatenate([full_two, after(full_one, arrived[0])], 0)

    early_two = jnp.concatenate([piece[panel:] for piece in early_two], 0)
    early_two = after(early_two, arrived[final], other[0])
    top_both = panels_of(whole, early_two, factor_of(own_cross), height)
    terms = wide_dot(top_both.T, trail[:, last:])
    placed = lax.dynamic_update_slice_in_dim(
        jnp.zeros((2 * panel, panel), F32),
        jnp.where(is_two, 0, after(adj_row_two, first[final])[:, last:]),
        row_start,
        0,
    )
    terms = terms - placed
    own_terms = terms
    step = 1
    while step < row_count:
        pairs = [
            (i * col_count + c, (i ^ step) * col_count + c)
            for i in range(row_count)
            for c in (col_count - 2, col_count - 1)
        ]
        if step > 1:
            terms = terms.astype(BF16)
        moved = lax.ppermute(terms, ("row", "col"), pairs)
        terms = terms.astype(F32) + moved.astype(F32)
        step *= 2
    terms = terms.astype(BF16)
    terms_other = pair_swap(terms, [top])

    whole_other = jnp.where(is_two, after(early_one, own_terms), early_two)
    for k, (start, stop) in enumerate(cuts):
        low = after(other[k][panel:], own_terms, *other[:k])
        other[k] = jnp.where(at_top, whole_other[start:stop], low)
    cross = jnp.where(at_top, side_cross, own[final][:panel])
    factor = factor_of(cross)
    column = lax.broadcasted_iota(jnp.int32, (1, width), 1)
    in_block = column >= last

    def put(matrix, block_one, block_two):
        block = jnp.where(here_one, block_one, block_two).astype(matrix.dtype)
        block = jnp.pad(block, ((0, 0), (last, 0)))
        return jnp.where(in_block & (here_one | here_two), block, matrix)

    def updated(both, start, previous):
        rows = adj_trail[start : start + both.shape[0]]
        left = (rows - wide_dot(both, full_both)).astype(BF16)
        left = put(left, both[:, panel:], both[:, :panel])
        return lax.dynamic_update_slice(previous, left, (start, 0))

    sums = 0
    grad_trail = blank((height, width))
    for (start, stop), mine, theirs in zip(cuts[:-1], own, other):
        both = panels_of(mine, theirs, factor, stop - start)
        sums = sums + wide_dot(both.T, trail[start:stop])
        grad_trail = updated(both, start, grad_trail)
    diag_term_two = jnp.where(is_two, terms, terms_other)[:panel]
    terms = jnp.concatenate([diag_term_two, jnp.where(is_two, terms_other, terms)], 0)
    terms = choose(
        [([top], terms)] + [([k], hop(terms, [(top, k)])) for k in range(levels - 1)]
    )
    whole_terms = terms.astype(F32)
    diag_term_two = whole_terms[:panel]
    crossing = whole_terms[panel : 2 * panel]
    diag_term_one = whole_terms[2 * panel :]

    start, stop = cuts[-1]
    theirs = after(other[-1], sums)
    both = panels_of(own[-1], theirs, factor, stop - start)
    sums = (sums + wide_dot(both.T, trail[start:stop])).astype(BF16)

    parts = sums.reshape(2, row_count, band, width)
    step = 1
    while step < row_count:
        low = (row_here // step) % 2 == 0
        parts = parts.reshape(2, -1, 2, band, width)
        keep = jnp.where(low, parts[:, :, 0], parts[:, :, 1])
        give = jnp.where(low, parts[:, :, 1], parts[:, :, 0])
        give = give.astype(BF16)
        if 2 * step >= row_count:
            grad_trail = updated(both, start, grad_trail)
            give = after(give, grad_trail[:16, :panel])
        parts = keep + row_swap(give, step).astype(F32)
        step *= 2
    parts = parts.reshape(2, band, width)

    grad_diag_two = block_adjoint(
        diag_two, inverse_two, jnp.tril(adj_diag_two - after(diag_term_two, sums))
    )
    mirror_two = grad_diag_two + grad_diag_two.T
    adj_two = -crossing - exact_dot(mirror_two, cross.astype(F32))
    head = exact_dot(adj_two, inverse_one).astype(BF16)
    seed_one = jnp.tril(adj_diag_one - wide_dot(head.T, cross) - diag_term_one)
    grad_diag_one = block_adjoint(diag_one, inverse_one, seed_one)
    mirror_one = grad_diag_one + grad_diag_one.T

    head_wide = head.astype(F32)
    mix_two = jnp.concatenate([own_rows(mirror_two), own_rows(head_wide)], 1)
    mix_one = jnp.concatenate([own_rows(head_wide.T), own_rows(mirror_one)], 1)
    mix = jnp.concatenate([mix_two, mix_one], 0)
    mixed = wide_dot(
        jnp.concatenate(halves(mix), 1), jnp.concatenate([full_both, full_both], 0)
    )
    two_left = adj_row_two - mixed[:band] - parts[0]
    one_left = adj_row_one - mixed[band:] - parts[1]

    nothing = jnp.zeros((band, panel), F32)
    grad_row_one = put(one_left, nothing, nothing)
    grad_row_two = put(two_left, own_rows(head_wide), nothing)
    return (grad_trail, grad_row_one, grad_row_two, grad_diag_one, grad_diag_two)


def solution(mesh):
    split = P("row", "col")
    in_specs = (split, split, split, P(), P(), split, split, split, P(), P())
    out_specs = (split, split, split, P(), P())
    return jax.shard_map(
        per_device, mesh=mesh, in_specs=in_specs, out_specs=out_specs, check_vma=False
    )
```
